32 devices in a mesh: dom: 8 (over y, x, core), tool: 4 (over z).
Axes of the slice: x: 2, y: 2, z: 4, core: 2. Of those that a mesh axis runs over, the one named last changes fastest.
Arguments:
- records: float32 [2048, 512], P(('dom', 'tool')), may hold values from -6 to 6
- tool_data: float32 [8192, 512], P(('dom', 'tool')), may hold values from -6 to 6
- owners: int32 [2048, 2], P(('dom', 'tool')), may hold values from 0 to 31, all different within a row; in each aligned block of 64 rows (0 to 63, 64 to 127, ...) at most 6 rows name the same one
- local_seg: int32 [2048, 2], P(('dom', 'tool')), may hold values from 0 to 255
- active: int32 [2048, 64], P(('dom', 'tool')), may hold values 0 or 1
- stiffness: float32 [2048, 5, 4096], P(('dom', 'tool')), may hold values from -0.3125 to 0.3125
- columns: int32 [2048, 5], P(('dom', 'tool')), may hold values from 0 to 67, as said below
- vectors: float32 [2048, 4096], P(('dom', 'tool')), may hold values from -6 to 6
Outputs:
- product: float32 [2048, 4096], P(('dom', 'tool'))
The draws below stay inside these ranges and needn't reach their ends.
Inputs may be any that keep to these rules, and one draw needn't show every extreme that they name: Among the 64 node blocks of one device no owner is named by more than 6 candidates, a bound that some block reaches; a block's candidates name different owners. `columns`: the first column of each row is the row's own block, column 2 + b mod 64; the others lie within 2 blocks of it.
All inputs are finite; a program needn't handle non-finite values. No bound on the sum of `active` on one device may be relied on, other than what follows from the above.
Results may differ from the reference program's by a relative error of at most 0.0003.
Values sent between devices are 32-bit elements; how exact they have to be, the bound alone decides.
No kernel may reach another device: no remote copies, remote signals or barrier semaphores. Data moves between devices by JAX's collectives and lax.ppermute only.
A program may use at most 128 MiB of HBM per device.

```python
import math
import jax
import jax.numpy as jnp
import numpy as np
from jax import lax

NODE = 64
NVEC = 64
FIELDS = 8
CAND = 2
NNZ = 5
HB = 2
BLK_DEV = 64
SEG_DEV = 256
CAP = 6
BLOCKS = 2048
SEGS = 8192
N_DOM = 8
N_TOOL = 4


def draw_columns(key, part):
    local_row = jnp.arange(BLOCKS, dtype=jnp.int32) % BLK_DEV
    offsets = jax.random.randint(key, (BLOCKS, NNZ), -HB, HB + 1).astype(jnp.int32)
    offsets = offsets.at[:, 0].set(0)
    return local_row[:, None] + HB + offsets


def set_ends(values, rng, low, top_value):
    extent = values.shape
    spot = [jax.random.randint(jax.random.fold_in(rng, axis), (), 0, extent[axis]) for axis in range(len(extent))]
    values = values.at[tuple(spot)].set(low)
    longest = extent.index(max(extent))
    spot[longest] = (spot[longest] + 1) % extent[longest]
    return values.at[tuple(spot)].set(top_value)


def block_levels(key, extent, split, low, top_value):
    def one(axis_at, blocks):
        draws = jax.random.uniform(jax.random.fold_in(jax.random.fold_in(key, 6), axis_at), (blocks,), jnp.float32, low / len(split), top_value / len(split))
        return jnp.repeat(jnp.exp(draws), extent[axis_at] // blocks).reshape((-1,) + (1,) * (len(extent) - axis_at - 1))

    level = one(*split[0])
    for cut in split[1:]:
        level = level * one(*cut)
    return level


def routed_block(rng, own, number, rows, number_of, top, reach, skew):
    sequence = jax.random.permutation(rng, number_of)
    heavy_load, ordinary = load_shares(number_of, rows * top, reach, skew, True), load_shares(number_of, rows * top, reach, skew, False)
    places = jnp.arange(number_of)

    def named(lengths, turn):
        used = int((lengths > 0).sum())
        fixed = max(1, used // 4)
        passed = fixed + (places - fixed + turn * (used - fixed)) % max(1, number_of - fixed)
        return jnp.zeros((number_of,), jnp.int32).at[sequence[jnp.where(places < fixed, places, passed)]].set(jnp.asarray(lengths, jnp.int32))

    lengths = jnp.where(number % 4 == 0, named(heavy_load, number // 4), named(ordinary, number - number // 4 - 1))
    mixed = jax.random.permutation(jax.random.fold_in(own, 3), number_of)
    source_of, taker = mixed[0:number_of // 2 * 2:2], mixed[1:number_of // 2 * 2:2]
    margin = jnp.minimum(lengths[source_of] - 1, reach - lengths[taker]) // 2
    margin = jnp.where((source_of == sequence[0]) | (taker == sequence[0]) | (lengths[taker] == 0), 0, jnp.maximum(margin, 0))
    passed = jax.random.randint(jax.random.fold_in(own, 4), (number_of // 2,), 0, 1 << 20) % (margin + 1)
    lengths = lengths.at[source_of].add(-passed).at[taker].add(passed)
    members = jnp.searchsorted(jnp.cumsum(lengths), jnp.arange(rows * top), side="right").astype(jnp.int32)
    grid = members.reshape(top, rows).T
    grid = grid[jax.random.permutation(jax.random.fold_in(own, 1), rows)]
    turn = jax.random.randint(jax.random.fold_in(own, 2), (rows, 1), 0, top)
    return jnp.take_along_axis(grid, (jnp.arange(top)[None, :] + turn) % top, axis=1)


def load_shares(amount, total, most, lean, full):
    loads = [(1 << 20) // math.isqrt(rank ** lean) + 1 for rank in range(1, amount + 1)]
    largest = most if full else min(most, max(-(-total // amount), total * loads[0] // sum(loads)))
    least = 1 if total - largest >= amount - 1 else 0
    counts, surplus = [largest] + [least] * (amount - 1), total - largest - least * (amount - 1)
    while surplus > 0:
        candidates = [i for i in range(1, amount) if counts[i] < largest] or [i for i in range(1, amount) if counts[i] < most]
        whole, left = sum([loads[i] for i in candidates]), surplus
        for i in candidates:
            more = min(most - counts[i], max(1, left * loads[i] // whole), surplus)
            counts[i] = counts[i] + more
            surplus = surplus - more
    return np.array(counts)


def scatter_about(own_key, extent, scale, bound, split=(), kind=jnp.bfloat16):
    values = jax.random.normal(own_key, extent, jnp.float32) * scale
    if len(split) > 0:
        values = block_levels(own_key, extent, split, -0.22, 0.18) * values
    return jnp.clip(values, min=-bound, max=bound).astype(kind)


def setup_inputs(seed: int = 0) -> dict:
    key_list = jax.random.split(jax.random.key(seed), 9)
    records = scatter_about(key_list[0], (BLOCKS, FIELDS * NODE), 1.0, 6.0, ((0, 32),), jnp.float32)
    tool_data = scatter_about(key_list[1], (SEGS, FIELDS * NODE), 1.0, 6.0, ((0, 32),), jnp.float32)
    owners_keys = jax.random.split(jax.random.fold_in(key_list[2], 1), BLOCKS // BLK_DEV)
    owners_turns = jax.random.permutation(jax.random.fold_in(key_list[2], 3), BLOCKS // BLK_DEV)
    owners = jax.vmap(lambda own, number: routed_block(jax.random.fold_in(key_list[2], 2), own, number, BLK_DEV, N_DOM * N_TOOL, CAND, CAP, 2))(owners_keys, owners_turns).reshape((BLOCKS, CAND))
    local_seg = set_ends(jax.random.randint(key_list[3], (BLOCKS, CAND), 0, SEG_DEV), jax.random.fold_in(key_list[3], 1), 0, SEG_DEV - 1).astype(jnp.int32)
    active = set_ends((jax.random.randint(key_list[4], (BLOCKS, NODE), 0, 4) < 3).astype(jnp.int32), jax.random.fold_in(key_list[4], 1), 0, 1)
    stiffness = scatter_about(key_list[5], (BLOCKS, NNZ, NODE * NODE), (NODE * NNZ) ** -0.5, 0.3125, ((0, 32),), jnp.float32)
    columns = draw_columns(jax.random.fold_in(key_list[8], 71), 0)
    vectors = scatter_about(key_list[7], (BLOCKS, NODE * NVEC), 1.0, 6.0, ((0, 32),), jnp.float32)
    return dict(records=records, tool_data=tool_data, owners=owners, local_seg=local_seg, active=active, stiffness=stiffness, columns=columns, vectors=vectors)


def mortar_tiles(part_rec, tool_rec):
    part = part_rec.reshape(part_rec.shape[:-1] + (FIELDS, NODE))
    tool = tool_rec.reshape(tool_rec.shape[:-1] + (FIELDS, NODE))
    apart = part[..., 0:3, :, None] - tool[..., 0:3, None, :]
    distance = jnp.sum(apart * apart, axis=-3)
    aligned = jnp.sum(part[..., 3:6, :, None] * tool[..., 3:6, None, :], axis=-3)
    phase = 3.0 * aligned + part[..., 6, :, None] * tool[..., 6, None, :]
    sliding = 1.0 + 0.5 * jnp.tanh(part[..., 7, :, None] * tool[..., 7, None, :])
    return jnp.exp(-distance / 8.0) * jnp.cos(phase) * sliding


def reference(records, tool_data, owners, local_seg, active, stiffness, columns, vectors):
    devices = N_DOM * N_TOOL
    hp = lax.Precision.HIGHEST
    vec_blocks = vectors.reshape(BLOCKS, NODE, NVEC)
    rim_zeros = jnp.zeros((HB, NODE, NVEC), jnp.float32)
    padded = jnp.concatenate([rim_zeros, vec_blocks, rim_zeros], axis=0)

    def one_device(device):
        start = (device * BLK_DEV).astype(jnp.int32)
        part_rows = lax.dynamic_slice_in_dim(records, start, BLK_DEV, 0)
        owner_ids = lax.dynamic_slice_in_dim(owners, start, BLK_DEV, 0)
        seg_local = lax.dynamic_slice_in_dim(local_seg, start, BLK_DEV, 0)
        flags = lax.dynamic_slice_in_dim(active, start, BLK_DEV, 0).astype(jnp.float32)[:, :, None]
        blocks_here = lax.dynamic_slice_in_dim(stiffness, start, BLK_DEV, 0).reshape(BLK_DEV, NNZ, NODE, NODE)
        column_ids = lax.dynamic_slice_in_dim(columns, start, BLK_DEV, 0)
        segment = (owner_ids * SEG_DEV + seg_local).astype(jnp.int32)
        tiles = mortar_tiles(part_rows[:, None, :], tool_data[segment])
        local_vec = lax.dynamic_slice_in_dim(vec_blocks, start, BLK_DEV, 0)
        masked = flags * local_vec
        inward = jnp.einsum('bkij,biv->bkjv', tiles, masked, precision=hp)
        outward = jnp.einsum('bkij,bkjv->biv', tiles, inward, precision=hp)
        contact = 0.05 * flags * outward
        extended = lax.dynamic_slice_in_dim(padded, start, BLK_DEV + 2 * HB, 0)
        nearby = extended[column_ids]
        inner = jnp.einsum('bkij,bkjv->biv', blocks_here, nearby, precision=hp)
        return (inner + contact).reshape(BLK_DEV, NODE * NVEC)

    result = lax.map(one_device, jnp.arange(devices, dtype=jnp.int32))
    return result.reshape(BLOCKS, NODE * NVEC)
```

```python
import functools
import math

import jax
import jax.numpy as jnp
from jax import lax
from jax.experimental import pallas as pl
from jax.experimental.pallas import tpu as pltpu
from jax.sharding import PartitionSpec as P

NODE = 64
NVEC = 64
FIELDS = 8
HB = 2
LANES = 128
SUB = 8
AXES = ("dom", "tool")
TURN = 1.0 / (2.0 * math.pi)
REACH = math.sqrt(math.log2(math.e) / 8.0)
SHARE = math.sqrt(0.05)
FAR = 1e18
SINE = (6.283185160087854, -41.3416550310025, 81.60100404550954, -76.54978161791087, 39.53670066614222)
F32 = jnp.float32
BF16 = jnp.bfloat16
VMEM = pl.BlockSpec(memory_space=pltpu.VMEM)
SMEM = pl.BlockSpec(memory_space=pltpu.SMEM)


def params(mib):
    return pltpu.CompilerParams(vmem_limit_bytes=mib << 20)


def left_half(rows):
    return lax.broadcasted_iota(jnp.int32, (rows, LANES), 1) < NODE


def swap(x):
    return pltpu.roll(x, NODE, 1)


def split(x):
    high = x.astype(BF16)
    return high, (x - high.astype(F32)).astype(BF16)


def prep_kernel(capacity, owners_ref, seg_ref, first_ref, last_ref, send_ref, slot_ref, head_ref, tail_ref):
    cands, blocks = owners_ref.shape
    peers = send_ref.shape[0]
    owner_ids = lax.broadcasted_iota(jnp.int32, (peers, blocks), 0)
    upper = (
        lax.broadcasted_iota(jnp.int32, (blocks, blocks), 0)
        <= lax.broadcasted_iota(jnp.int32, (blocks, blocks), 1)
    ).astype(BF16)
    lanes = lax.broadcasted_iota(jnp.int32, (peers, LANES), 1)
    send = jnp.zeros((peers, LANES), jnp.int32)
    before = jnp.zeros((peers, 1), F32)
    for k in range(cands):
        target = owners_ref[k : k + 1, :]
        segment = seg_ref[k : k + 1, :]
        hits = owner_ids == jnp.broadcast_to(target, (peers, blocks))
        ones = hits.astype(F32)
        counts = before + jnp.dot(ones.astype(BF16), upper, preferred_element_type=F32)
        before = before + jnp.sum(ones, axis=1, keepdims=True)
        places = jnp.where(hits, counts - 1.0, -1.0).astype(jnp.int32)
        rank = jnp.sum(jnp.where(hits, counts - 1.0, 0.0), axis=0, keepdims=True).astype(jnp.int32)
        slot_ref[k : k + 1, :] = target * capacity + rank
        wanted = jnp.broadcast_to(segment, (peers, blocks))
        for s in range(capacity):
            named = jnp.sum(jnp.where(places == s, wanted, 0), axis=1, keepdims=True)
            send = send + jnp.where(lanes == s, named, 0)
    send_ref[:, 0, :] = send
    pairs = NODE // 2
    for h in range(HB):
        head_ref[h * pairs : (h + 1) * pairs, :] = first_ref[0, pl.ds(h, pairs, stride=SUB), :]
        tail_ref[h * pairs : (h + 1) * pairs, :] = last_ref[0, pl.ds(SUB - HB + h, pairs, stride=SUB), :]


def rows_kernel(capacity, index_ref, tool_ref, out_ref):
    peers = index_ref.shape[0]
    chunks = tool_ref.shape[1] // SUB

    def one(peer, carry):
        for s in range(capacity):
            row = index_ref[peer, 0, s]
            out_ref[peer, s] = tool_ref[row // SUB, pl.ds(row % SUB, chunks, stride=SUB), :]
        return carry

    lax.fori_loop(0, peers, one, 0, unroll=2)


def inner_kernel(
    columns_ref, stiff_ref, vec_ref, before_ref, after_ref, rec_ref, act_ref,
    out_ref, own_ref, field_ref, wide_ref, hold_ref, turn_ref,
):
    nnz, groups = stiff_ref.shape[:2]
    blocks = groups * SUB
    pairs = NODE // 2
    half = left_half(pairs)
    full = left_half(NODE)

    def widen(x):
        other = swap(x)
        return jnp.where(half, x, other), jnp.where(half, other, x)

    def store_wide(at, even, odd, spot):
        hold_ref[spot, pl.ds(0, pairs, stride=2), :] = even
        hold_ref[spot, pl.ds(1, pairs, stride=2), :] = odd
        whole = hold_ref[spot]
        high = whole.astype(BF16).astype(F32)
        wide_ref[at] = jnp.where(full, whole, whole - high).astype(BF16)

    for h in range(HB):
        store_wide(h, *widen(before_ref[h * pairs : (h + 1) * pairs, :]), h)
        store_wide(blocks + HB + h, *widen(after_ref[h * pairs : (h + 1) * pairs, :]), HB + h)

    def spread(g, carry):
        for j in range(SUB):
            even, odd = widen(vec_ref[g, pl.ds(j, pairs, stride=SUB), :])
            store_wide(HB + g * SUB + j, even, odd, j)
            both = jnp.concatenate([even, odd], axis=0)
            high = both.astype(BF16).astype(F32)
            own_ref[g * SUB + j] = jnp.where(full, both, both - high).astype(BF16)
        return carry

    lax.fori_loop(0, groups, spread, 0)

    field_of = lax.broadcasted_iota(jnp.int32, (blocks, LANES), 1) // NODE
    for c in range(FIELDS // 2):
        part = rec_ref[:, c * LANES : (c + 1) * LANES]
        if c == 0:
            idle = jnp.concatenate([act_ref[...], jnp.ones((blocks, NODE), jnp.int32)], axis=1) == 0
            part = jnp.where(idle, FAR, part * REACH)
        elif c == 1:
            part = part * jnp.where(field_of == 0, REACH, 1.0)
        turn_ref[...] = jnp.concatenate([part.T, jnp.zeros((LANES, LANES - blocks), F32)], axis=1)
        for q in range(4):
            start = (q // 2) * NODE + q % 2
            field_ref[c * LANES + q * pairs : c * LANES + (q + 1) * pairs, :] = turn_ref[pl.ds(start, pairs, stride=2), :]

    def product(g, carry):
        for j in range(SUB):
            b = g * SUB + j
            rows = [stiff_ref[e, g, pl.ds(j, pairs, stride=SUB), :] for e in range(nnz)]
            cols = [wide_ref[columns_ref[e, b]] for e in range(nnz)]
            left = []
            for e in range(0, nnz - 1, 2):
                x, y = rows[e], rows[e + 1]
                left.append(jnp.concatenate([jnp.where(half, x, swap(y)), jnp.where(half, swap(x), y)], axis=0))
            if nnz % 2:
                x = rows[nnz - 1]
                left.append(jnp.concatenate([x, swap(x)], axis=0)[:, :NODE])
            left = jnp.concatenate(left, axis=1)
            high, low = split(left)
            out = jnp.dot(
                jnp.concatenate([high, low], axis=0), jnp.concatenate(cols, axis=0), preferred_element_type=F32
            )
            out = out[:NODE] + out[NODE:]
            even, odd = out[:pairs], out[pairs:]
            out_ref[g, pl.ds(j, pairs, stride=SUB), :] = jnp.where(half, even, odd) + swap(
                jnp.where(half, odd, even)
            )
        return carry

    lax.fori_loop(0, groups, product, 0)


def contact_kernel(slot_ref, rows_ref, field_ref, own_ref, inner_ref, out_ref):
    cands, blocks = slot_ref.shape
    groups = blocks // SUB
    chunks = rows_ref.shape[1]
    pairs = NODE // 2
    half = left_half(pairs)
    quarter = left_half(chunks)
    chunk = lax.broadcasted_iota(jnp.int32, (chunks, LANES), 0)
    even_scale = jnp.where(chunk < 2, REACH, jnp.where(chunk == 2, 3.0 * TURN, TURN))
    odd_scale = jnp.where(chunk < 1, REACH, jnp.where(chunk < 3, 3.0 * TURN, 1.0))

    def one_group(g, carry):
        turned = pltpu.roll(field_ref[...], LANES - g * SUB, 1)
        for j in range(SUB):
            b = g * SUB + j
            x = rows_ref[slot_ref[0, b]]
            y = rows_ref[slot_ref[1, b]]
            even = jnp.where(quarter, x, swap(y)) * even_scale
            odd = jnp.where(quarter, swap(x), y) * odd_scale
            tool = [(even, odd)[f % 2][f // 2 : f // 2 + 1, :] for f in range(FIELDS)]

            def part(f):
                return jnp.broadcast_to(turned[f * NODE : (f + 1) * NODE, j : j + 1], (NODE, LANES))

            dist = None
            for f in range(3):
                gap = part(f) - tool[f]
                dist = gap * gap if dist is None else dist + gap * gap
            phase = part(3) * tool[3]
            for f in range(4, 7):
                phase = phase + part(f) * tool[f]
            turn = 0.25 - jnp.abs(phase - jnp.round(phase))
            square = turn * turn
            wave = SINE[4]
            for c in SINE[3::-1]:
                wave = wave * square + c
            slide = SHARE + (0.5 * SHARE) * jnp.tanh(part(7) * tool[7])
            tile = jnp.exp2(-dist) * (wave * turn) * slide
            high, low = split(tile)
            tall = jnp.concatenate([high, low], axis=0)
            gram = lax.dot_general(tall, tall, (((1,), (1,)), ((), ())), preferred_element_type=F32)
            gram = gram[:NODE] + gram[NODE:]
            gram = gram + swap(gram)
            high, low = split(gram)
            left = jnp.concatenate([high, low], axis=0)[:, :NODE]
            out = jnp.dot(left, own_ref[b], preferred_element_type=F32)
            out = out[:NODE] + out[NODE:]
            even_out, odd_out = out[:pairs], out[pairs:]
            spot = pl.ds(j, pairs, stride=SUB)
            out_ref[g, spot, :] = (
                inner_ref[g, spot, :] + jnp.where(half, even_out, odd_out) + swap(jnp.where(half, odd_out, even_out))
            )
        return carry

    lax.fori_loop(0, groups, one_group, 0)


def per_device(records, tool_data, owners, local_seg, active, stiffness, columns, vectors):
    peers = lax.axis_size(AXES)
    blocks, cands = owners.shape
    nnz = columns.shape[1]
    segs, width = tool_data.shape
    capacity = max(2, (3 * blocks * cands + 2 * peers - 1) // (2 * peers))
    groups = blocks // SUB
    pairs = NODE // 2
    chunks = width // LANES
    edge = jax.ShapeDtypeStruct((HB * pairs, LANES), F32)

    def tiles_of(x, rows):
        lead = x.shape[:-2]
        n = len(lead)
        x = x.reshape(lead + (rows // SUB, SUB, x.shape[-1] // LANES, LANES))
        x = jnp.swapaxes(x, n + 1, n + 2)
        return x.reshape(lead + (rows // SUB, -1, LANES))

    vec = tiles_of(vectors, blocks)
    stiff = tiles_of(jnp.swapaxes(stiffness, 0, 1), blocks)
    tool = tiles_of(tool_data, segs)

    send, slot, head, tail = pl.pallas_call(
        functools.partial(prep_kernel, capacity),
        grid=(1,),
        out_shape=(
            jax.ShapeDtypeStruct((peers, 1, LANES), jnp.int32),
            jax.ShapeDtypeStruct((cands, blocks), jnp.int32),
            edge,
            edge,
        ),
        in_specs=[
            pl.BlockSpec((cands, blocks), lambda i: (0, 0)),
            pl.BlockSpec((cands, blocks), lambda i: (0, 0)),
            pl.BlockSpec((1,) + vec.shape[1:], lambda i: (0, 0, 0)),
            pl.BlockSpec((1,) + vec.shape[1:], lambda i: (groups - 1, 0, 0)),
        ],
        out_specs=(
            pl.BlockSpec((peers, 1, LANES), lambda i: (0, 0, 0)),
            pl.BlockSpec((cands, blocks), lambda i: (0, 0)),
            pl.BlockSpec(edge.shape, lambda i: (0, 0)),
            pl.BlockSpec(edge.shape, lambda i: (0, 0)),
        ),
        compiler_params=params(8),
        name="prep",
    )(owners.T, local_seg.T, vec, vec)

    wanted = lax.all_to_all(send, AXES, split_axis=0, concat_axis=0, tiled=True)
    up = [(i, i + 1) for i in range(peers - 1)]
    down = [(j, i) for i, j in up]
    before = lax.ppermute(tail, AXES, up)
    after = lax.ppermute(head, AXES, down)

    rows_out = pl.pallas_call(
        functools.partial(rows_kernel, capacity),
        out_shape=jax.ShapeDtypeStruct((peers, capacity, chunks, LANES), F32),
        in_specs=[SMEM, VMEM],
        out_specs=VMEM,
        compiler_params=params(8),
        name="rows",
    )(wanted, tool)
    fetched = lax.all_to_all(rows_out, AXES, split_axis=0, concat_axis=0, tiled=True)

    inner, own, fields = pl.pallas_call(
        inner_kernel,
        out_shape=(
            jax.ShapeDtypeStruct(vec.shape, F32),
            jax.ShapeDtypeStruct((blocks, NODE, LANES), BF16),
            jax.ShapeDtypeStruct((width, LANES), F32),
        ),
        in_specs=[SMEM] + [VMEM] * 6,
        out_specs=(VMEM,) * 3,
        scratch_shapes=[
            pltpu.VMEM((blocks + 2 * HB, NODE, LANES), BF16),
            pltpu.VMEM((SUB, NODE, LANES), F32),
            pltpu.VMEM((LANES, LANES), F32),
        ],
        compiler_params=params(24),
        cost_estimate=pl.CostEstimate(flops=6 * blocks * nnz * NODE * NODE * NVEC, bytes_accessed=8 << 20, transcendentals=0),
        name="inner",
    )(columns.T, stiff, vec, before, after, records, active)

    out = pl.pallas_call(
        contact_kernel,
        out_shape=jax.ShapeDtypeStruct(vec.shape, F32),
        in_specs=[SMEM] + [VMEM] * 4,
        out_specs=VMEM,
        compiler_params=params(16),
        cost_estimate=pl.CostEstimate(
            flops=80 * blocks * cands * NODE * NODE, bytes_accessed=4 << 20, transcendentals=2 * blocks * cands * NODE * NODE
        ),
        name="contact",
    )(slot, fetched.reshape(peers * capacity, chunks, LANES), fields, own, inner)
    out = out.reshape(groups, pairs, SUB, LANES)
    return jnp.swapaxes(out, 1, 2).reshape(blocks, NODE * NVEC)


def solution(mesh):
    split_rows = P(AXES, None)
    return jax.shard_map(
        per_device,
        mesh=mesh,
        in_specs=(split_rows,) * 5 + (P(AXES, None, None),) + (split_rows,) * 2,
        out_specs=split_rows,
        check_vma=False,
    )
```

```python
import functools
import math

import jax
import jax.numpy as jnp
from jax import lax
from jax.experimental import pallas as pl
from jax.experimental.pallas import tpu as pltpu
from jax.sharding import PartitionSpec as P

NODE = 64
NVEC = 64
FIELDS = 8
HB = 2
LANES = 128
SUB = 8
AXES = ("dom", "tool")
TURN = 1.0 / (2.0 * math.pi)
REACH = math.sqrt(math.log2(math.e) / 4.0)
SHARE = math.sqrt(0.05)
FAR = -1e30
SINE = (6.283185160087854, -41.3416550310025, 81.60100404550954, -76.54978161791087, 39.53670066614222)
F32 = jnp.float32
BF16 = jnp.bfloat16
VMEM = pl.BlockSpec(memory_space=pltpu.VMEM)
SMEM = pl.BlockSpec(memory_space=pltpu.SMEM)
HBM = pl.BlockSpec(memory_space=pltpu.HBM)
STEP = 4
PARTS = 3


def params(mib):
    return pltpu.CompilerParams(vmem_limit_bytes=mib << 20)


def left_half(rows):
    return lax.broadcasted_iota(jnp.int32, (rows, LANES), 1) < NODE


def swap(x):
    return pltpu.roll(x, NODE, 1)


def split(x):
    high = x.astype(BF16)
    return high, (x - high.astype(F32)).astype(BF16)


def three(x):
    high = x.astype(BF16).astype(F32)
    rest = x - high
    mid = rest.astype(BF16).astype(F32)
    return high, mid, rest - mid


def fold(out, half):
    pairs = NODE // 2
    out = out[:NODE] + out[NODE:]
    even, odd = out[:pairs], out[pairs:]
    return jnp.where(half, even, odd) + swap(jnp.where(half, odd, even))


def copies_of(sources, targets, sems):
    made = [pltpu.make_async_copy(a, b, sems.at[i]) for i, (a, b) in enumerate(zip(sources, targets))]
    for copy in made:
        copy.start()
    return made


def pair_fields(x, y):
    quarter = left_half(x.shape[0])
    return jnp.concatenate([jnp.where(quarter, x, swap(y)), jnp.where(quarter, swap(x), y)], axis=0)


def field_rows(shape):
    row = lax.broadcasted_iota(jnp.int32, shape, 0)
    place = (row < 2) | (row == 4)
    return row, place, (row != 7) & ~place


def prep_kernel(
    segs, owners_hbm, seg_hbm, vec_hbm, want_ref, head_ref, tail_ref,
    owners_ref, seg_ref, first_ref, last_ref, sems,
):
    last = vec_hbm.shape[0] - 1
    got = copies_of(
        (owners_hbm, seg_hbm, vec_hbm.at[0], vec_hbm.at[last]), (owners_ref, seg_ref, first_ref, last_ref), sems
    )
    cands = owners_ref.shape[0]
    got[0].wait()
    got[1].wait()
    want_ref[...] = jnp.concatenate(
        [owners_ref[k : k + 1, :] * segs + seg_ref[k : k + 1, :] for k in range(cands)], axis=1
    )
    for copy in got[2:]:
        copy.wait()
    pairs = NODE // 2
    for h in range(HB):
        head_ref[h * pairs : (h + 1) * pairs, :] = first_ref[pl.ds(h, pairs, stride=SUB), :]
        tail_ref[h * pairs : (h + 1) * pairs, :] = last_ref[pl.ds(SUB - HB + h, pairs, stride=SUB), :]


def ranks(hits):
    n = hits.shape[1]
    upper = (
        lax.broadcasted_iota(jnp.int32, (n, n), 0) <= lax.broadcasted_iota(jnp.int32, (n, n), 1)
    ).astype(BF16)
    return jnp.dot(hits.astype(F32).astype(BF16), upper, preferred_element_type=F32)


def rows_kernel(capacity, want_ref, part_ref, out_ref):
    peers = want_ref.shape[0]
    segs, width = part_ref.shape[0], part_ref.shape[1] // PARTS
    chunks = width // LANES
    me = lax.axis_index(AXES[0]) * lax.axis_size(AXES[1]) + lax.axis_index(AXES[1])
    local = want_ref[...] - me * segs
    hits = (local >= 0) & (local < segs)
    rank = ranks(hits)
    seg = lax.broadcasted_iota(jnp.int32, (peers, segs), 1)
    picks = []
    for s in range(capacity):
        chosen = hits & (rank == s + 1.0)
        row = jnp.sum(jnp.where(chosen, local + 1, 0).astype(F32), axis=1, keepdims=True).astype(jnp.int32) - 1
        picks.append((seg == row).astype(F32).astype(BF16))
    picks = jnp.concatenate(picks, axis=0)
    for c in range(chunks):
        got = None
        for p in range(PARTS):
            at = p * width + c * LANES
            term = jnp.dot(picks, part_ref[:, at : at + LANES], preferred_element_type=F32)
            got = term if got is None else got + term
        for s in range(capacity):
            out_ref[pl.ds(s * chunks + c, peers, stride=capacity * chunks), :] = got[s * peers : (s + 1) * peers]


def inner_kernel(
    capacity, peers, columns_hbm, owners_hbm, vec_hbm, rec_hbm, act_hbm, stiff_hbm, tool_hbm,
    out_ref, own_ref, field_ref, part_ref, edge_ref, slot_ref,
    columns_ref, owners_ref, vec_ref, rec_ref, act_ref, stiff_ref, tool_ref, wide_ref, hold_ref, turn_ref, sems,
):
    nnz, groups = stiff_ref.shape[:2]
    blocks = groups * SUB
    pairs = NODE // 2
    half = left_half(pairs)
    full = left_half(NODE)
    got = copies_of(
        (columns_hbm, owners_hbm, vec_hbm, rec_hbm, act_hbm) + tuple(stiff_hbm.at[:, g] for g in range(groups)) + (tool_hbm,),
        (columns_ref, owners_ref, vec_ref, rec_ref, act_ref) + tuple(stiff_ref.at[:, g] for g in range(groups)) + (tool_ref,),
        sems,
    )
    got[1].wait()
    owner_ids = lax.broadcasted_iota(jnp.int32, (peers, blocks), 0)
    before = jnp.zeros((peers, 1), F32)
    for k in range(owners_ref.shape[0]):
        target = owners_ref[k : k + 1, :]
        hits = owner_ids == jnp.broadcast_to(target, (peers, blocks))
        counts = jnp.where(hits, before + ranks(hits) - 1.0, 0.0)
        before = before + jnp.sum(hits.astype(F32), axis=1, keepdims=True)
        slot_ref[k : k + 1, :] = target * capacity + jnp.sum(counts, axis=0, keepdims=True).astype(jnp.int32)

    got[0].wait()
    got[2].wait()
    zero = jnp.zeros((NODE, LANES), BF16)
    for h in range(HB):
        wide_ref[h] = zero
        wide_ref[blocks + HB + h] = zero

    def spread(g, carry):
        for j in range(SUB):
            x = vec_ref[g, pl.ds(j, pairs, stride=SUB), :]
            other = swap(x)
            even, odd = jnp.where(half, x, other), jnp.where(half, other, x)
            hold_ref[j, pl.ds(0, pairs, stride=2), :] = even
            hold_ref[j, pl.ds(1, pairs, stride=2), :] = odd
            both = jnp.concatenate([even, odd], axis=0)
            own_ref[g * SUB + j] = jnp.where(full, both, both - both.astype(BF16).astype(F32)).astype(BF16)
        for j in range(SUB):
            whole = hold_ref[j]
            wide_ref[HB + g * SUB + j] = jnp.where(full, whole, whole - whole.astype(BF16).astype(F32)).astype(BF16)
        return carry

    lax.fori_loop(0, groups, spread, 0)

    got[3].wait()
    got[4].wait()
    row, place, _ = field_rows((SUB, LANES))
    scale = jnp.where(place, REACH, 1.0)

    def fields(g, carry):
        for j in range(0, SUB, 2):
            x = rec_ref[g, pl.ds(j, FIELDS // 2, stride=SUB), :]
            y = rec_ref[g, pl.ds(j + 1, FIELDS // 2, stride=SUB), :]
            part = pair_fields(x, y) * scale
            norm = -0.5 * jnp.sum(jnp.where(place, part * part, 0.0), axis=0, keepdims=True)
            at = g * SUB + j
            flags = jnp.concatenate([act_ref[pl.ds(at, 1), :], act_ref[pl.ds(at + 1, 1), :]], axis=1)
            norm = jnp.where(flags == 0, FAR, norm)
            h, m, l = three(part)
            nh, nm, nl = three(norm)
            extra = jnp.where(row == 0, nh, jnp.where(row == 1, nm, jnp.where(row == 2, nl, jnp.where(row < 6, 1.0, 0.0))))
            stack = jnp.concatenate([h, h, m, h, l, m, extra, jnp.zeros((LANES - 7 * SUB, LANES), F32)], axis=0)
            turn_ref[j // 2] = stack.T
        for j in range(SUB):
            for q in range(2):
                field_ref[g * SUB + j, q * pairs : (q + 1) * pairs, :] = turn_ref[
                    j // 2, pl.ds((j % 2) * NODE + q, pairs, stride=2), :
                ].astype(BF16)
        return carry

    lax.fori_loop(0, groups, fields, 0)

    def left_of(g, j):
        rows = [stiff_ref[e, g, pl.ds(j, pairs, stride=SUB), :] for e in range(nnz)]
        left = []
        for e in range(0, nnz - 1, 2):
            x, y = rows[e], rows[e + 1]
            left.append(jnp.concatenate([jnp.where(half, x, swap(y)), jnp.where(half, swap(x), y)], axis=0))
        if nnz % 2:
            x = rows[nnz - 1]
            left.append(jnp.concatenate([x, swap(x)], axis=0)[:, :NODE])
        return jnp.concatenate(split(jnp.concatenate(left, axis=1)), axis=0)

    def product(g, carry):
        for i in range(groups):

            @pl.when(g == i)
            def _():
                got[5 + i].wait()

        for j in range(SUB):
            b = g * SUB + j
            cols = [wide_ref[columns_ref[e, b]] for e in range(nnz)]
            out = jnp.dot(left_of(g, j), jnp.concatenate(cols, axis=0), preferred_element_type=F32)
            out_ref[g, pl.ds(j, pairs, stride=SUB), :] = fold(out, half)
        return carry

    lax.fori_loop(0, groups, product, 0)
    for i in range(2 * HB):
        edge_ref[i] = left_of(*((0, i) if i < HB else (groups - 1, SUB - 2 * HB + i)))

    got[5 + groups].wait()
    width = tool_ref.shape[1]
    for p, part in enumerate(three(tool_ref[...])):
        part_ref[:, p * width : (p + 1) * width] = part.astype(BF16)


def edge_kernel(columns_ref, edge_ref, before_ref, after_ref, out_ref, wide_ref, hold_ref):
    nnz, blocks = columns_ref.shape
    pairs = NODE // 2
    half = left_half(pairs)
    full = left_half(NODE)
    for h in range(2 * HB):
        source = before_ref if h < HB else after_ref
        at = (h % HB) * pairs
        x = source[at : at + pairs, :]
        other = swap(x)
        hold_ref[h, pl.ds(0, pairs, stride=2), :] = jnp.where(half, x, other)
        hold_ref[h, pl.ds(1, pairs, stride=2), :] = jnp.where(half, other, x)
        whole = hold_ref[h]
        wide_ref[h] = jnp.where(full, whole, whole - whole.astype(BF16).astype(F32)).astype(BF16)
    wide_ref[2 * HB] = jnp.zeros((NODE, LANES), BF16)
    for i in range(2 * HB):
        b = i if i < HB else blocks - 2 * HB + i
        cols = []
        for e in range(nnz):
            c = columns_ref[e, b]
            spot = jnp.where(c < HB, c, jnp.where(c >= blocks + HB, c - blocks, 2 * HB))
            cols.append(wide_ref[spot])
        out = jnp.dot(edge_ref[i], jnp.concatenate(cols, axis=0), preferred_element_type=F32)
        out_ref[i * pairs : (i + 1) * pairs, :] = fold(out, half)


def contact_kernel(slot_ref, rows_ref, field_ref, own_ref, inner_ref, delta_ref, out_ref, raw_ref, tall_ref, gram_ref):
    blocks = slot_ref.shape[1]
    groups = blocks // SUB
    steps = blocks // STEP
    per = SUB // STEP
    pairs = NODE // 2
    half = left_half(pairs)
    row, place, angle = field_rows((SUB, LANES))
    slide = row == 7
    scale = jnp.where(place, REACH, jnp.where(row == 3, TURN, jnp.where(angle, 3.0 * TURN, 1.0)))
    none = jnp.zeros((SUB, LANES), F32)

    def sums(t):
        for j in range(STEP):
            b = t * STEP + j
            tool = pair_fields(rows_ref[slot_ref[0, b]], rows_ref[slot_ref[1, b]]) * scale
            norm = -0.5 * jnp.sum(jnp.where(place, tool * tool, 0.0), axis=0, keepdims=True)
            h, m, l = three(tool)
            nh, nm, nl = three(norm)
            extra = jnp.where(row < 3, 1.0, jnp.where(row == 3, nh, jnp.where(row == 4, nm, jnp.where(row == 5, nl, 0.0))))
            right = []
            for mask, more in ((place, extra), (angle, none), (slide, none)):
                hm, mm, lm = (jnp.where(mask, v, 0.0) for v in (h, m, l))
                right.append(jnp.concatenate([hm, mm, hm, lm, hm, mm, more, none], axis=0).astype(BF16))
            raw_ref[j] = jnp.dot(
                field_ref[b][:, :NODE], jnp.concatenate(right, axis=1), preferred_element_type=F32
            )

    def tiles(t):
        for j in range(STEP):
            phase = raw_ref[j, :, LANES : 2 * LANES]
            turn = 0.25 - jnp.abs(phase - jnp.round(phase))
            square = turn * turn
            wave = SINE[4]
            for c in SINE[3::-1]:
                wave = wave * square + c
            sliding = SHARE + (0.5 * SHARE) * jnp.tanh(raw_ref[j, :, 2 * LANES :])
            tile = jnp.exp2(raw_ref[j, :, :LANES]) * (wave * turn) * sliding
            high, low = split(tile)
            tall_ref[j, :NODE, :] = high
            tall_ref[j, NODE:, :] = low

    def grams(t):
        for j in range(STEP):
            tall = tall_ref[j]
            gram = lax.dot_general(tall, tall, (((1,), (1,)), ((), ())), preferred_element_type=F32)
            gram = gram[:NODE] + gram[NODE:]
            high, low = split(gram + swap(gram))
            gram_ref[j, :NODE, :] = high
            gram_ref[j, NODE:, :] = low

    def apply(t):
        for j in range(STEP):
            out = jnp.dot(gram_ref[j][:, :NODE], own_ref[t * STEP + j], preferred_element_type=F32)
            spot = pl.ds(t % per * STEP + j, pairs, stride=SUB)
            out_ref[t // per, spot, :] = inner_ref[t // per, spot, :] + fold(out, half)

    stages = (apply, grams, tiles, sums)
    depth = len(stages) - 1
    for t in range(depth):
        for k in range(depth - t, depth + 1):
            stages[k](t - depth + k)

    def body(t, carry):
        for k in range(depth + 1):
            stages[k](t - depth + k)
        return carry

    lax.fori_loop(depth, steps, body, 0)
    for t in range(steps, steps + depth):
        for k in range(depth + 1):
            if t - depth + k < steps:
                stages[k](t - depth + k)
    for i in range(2 * HB):
        g, j = (0, i) if i < HB else (groups - 1, SUB - 2 * HB + i)
        spot = pl.ds(j, pairs, stride=SUB)
        out_ref[g, spot, :] = out_ref[g, spot, :] + delta_ref[i * pairs : (i + 1) * pairs, :]


def per_device(records, tool_data, owners, local_seg, active, stiffness, columns, vectors):
    peers = lax.axis_size(AXES)
    blocks, cands = owners.shape
    nnz = columns.shape[1]
    segs, width = tool_data.shape
    capacity = max(2, (3 * blocks * cands + 2 * peers - 1) // (2 * peers))
    groups = blocks // SUB
    pairs = NODE // 2
    chunks = width // LANES
    i32 = jnp.int32

    def shape(dims, dtype=F32):
        return jax.ShapeDtypeStruct(dims, dtype)

    def tiles_of(x, rows):
        lead = x.shape[:-2]
        n = len(lead)
        x = x.reshape(lead + (rows // SUB, SUB, x.shape[-1] // LANES, LANES))
        x = jnp.swapaxes(x, n + 1, n + 2)
        return x.reshape(lead + (rows // SUB, -1, LANES))

    vec = tiles_of(vectors, blocks)
    rec = tiles_of(records, blocks)
    stiff = tiles_of(jnp.swapaxes(stiffness, 0, 1), blocks)
    edge = shape((HB * pairs, LANES))

    want, head, tail = pl.pallas_call(
        functools.partial(prep_kernel, segs),
        out_shape=(shape((1, cands * blocks), i32), edge, edge),
        in_specs=[HBM] * 3,
        out_specs=(VMEM,) * 3,
        scratch_shapes=[
            pltpu.VMEM((cands, blocks), i32),
            pltpu.VMEM((cands, blocks), i32),
            pltpu.VMEM(vec.shape[1:], F32),
            pltpu.VMEM(vec.shape[1:], F32),
            pltpu.SemaphoreType.DMA((4,)),
        ],
        compiler_params=params(8),
        name="prep",
    )(owners.T, local_seg.T, vec)

    wanted = lax.all_gather(want, AXES, axis=0, tiled=True)

    inner, own, fields, parts, edges, slot = pl.pallas_call(
        functools.partial(inner_kernel, capacity, peers),
        out_shape=(
            shape(vec.shape),
            shape((blocks, NODE, LANES), BF16),
            shape((blocks, NODE, LANES), BF16),
            shape((segs, PARTS * width), BF16),
            shape((2 * HB, 2 * NODE, nnz * NODE), BF16),
            shape((cands, blocks), i32),
        ),
        in_specs=[HBM] * 7,
        out_specs=(VMEM,) * 6,
        scratch_shapes=[
            pltpu.SMEM((nnz, blocks), i32),
            pltpu.VMEM((cands, blocks), i32),
            pltpu.VMEM(vec.shape, F32),
            pltpu.VMEM(rec.shape, F32),
            pltpu.VMEM(active.shape, i32),
            pltpu.VMEM(stiff.shape, F32),
            pltpu.VMEM(tool_data.shape, F32),
            pltpu.VMEM((blocks + 2 * HB, NODE, LANES), BF16),
            pltpu.VMEM((SUB, NODE, LANES), F32),
            pltpu.VMEM((SUB // 2, LANES, LANES), F32),
            pltpu.SemaphoreType.DMA((groups + 6,)),
        ],
        compiler_params=params(28),
        cost_estimate=pl.CostEstimate(
            flops=6 * blocks * nnz * NODE * NODE * NVEC, bytes_accessed=16 << 20, transcendentals=0
        ),
        name="inner",
    )(columns.T, owners.T, vec, rec, active, stiff, tool_data)

    rows_out = pl.pallas_call(
        functools.partial(rows_kernel, capacity),
        out_shape=shape((peers * capacity * chunks, LANES)),
        in_specs=[VMEM] * 2,
        out_specs=VMEM,
        compiler_params=params(8),
        name="rows",
    )(wanted, parts)
    fetched = lax.all_to_all(
        rows_out.reshape(peers, capacity * chunks, LANES), AXES, split_axis=0, concat_axis=0, tiled=True
    )

    up = [(i, i + 1) for i in range(peers - 1)]
    down = [(j, i) for i, j in up]
    before = lax.ppermute(tail, AXES, up)
    after = lax.ppermute(head, AXES, down)
    delta = pl.pallas_call(
        edge_kernel,
        out_shape=shape((2 * HB * pairs, LANES)),
        in_specs=[SMEM] + [VMEM] * 3,
        out_specs=VMEM,
        scratch_shapes=[
            pltpu.VMEM((2 * HB + 1, NODE, LANES), BF16),
            pltpu.VMEM((2 * HB, NODE, LANES), F32),
        ],
        compiler_params=params(8),
        name="edge",
    )(columns.T, edges, before, after)

    out = pl.pallas_call(
        contact_kernel,
        out_shape=shape(vec.shape),
        in_specs=[SMEM] + [VMEM] * 5,
        out_specs=VMEM,
        scratch_shapes=[
            pltpu.VMEM((STEP, NODE, 3 * LANES), F32),
            pltpu.VMEM((STEP, 2 * NODE, LANES), BF16),
            pltpu.VMEM((STEP, 2 * NODE, LANES), BF16),
        ],
        compiler_params=params(16),
        cost_estimate=pl.CostEstimate(
            flops=80 * blocks * cands * NODE * NODE, bytes_accessed=4 << 20, transcendentals=2 * blocks * cands * NODE * NODE
        ),
        name="contact",
    )(slot, fetched.reshape(peers * capacity, chunks, LANES), fields, own, inner, delta)
    out = out.reshape(groups, pairs, SUB, LANES)
    return jnp.swapaxes(out, 1, 2).reshape(blocks, NODE * NVEC)


def solution(mesh):
    split_rows = P(AXES, None)
    return jax.shard_map(
        per_device,
        mesh=mesh,
        in_specs=(split_rows,) * 5 + (P(AXES, None, None),) + (split_rows,) * 2,
        out_specs=split_rows,
        check_vma=False,
    )
```

```python
import functools
import math

import jax
import jax.numpy as jnp
from jax import lax
from jax.experimental import pallas as pl
from jax.experimental.pallas import tpu as pltpu
from jax.sharding import PartitionSpec as P

NODE = 64
NVEC = 64
FIELDS = 8
HB = 2
LANES = 128
SUB = 8
AXES = ("dom", "tool")
TURN = 1.0 / (2.0 * math.pi)
REACH = math.sqrt(math.log2(math.e) / 4.0)
SHARE = math.sqrt(0.05)
FAR = -1e30
SINE = (6.283185160087854, -41.3416550310025, 81.60100404550954, -76.54978161791087, 39.53670066614222)
F32 = jnp.float32
BF16 = jnp.bfloat16
VMEM = pl.BlockSpec(memory_space=pltpu.VMEM)
SMEM = pl.BlockSpec(memory_space=pltpu.SMEM)
HBM = pl.BlockSpec(memory_space=pltpu.HBM)
STEP = 4
PARTS = 3


def params(mib):
    return pltpu.CompilerParams(vmem_limit_bytes=mib << 20)


def left_half(rows):
    return lax.broadcasted_iota(jnp.int32, (rows, LANES), 1) < NODE


def swap(x):
    return pltpu.roll(x, NODE, 1)


def split(x):
    high = x.astype(BF16)
    return high, (x - high.astype(F32)).astype(BF16)


def three(x):
    high = x.astype(BF16).astype(F32)
    rest = x - high
    mid = rest.astype(BF16).astype(F32)
    return high, mid, rest - mid


def fold(out, half):
    pairs = NODE // 2
    out = out[:NODE] + out[NODE:]
    even, odd = out[:pairs], out[pairs:]
    return jnp.where(half, even, odd) + swap(jnp.where(half, odd, even))


def copies_of(sources, targets, sems):
    made = [pltpu.make_async_copy(a, b, sems.at[i]) for i, (a, b) in enumerate(zip(sources, targets))]
    for copy in made:
        copy.start()
    return made


def pair_fields(x, y):
    quarter = left_half(x.shape[0])
    return jnp.concatenate([jnp.where(quarter, x, swap(y)), jnp.where(quarter, swap(x), y)], axis=0)


def field_rows(shape):
    row = lax.broadcasted_iota(jnp.int32, shape, 0)
    place = (row < 2) | (row == 4)
    return row, place, (row != 7) & ~place


def ranks(hits):
    n = hits.shape[1]
    upper = (
        lax.broadcasted_iota(jnp.int32, (n, n), 0) <= lax.broadcasted_iota(jnp.int32, (n, n), 1)
    ).astype(BF16)
    return jnp.dot(hits.astype(F32).astype(BF16), upper, preferred_element_type=F32)


def prep_kernel(capacity, owners_hbm, seg_hbm, send_ref, slot_ref, owners_ref, seg_ref, sems):
    for copy in copies_of((owners_hbm, seg_hbm), (owners_ref, seg_ref), sems):
        copy.wait()
    cands, blocks = owners_ref.shape
    peers = send_ref.shape[0]
    owner_ids = lax.broadcasted_iota(jnp.int32, (peers, blocks), 0)
    lanes = lax.broadcasted_iota(jnp.int32, (peers, LANES), 1)
    send = jnp.zeros((peers, LANES), jnp.int32)
    before = jnp.zeros((peers, 1), F32)
    for k in range(cands):
        target = owners_ref[k : k + 1, :]
        hits = owner_ids == jnp.broadcast_to(target, (peers, blocks))
        places = jnp.where(hits, before + ranks(hits) - 1.0, -1.0)
        before = before + jnp.sum(hits.astype(F32), axis=1, keepdims=True)
        rank = jnp.sum(jnp.maximum(places, 0.0), axis=0, keepdims=True)
        slot_ref[k : k + 1, :] = target * capacity + rank.astype(jnp.int32)
        wanted = jnp.broadcast_to(seg_ref[k : k + 1, :].astype(F32), (peers, blocks))
        for s in range(capacity):
            named = jnp.sum(jnp.where(places == float(s), wanted, 0.0), axis=1, keepdims=True)
            send = send + jnp.where(lanes == s, named.astype(jnp.int32), 0)
    send_ref[...] = send


def rows_kernel(capacity, want_ref, part_ref, out_ref):
    peers = want_ref.shape[0]
    segs, width = part_ref.shape[0], part_ref.shape[1] // PARTS
    chunks = width // LANES
    seg = lax.broadcasted_iota(jnp.int32, (peers, segs), 1)
    want = want_ref[...]
    picks = jnp.concatenate([(seg == want[:, s : s + 1]).astype(F32).astype(BF16) for s in range(capacity)], axis=0)
    for c in range(chunks):
        got = None
        for p in range(PARTS):
            at = p * width + c * LANES
            term = jnp.dot(picks, part_ref[:, at : at + LANES], preferred_element_type=F32)
            got = term if got is None else got + term
        for s in range(capacity):
            out_ref[pl.ds(s * chunks + c, peers, stride=capacity * chunks), :] = got[s * peers : (s + 1) * peers]


def early_kernel(
    after_prep, vec_hbm, rec_hbm, act_hbm, tool_hbm, own_ref, wide_ref, field_ref, part_ref, head_ref, tail_ref,
    vec_ref, rec_ref, act_ref, tool_ref, hold_ref, turn_ref, sems,
):
    groups = vec_ref.shape[0]
    blocks = groups * SUB
    pairs = NODE // 2
    half = left_half(pairs)
    full = left_half(NODE)
    got = copies_of((tool_hbm, vec_hbm, rec_hbm, act_hbm), (tool_ref, vec_ref, rec_ref, act_ref), sems)
    got[0].wait()
    width = tool_ref.shape[1]
    for p, part in enumerate(three(tool_ref[...])):
        part_ref[:, p * width : (p + 1) * width] = part.astype(BF16)

    got[1].wait()
    zero = jnp.zeros((NODE, LANES), BF16)
    for h in range(HB):
        wide_ref[h] = zero
        wide_ref[blocks + HB + h] = zero
        head_ref[h * pairs : (h + 1) * pairs, :] = vec_ref[0, pl.ds(h, pairs, stride=SUB), :]
        tail_ref[h * pairs : (h + 1) * pairs, :] = vec_ref[groups - 1, pl.ds(SUB - HB + h, pairs, stride=SUB), :]

    def spread(g, carry):
        for j in range(SUB):
            x = vec_ref[g, pl.ds(j, pairs, stride=SUB), :]
            other = swap(x)
            even, odd = jnp.where(half, x, other), jnp.where(half, other, x)
            hold_ref[j, pl.ds(0, pairs, stride=2), :] = even
            hold_ref[j, pl.ds(1, pairs, stride=2), :] = odd
            both = jnp.concatenate([even, odd], axis=0)
            own_ref[g * SUB + j] = jnp.where(full, both, both - both.astype(BF16).astype(F32)).astype(BF16)
        for j in range(SUB):
            whole = hold_ref[j]
            wide_ref[HB + g * SUB + j] = jnp.where(full, whole, whole - whole.astype(BF16).astype(F32)).astype(BF16)
        return carry

    lax.fori_loop(0, groups, spread, 0)

    got[2].wait()
    got[3].wait()
    row, place, _ = field_rows((SUB, LANES))
    scale = jnp.where(place, REACH, 1.0)

    def fields(g, carry):
        for j in range(0, SUB, 2):
            x = rec_ref[g, pl.ds(j, FIELDS // 2, stride=SUB), :]
            y = rec_ref[g, pl.ds(j + 1, FIELDS // 2, stride=SUB), :]
            part = pair_fields(x, y) * scale
            norm = -0.5 * jnp.sum(jnp.where(place, part * part, 0.0), axis=0, keepdims=True)
            at = g * SUB + j
            flags = jnp.concatenate([act_ref[pl.ds(at, 1), :], act_ref[pl.ds(at + 1, 1), :]], axis=1)
            norm = jnp.where(flags == 0, FAR, norm)
            h, m, l = three(part)
            nh, nm, nl = three(norm)
            extra = jnp.where(row == 0, nh, jnp.where(row == 1, nm, jnp.where(row == 2, nl, jnp.where(row < 6, 1.0, 0.0))))
            stack = jnp.concatenate([h, h, m, h, l, m, extra, jnp.zeros((LANES - 7 * SUB, LANES), F32)], axis=0)
            turn_ref[j // 2] = stack.T
        for j in range(SUB):
            for q in range(2):
                field_ref[g * SUB + j, q * pairs : (q + 1) * pairs, :] = turn_ref[
                    j // 2, pl.ds((j % 2) * NODE + q, pairs, stride=2), :
                ].astype(BF16)
        return carry

    lax.fori_loop(0, groups, fields, 0)


def inner_kernel(columns_hbm, stiff_hbm, wide_ref, out_ref, edge_ref, columns_ref, stiff_ref, sems):
    nnz, groups = stiff_ref.shape[:2]
    pairs = NODE // 2
    half = left_half(pairs)
    got = copies_of(
        (columns_hbm,) + tuple(stiff_hbm.at[:, g] for g in range(groups)),
        (columns_ref,) + tuple(stiff_ref.at[:, g] for g in range(groups)),
        sems,
    )
    got[0].wait()

    def left_of(g, j):
        rows = [stiff_ref[e, g, pl.ds(j, pairs, stride=SUB), :] for e in range(nnz)]
        left = []
        for e in range(0, nnz - 1, 2):
            x, y = rows[e], rows[e + 1]
            left.append(jnp.concatenate([jnp.where(half, x, swap(y)), jnp.where(half, swap(x), y)], axis=0))
        if nnz % 2:
            x = rows[nnz - 1]
            left.append(jnp.concatenate([x, swap(x)], axis=0)[:, :NODE])
        return jnp.concatenate(split(jnp.concatenate(left, axis=1)), axis=0)

    def product(g, carry):
        for i in range(groups):

            @pl.when(g == i)
            def _():
                got[1 + i].wait()

        for j in range(SUB):
            b = g * SUB + j
            cols = [wide_ref[columns_ref[e, b]] for e in range(nnz)]
            out = jnp.dot(left_of(g, j), jnp.concatenate(cols, axis=0), preferred_element_type=F32)
            out_ref[g, pl.ds(j, pairs, stride=SUB), :] = fold(out, half)
        return carry

    lax.fori_loop(0, groups, product, 0)
    for i in range(2 * HB):
        edge_ref[i] = left_of(*((0, i) if i < HB else (groups - 1, SUB - 2 * HB + i)))


def edge_kernel(columns_hbm, edge_ref, before_ref, after_ref, out_ref, columns_ref, wide_ref, hold_ref, sems):
    nnz, blocks = columns_ref.shape
    copies = copies_of((columns_hbm,), (columns_ref,), sems)
    pairs = NODE // 2
    half = left_half(pairs)
    full = left_half(NODE)
    for h in range(2 * HB):
        source = before_ref if h < HB else after_ref
        at = (h % HB) * pairs
        x = source[at : at + pairs, :]
        other = swap(x)
        hold_ref[h, pl.ds(0, pairs, stride=2), :] = jnp.where(half, x, other)
        hold_ref[h, pl.ds(1, pairs, stride=2), :] = jnp.where(half, other, x)
        whole = hold_ref[h]
        wide_ref[h] = jnp.where(full, whole, whole - whole.astype(BF16).astype(F32)).astype(BF16)
    wide_ref[2 * HB] = jnp.zeros((NODE, LANES), BF16)
    copies[0].wait()
    for i in range(2 * HB):
        b = i if i < HB else blocks - 2 * HB + i
        cols = []
        for e in range(nnz):
            c = columns_ref[e, b]
            spot = jnp.where(c < HB, c, jnp.where(c >= blocks + HB, c - blocks, 2 * HB))
            cols.append(wide_ref[spot])
        out = jnp.dot(edge_ref[i], jnp.concatenate(cols, axis=0), preferred_element_type=F32)
        out_ref[i * pairs : (i + 1) * pairs, :] = fold(out, half)


def contact_kernel(
    slot_hbm, rows_ref, field_ref, own_ref, inner_ref, delta_ref, out_ref, slot_ref, raw_ref, tall_ref, gram_ref, sems
):
    copies_of((slot_hbm,), (slot_ref,), sems)[0].wait()
    blocks = slot_ref.shape[1]
    groups = blocks // SUB
    steps = blocks // STEP
    per = SUB // STEP
    pairs = NODE // 2
    half = left_half(pairs)
    row, place, angle = field_rows((SUB, LANES))
    slide = row == 7
    scale = jnp.where(place, REACH, jnp.where(row == 3, TURN, jnp.where(angle, 3.0 * TURN, 1.0)))
    none = jnp.zeros((SUB, LANES), F32)

    def sums(t):
        for j in range(STEP):
            b = t * STEP + j
            tool = pair_fields(rows_ref[slot_ref[0, b]], rows_ref[slot_ref[1, b]]) * scale
            norm = -0.5 * jnp.sum(jnp.where(place, tool * tool, 0.0), axis=0, keepdims=True)
            h, m, l = three(tool)
            nh, nm, nl = three(norm)
            extra = jnp.where(row < 3, 1.0, jnp.where(row == 3, nh, jnp.where(row == 4, nm, jnp.where(row == 5, nl, 0.0))))
            right = []
            for mask, more in ((place, extra), (angle, none), (slide, none)):
                hm, mm, lm = (jnp.where(mask, v, 0.0) for v in (h, m, l))
                right.append(jnp.concatenate([hm, mm, hm, lm, hm, mm, more, none], axis=0).astype(BF16))
            raw_ref[j] = jnp.dot(
                field_ref[b][:, :NODE], jnp.concatenate(right, axis=1), preferred_element_type=F32
            )

    def tiles(t):
        for j in range(STEP):
            phase = raw_ref[j, :, LANES : 2 * LANES]
            turn = 0.25 - jnp.abs(phase - jnp.round(phase))
            square = turn * turn
            wave = SINE[4]
            for c in SINE[3::-1]:
                wave = wave * square + c
            sliding = SHARE + (0.5 * SHARE) * jnp.tanh(raw_ref[j, :, 2 * LANES :])
            tile = jnp.exp2(raw_ref[j, :, :LANES]) * (wave * turn) * sliding
            high, low = split(tile)
            tall_ref[j, :NODE, :] = high
            tall_ref[j, NODE:, :] = low

    def grams(t):
        for j in range(STEP):
            tall = tall_ref[j]
            gram = lax.dot_general(tall, tall, (((1,), (1,)), ((), ())), preferred_element_type=F32)
            gram = gram[:NODE] + gram[NODE:]
            high, low = split(gram + swap(gram))
            gram_ref[j, :NODE, :] = high
            gram_ref[j, NODE:, :] = low

    def apply(t):
        for j in range(STEP):
            out = jnp.dot(gram_ref[j][:, :NODE], own_ref[t * STEP + j], preferred_element_type=F32)
            spot = pl.ds(t % per * STEP + j, pairs, stride=SUB)
            out_ref[t // per, spot, :] = inner_ref[t // per, spot, :] + fold(out, half)

    stages = (apply, grams, tiles, sums)
    depth = len(stages) - 1
    for t in range(depth):
        for k in range(depth - t, depth + 1):
            stages[k](t - depth + k)

    def body(t, carry):
        for k in range(depth + 1):
            stages[k](t - depth + k)
        return carry

    lax.fori_loop(depth, steps, body, 0)
    for t in range(steps, steps + depth):
        for k in range(depth + 1):
            if t - depth + k < steps:
                stages[k](t - depth + k)
    for i in range(2 * HB):
        g, j = (0, i) if i < HB else (groups - 1, SUB - 2 * HB + i)
        spot = pl.ds(j, pairs, stride=SUB)
        out_ref[g, spot, :] = out_ref[g, spot, :] + delta_ref[i * pairs : (i + 1) * pairs, :]


def per_device(records, tool_data, owners, local_seg, active, stiffness, columns, vectors):
    peers = lax.axis_size(AXES)
    blocks, cands = owners.shape
    nnz = columns.shape[1]
    segs, width = tool_data.shape
    capacity = max(2, (3 * blocks * cands + 2 * peers - 1) // (2 * peers))
    groups = blocks // SUB
    pairs = NODE // 2
    chunks = width // LANES
    i32 = jnp.int32

    def shape(dims, dtype=F32):
        return jax.ShapeDtypeStruct(dims, dtype)

    def tiles_of(x, rows):
        lead = x.shape[:-2]
        n = len(lead)
        x = x.reshape(lead + (rows // SUB, SUB, x.shape[-1] // LANES, LANES))
        x = jnp.swapaxes(x, n + 1, n + 2)
        return x.reshape(lead + (rows // SUB, -1, LANES))

    vec = tiles_of(vectors, blocks)
    rec = tiles_of(records, blocks)
    stiff = tiles_of(jnp.swapaxes(stiffness, 0, 1), blocks)
    edge = shape((HB * pairs, LANES))

    def in_hbm(*arrays):
        return [pltpu.with_memory_space_constraint(x, pltpu.HBM) for x in arrays]

    send, slot = pl.pallas_call(
        functools.partial(prep_kernel, capacity),
        out_shape=(shape((peers, LANES), i32), shape((cands, blocks), i32)),
        in_specs=[HBM] * 2,
        out_specs=(VMEM,) * 2,
        scratch_shapes=[
            pltpu.VMEM((cands, blocks), i32),
            pltpu.VMEM((cands, blocks), i32),
            pltpu.SemaphoreType.DMA((2,)),
        ],
        compiler_params=params(8),
        name="prep",
    )(*in_hbm(owners.T, local_seg.T))

    wanted = lax.all_to_all(send.reshape(peers, 1, LANES), AXES, split_axis=0, concat_axis=0, tiled=True)

    own, wide, fields, parts, head, tail = pl.pallas_call(
        early_kernel,
        out_shape=(
            shape((blocks, NODE, LANES), BF16),
            shape((blocks + 2 * HB, NODE, LANES), BF16),
            shape((blocks, NODE, LANES), BF16),
            shape((segs, PARTS * width), BF16),
            edge,
            edge,
        ),
        in_specs=[HBM] * 5,
        out_specs=(VMEM,) * 6,
        scratch_shapes=[
            pltpu.VMEM(vec.shape, F32),
            pltpu.VMEM(rec.shape, F32),
            pltpu.VMEM(active.shape, i32),
            pltpu.VMEM(tool_data.shape, F32),
            pltpu.VMEM((SUB, NODE, LANES), F32),
            pltpu.VMEM((SUB // 2, LANES, LANES), F32),
            pltpu.SemaphoreType.DMA((4,)),
        ],
        compiler_params=params(16),
        cost_estimate=pl.CostEstimate(flops=1 << 20, bytes_accessed=8 << 20, transcendentals=0),
        name="early",
    )(*in_hbm(slot, vec, rec, active, tool_data))

    rows_out = pl.pallas_call(
        functools.partial(rows_kernel, capacity),
        out_shape=shape((peers * capacity * chunks, LANES)),
        in_specs=[VMEM] * 2,
        out_specs=VMEM,
        compiler_params=params(8),
        name="rows",
    )(wanted.reshape(peers, LANES), parts)
    fetched = lax.all_to_all(
        rows_out.reshape(peers, capacity * chunks, LANES), AXES, split_axis=0, concat_axis=0, tiled=True
    )

    up = [(i, i + 1) for i in range(peers - 1)]
    down = [(j, i) for i, j in up]
    before = lax.ppermute(tail, AXES, up)
    after = lax.ppermute(head, AXES, down)

    inner, edges = pl.pallas_call(
        inner_kernel,
        out_shape=(shape(vec.shape), shape((2 * HB, 2 * NODE, nnz * NODE), BF16)),
        in_specs=[HBM] * 2 + [VMEM],
        out_specs=(VMEM,) * 2,
        scratch_shapes=[
            pltpu.SMEM((nnz, blocks), i32),
            pltpu.VMEM(stiff.shape, F32),
            pltpu.SemaphoreType.DMA((groups + 1,)),
        ],
        compiler_params=params(16),
        cost_estimate=pl.CostEstimate(
            flops=6 * blocks * nnz * NODE * NODE * NVEC, bytes_accessed=16 << 20, transcendentals=0
        ),
        name="inner",
    )(*in_hbm(columns.T, stiff), wide)

    delta = pl.pallas_call(
        edge_kernel,
        out_shape=shape((2 * HB * pairs, LANES)),
        in_specs=[HBM] + [VMEM] * 3,
        out_specs=VMEM,
        scratch_shapes=[
            pltpu.SMEM((nnz, blocks), i32),
            pltpu.VMEM((2 * HB + 1, NODE, LANES), BF16),
            pltpu.VMEM((2 * HB, NODE, LANES), F32),
            pltpu.SemaphoreType.DMA((1,)),
        ],
        compiler_params=params(8),
        name="edge",
    )(*in_hbm(columns.T), edges, before, after)

    out = pl.pallas_call(
        contact_kernel,
        out_shape=shape(vec.shape),
        in_specs=[HBM] + [VMEM] * 5,
        out_specs=VMEM,
        scratch_shapes=[
            pltpu.SMEM((cands, blocks), i32),
            pltpu.VMEM((STEP, NODE, 3 * LANES), F32),
            pltpu.VMEM((STEP, 2 * NODE, LANES), BF16),
            pltpu.VMEM((STEP, 2 * NODE, LANES), BF16),
            pltpu.SemaphoreType.DMA((1,)),
        ],
        compiler_params=params(16),
        cost_estimate=pl.CostEstimate(
            flops=80 * blocks * cands * NODE * NODE, bytes_accessed=4 << 20, transcendentals=2 * blocks * cands * NODE * NODE
        ),
        name="contact",
    )(*in_hbm(slot), fetched.reshape(peers * capacity, chunks, LANES), fields, own, inner, delta)
    out = out.reshape(groups, pairs, SUB, LANES)
    return jnp.swapaxes(out, 1, 2).reshape(blocks, NODE * NVEC)


def solution(mesh):
    split_rows = P(AXES, None)
    return jax.shard_map(
        per_device,
        mesh=mesh,
        in_specs=(split_rows,) * 5 + (P(AXES, None, None),) + (split_rows,) * 2,
        out_specs=split_rows,
        check_vma=False,
    )
```

```python
import functools
import math

import jax
import jax.numpy as jnp
from jax import lax
from jax.experimental import pallas as pl
from jax.experimental.pallas import tpu as pltpu
from jax.sharding import PartitionSpec as P

NODE = 64
NVEC = 64
FIELDS = 8
HB = 2
LANES = 128
SUB = 8
AXES = ("dom", "tool")
TURN = 1.0 / (2.0 * math.pi)
REACH = math.sqrt(math.log2(math.e) / 4.0)
SHARE = math.sqrt(0.05)
FAR = -1e30
SINE = (6.283185160087854, -41.3416550310025, 81.60100404550954, -76.54978161791087, 39.53670066614222)
F32 = jnp.float32
BF16 = jnp.bfloat16
VMEM = pl.BlockSpec(memory_space=pltpu.VMEM)
SMEM = pl.BlockSpec(memory_space=pltpu.SMEM)
HBM = pl.BlockSpec(memory_space=pltpu.HBM)
STEP = 4
PARTS = 3


def params(mib):
    return pltpu.CompilerParams(vmem_limit_bytes=mib << 20)


def left_half(rows):
    return lax.broadcasted_iota(jnp.int32, (rows, LANES), 1) < NODE


def swap(x):
    return pltpu.roll(x, NODE, 1)


def split(x):
    high = x.astype(BF16)
    return high, (x - high.astype(F32)).astype(BF16)


def three(x):
    high = x.astype(BF16).astype(F32)
    rest = x - high
    mid = rest.astype(BF16).astype(F32)
    return high, mid, rest - mid


def fold(out, half):
    pairs = NODE // 2
    even, odd = out[:pairs], out[pairs:]
    return jnp.where(half, even, odd) + swap(jnp.where(half, odd, even))


def copies_of(sources, targets, sems):
    made = [pltpu.make_async_copy(a, b, sems.at[i]) for i, (a, b) in enumerate(zip(sources, targets))]
    for copy in made:
        copy.start()
    return made


def pair_fields(x, y):
    quarter = left_half(x.shape[0])
    return jnp.concatenate([jnp.where(quarter, x, swap(y)), jnp.where(quarter, swap(x), y)], axis=0)


def field_rows(shape):
    row = lax.broadcasted_iota(jnp.int32, shape, 0)
    place = (row < 2) | (row == 4)
    return row, place, (row != 7) & ~place


def ranks(hits):
    n = hits.shape[1]
    upper = (
        lax.broadcasted_iota(jnp.int32, (n, n), 0) <= lax.broadcasted_iota(jnp.int32, (n, n), 1)
    ).astype(BF16)
    return jnp.dot(hits.astype(F32).astype(BF16), upper, preferred_element_type=F32)


def prep_kernel(
    capacity, owners_hbm, seg_hbm, vec_hbm, send_ref, slot_ref, head_ref, tail_ref,
    owners_ref, seg_ref, first_ref, last_ref, sems,
):
    last = vec_hbm.shape[0] - 1
    got = copies_of(
        (owners_hbm, seg_hbm, vec_hbm.at[0], vec_hbm.at[last]), (owners_ref, seg_ref, first_ref, last_ref), sems
    )
    got[0].wait()
    got[1].wait()
    cands, blocks = owners_ref.shape
    peers = send_ref.shape[0]
    owner_ids = lax.broadcasted_iota(jnp.int32, (peers, blocks), 0)
    lanes = lax.broadcasted_iota(jnp.int32, (peers, LANES), 1)
    send = jnp.zeros((peers, LANES), jnp.int32)
    before = jnp.zeros((peers, 1), F32)
    for k in range(cands):
        target = owners_ref[k : k + 1, :]
        hits = owner_ids == jnp.broadcast_to(target, (peers, blocks))
        places = jnp.where(hits, before + ranks(hits) - 1.0, -1.0)
        before = before + jnp.sum(hits.astype(F32), axis=1, keepdims=True)
        rank = jnp.sum(jnp.maximum(places, 0.0), axis=0, keepdims=True)
        slot_ref[k : k + 1, :] = target * capacity + rank.astype(jnp.int32)
        wanted = jnp.broadcast_to(seg_ref[k : k + 1, :].astype(F32), (peers, blocks))
        for s in range(capacity):
            named = jnp.sum(jnp.where(places == float(s), wanted, 0.0), axis=1, keepdims=True)
            send = send + jnp.where(lanes == s, named.astype(jnp.int32), 0)
    send_ref[...] = send
    got[2].wait()
    got[3].wait()
    pairs = NODE // 2
    for h in range(HB):
        head_ref[h * pairs : (h + 1) * pairs, :] = first_ref[pl.ds(h, pairs, stride=SUB), :]
        tail_ref[h * pairs : (h + 1) * pairs, :] = last_ref[pl.ds(SUB - HB + h, pairs, stride=SUB), :]


def rows_kernel(capacity, want_ref, part_ref, out_ref):
    peers = want_ref.shape[0]
    segs, width = part_ref.shape[0], part_ref.shape[1] // PARTS
    chunks = width // LANES
    seg = lax.broadcasted_iota(jnp.int32, (peers, segs), 1)
    want = want_ref[...]
    picks = jnp.concatenate([(seg == want[:, s : s + 1]).astype(F32).astype(BF16) for s in range(capacity)], axis=0)
    for c in range(chunks):
        got = None
        for p in range(PARTS):
            at = p * width + c * LANES
            term = jnp.dot(picks, part_ref[:, at : at + LANES], preferred_element_type=F32)
            got = term if got is None else got + term
        for s in range(capacity):
            out_ref[pl.ds(s * chunks + c, peers, stride=capacity * chunks), :] = got[s * peers : (s + 1) * peers]


def parts_kernel(after_prep, tool_hbm, part_ref, tool_ref, sems):
    copies_of((tool_hbm,), (tool_ref,), sems)[0].wait()
    width = tool_ref.shape[1]
    for p, part in enumerate(three(tool_ref[...])):
        part_ref[:, p * width : (p + 1) * width] = part.astype(BF16)


def ordered(row, h, m, l, order):
    out = jnp.zeros(row.shape, F32)
    for value, name in ((h, "h"), (m, "m"), (l, "l")):
        for i, at in enumerate(order):
            if at == name:
                out = jnp.where(row == i, value, out)
    return out


def main_kernel(
    columns_hbm, vec_hbm, rec_hbm, act_hbm, stiff_hbm, before_ref, after_ref, out_ref, own_ref, field_ref,
    columns_ref, vec_ref, rec_ref, act_ref, stiff_ref, wide_ref, hold_ref, turn_ref, sems,
):
    nnz, groups = stiff_ref.shape[:2]
    blocks = groups * SUB
    pairs = NODE // 2
    half = left_half(pairs)
    full = left_half(NODE)
    got = copies_of(
        (columns_hbm, vec_hbm, rec_hbm, act_hbm) + tuple(stiff_hbm.at[:, g] for g in range(groups)),
        (columns_ref, vec_ref, rec_ref, act_ref) + tuple(stiff_ref.at[:, g] for g in range(groups)),
        sems,
    )

    def widen(x):
        other = swap(x)
        both = jnp.concatenate([jnp.where(half, x, other), jnp.where(half, other, x)], axis=0)
        return jnp.where(full, both, both - both.astype(BF16).astype(F32))

    def hold(spot, both):
        hold_ref[spot, pl.ds(0, pairs, stride=2), :] = both[:pairs]
        hold_ref[spot, pl.ds(1, pairs, stride=2), :] = both[pairs:]

    for h in range(HB):
        for spot, source, at in ((h, before_ref, h), (HB + h, after_ref, blocks + HB + h)):
            hold(spot, widen(source[h * pairs : (h + 1) * pairs, :]))
            wide_ref[at] = hold_ref[spot].astype(BF16)

    def spread(g):
        for j in range(SUB):
            both = widen(vec_ref[g, pl.ds(j, pairs, stride=SUB), :])
            hold(j, both)
            own_ref[g * SUB + j] = both.astype(BF16)
        for j in range(SUB):
            wide_ref[HB + g * SUB + j] = hold_ref[j].astype(BF16)

    row, place, _ = field_rows((SUB, LANES))
    scale = jnp.where(place, REACH, 1.0)

    def fields(g):
        for j in range(0, SUB, 2):
            x = rec_ref[g, pl.ds(j, FIELDS // 2, stride=SUB), :]
            y = rec_ref[g, pl.ds(j + 1, FIELDS // 2, stride=SUB), :]
            part = pair_fields(x, y) * scale
            norm = -0.5 * jnp.sum(jnp.where(place, part * part, 0.0), axis=0, keepdims=True)
            at = g * SUB + j
            flags = jnp.concatenate([act_ref[pl.ds(at, 1), :], act_ref[pl.ds(at + 1, 1), :]], axis=1)
            norm = jnp.where(flags == 0, FAR, norm)
            h, m, l = three(part)
            nh, nm, nl = three(norm)
            extra = ordered(row, nh, nm, nl, "hml")
            extra = jnp.where((row > 2) & (row < 6), 1.0, extra)
            slip = ordered(row, h[7:8], m[7:8], l[7:8], "hhmhlm")
            none = jnp.zeros((LANES - 9 * SUB, LANES), F32)
            stack = jnp.concatenate([slip, swap(slip), h, h, m, h, l, m, extra, none], axis=0)
            turn_ref[j // 2] = stack.T
        for j in range(SUB):
            for q in range(2):
                field_ref[g * SUB + j, q * pairs : (q + 1) * pairs, :] = turn_ref[
                    j // 2, pl.ds((j % 2) * NODE + q, pairs, stride=2), :
                ].astype(BF16)

    def product(g):
        for j in range(SUB):
            b = g * SUB + j
            rows = [stiff_ref[e, g, pl.ds(j, pairs, stride=SUB), :] for e in range(nnz)]
            cols = [wide_ref[columns_ref[e, b]] for e in range(nnz)]
            even_count = nnz // 2 * 2
            left = []
            for e in range(0, even_count, 2):
                x, y = rows[e], rows[e + 1]
                left.append(jnp.concatenate([jnp.where(half, x, swap(y)), jnp.where(half, swap(x), y)], axis=0))
            high, low = split(jnp.concatenate(left, axis=1))
            out = jnp.dot(
                jnp.concatenate([high, low], axis=0),
                jnp.concatenate(cols[:even_count], axis=0),
                preferred_element_type=F32,
            )
            out = out[:NODE] + out[NODE:]
            if nnz % 2:
                out = out + jnp.dot(
                    widen(rows[-1]).astype(BF16),
                    jnp.concatenate([cols[-1], cols[-1]], axis=0),
                    preferred_element_type=F32,
                )
            out_ref[g, pl.ds(j, pairs, stride=SUB), :] = fold(out, half)

    got[1].wait()
    spread(0)
    spread(1)
    got[0].wait()
    got[2].wait()
    got[3].wait()

    def body(g, carry):
        pltpu.make_async_copy(stiff_hbm.at[:, g], stiff_ref.at[:, g], sems.at[4 + g]).wait()
        product(g)
        spread(jnp.minimum(g + 2, groups - 1))
        fields(g)
        return carry

    lax.fori_loop(0, groups, body, 0)


def contact_kernel(
    slot_hbm, rows_ref, field_ref, own_ref, inner_ref, out_ref,
    slot_ref, raw_ref, slide_ref, high_ref, low_ref, gram_ref, sems,
):
    got = copies_of((slot_hbm,), (slot_ref,), sems)
    blocks = slot_ref.shape[1]
    groups = blocks // SUB
    steps = blocks // STEP
    per = SUB // STEP
    pairs = NODE // 2
    half = left_half(pairs)
    full = left_half(NODE)
    row, place, angle = field_rows((SUB, LANES))
    scale = jnp.where(place, REACH, jnp.where(row == 3, TURN, jnp.where(angle, 3.0 * TURN, 1.0)))
    none = jnp.zeros((SUB, LANES), F32)
    idle = jnp.zeros((NODE, LANES), BF16)

    def sums(t):
        slips = []
        for j in range(STEP):
            b = t * STEP + j
            tool = pair_fields(rows_ref[slot_ref[0, b]], rows_ref[slot_ref[1, b]]) * scale
            norm = -0.5 * jnp.sum(jnp.where(place, tool * tool, 0.0), axis=0, keepdims=True)
            h, m, l = three(tool)
            extra = jnp.where(row < 3, 1.0, 0.0) + ordered(row, *three(norm), "---hml")
            right = []
            for mask, more in ((place, extra), (angle, none)):
                hm, mm, lm = (jnp.where(mask, v, 0.0) for v in (h, m, l))
                right.append(jnp.concatenate([none, none, hm, mm, hm, lm, hm, mm, more, none], axis=0).astype(BF16))
            right = jnp.concatenate(right, axis=1)
            raw_ref[j] = jnp.dot(field_ref[b][:, : right.shape[0]], right, preferred_element_type=F32)
            slips.append(ordered(row, h[7:8], m[7:8], l[7:8], "hmhlhm"))
            if j % 2:
                right = jnp.concatenate(
                    [jnp.concatenate([slips[j - 1], none], axis=1), jnp.concatenate([none, slips[j]], axis=1)], axis=0
                ).astype(BF16)
                slide_ref[j // 2] = jnp.dot(field_ref[b - 1][:, : 2 * SUB], right, preferred_element_type=F32)

    def tiles(t):
        for j in range(STEP):
            phase = raw_ref[j, :, LANES:]
            turn = 0.25 - jnp.abs(phase - jnp.round(phase))
            square = turn * turn
            wave = SINE[4]
            for c in SINE[3::-1]:
                wave = wave * square + c
            at = j % 2 * LANES
            sliding = SHARE + (0.5 * SHARE) * jnp.tanh(slide_ref[j // 2, :, at : at + LANES])
            tile = jnp.exp2(raw_ref[j, :, :LANES]) * (wave * turn) * sliding
            high_ref[j], low_ref[j] = split(tile)

    def grams(t):
        for j in range(STEP):
            high, low = high_ref[j], low_ref[j]
            left = jnp.concatenate([high, low], axis=1)
            right = jnp.concatenate(
                [jnp.concatenate([low, high], axis=1), jnp.concatenate([high, idle], axis=1)], axis=0
            )
            gram = lax.dot_general(left, right, (((1,), (1,)), ((), ())), preferred_element_type=F32)
            gram = gram + swap(gram)
            gram_ref[j] = jnp.where(full, gram, gram - gram.astype(BF16).astype(F32)).astype(BF16)

    def apply(t):
        for j in range(STEP):
            own = own_ref[t * STEP + j]
            out = jnp.dot(gram_ref[j], jnp.concatenate([own, own], axis=0), preferred_element_type=F32)
            spot = pl.ds(t % per * STEP + j, pairs, stride=SUB)
            out_ref[t // per, spot, :] = inner_ref[t // per, spot, :] + fold(out, half)

    got[0].wait()
    stages = (apply, grams, tiles, sums)
    depth = len(stages) - 1
    for t in range(depth):
        for k in range(depth - t, depth + 1):
            stages[k](t - depth + k)

    def body(t, carry):
        for k in range(depth + 1):
            stages[k](t - depth + k)
        return carry

    lax.fori_loop(depth, steps, body, 0)
    for t in range(steps, steps + depth):
        for k in range(depth + 1):
            if t - depth + k < steps:
                stages[k](t - depth + k)


def per_device(records, tool_data, owners, local_seg, active, stiffness, columns, vectors):
    peers = lax.axis_size(AXES)
    blocks, cands = owners.shape
    nnz = columns.shape[1]
    segs, width = tool_data.shape
    capacity = max(2, (3 * blocks * cands + 2 * peers - 1) // (2 * peers))
    groups = blocks // SUB
    pairs = NODE // 2
    chunks = width // LANES
    i32 = jnp.int32

    def shape(dims, dtype=F32):
        return jax.ShapeDtypeStruct(dims, dtype)

    def tiles_of(x, rows):
        lead = x.shape[:-2]
        n = len(lead)
        x = x.reshape(lead + (rows // SUB, SUB, x.shape[-1] // LANES, LANES))
        x = jnp.swapaxes(x, n + 1, n + 2)
        return x.reshape(lead + (rows // SUB, -1, LANES))

    vec = tiles_of(vectors, blocks)
    rec = tiles_of(records, blocks)
    stiff = tiles_of(jnp.swapaxes(stiffness, 0, 1), blocks)
    edge = shape((HB * pairs, LANES))

    def in_hbm(*arrays):
        return [pltpu.with_memory_space_constraint(x, pltpu.HBM) for x in arrays]

    send, slot, head, tail = pl.pallas_call(
        functools.partial(prep_kernel, capacity),
        out_shape=(shape((peers, LANES), i32), shape((cands, blocks), i32), edge, edge),
        in_specs=[HBM] * 3,
        out_specs=(VMEM,) * 4,
        scratch_shapes=[
            pltpu.VMEM((cands, blocks), i32),
            pltpu.VMEM((cands, blocks), i32),
            pltpu.VMEM(vec.shape[1:], F32),
            pltpu.VMEM(vec.shape[1:], F32),
            pltpu.SemaphoreType.DMA((4,)),
        ],
        compiler_params=params(8),
        name="prep",
    )(*in_hbm(owners.T, local_seg.T, vec))

    wanted = lax.all_to_all(send.reshape(peers, 1, LANES), AXES, split_axis=0, concat_axis=0, tiled=True)

    up = [(i, i + 1) for i in range(peers - 1)]
    down = [(j, i) for i, j in up]
    before = lax.ppermute(tail, AXES, up)
    after = lax.ppermute(head, AXES, down)

    parts = pl.pallas_call(
        parts_kernel,
        out_shape=shape((segs, PARTS * width), BF16),
        in_specs=[HBM] * 2,
        out_specs=VMEM,
        scratch_shapes=[pltpu.VMEM(tool_data.shape, F32), pltpu.SemaphoreType.DMA((1,))],
        compiler_params=params(8),
        cost_estimate=pl.CostEstimate(flops=1 << 20, bytes_accessed=4 << 20, transcendentals=0),
        name="parts",
    )(*in_hbm(slot, tool_data))

    rows_out = pl.pallas_call(
        functools.partial(rows_kernel, capacity),
        out_shape=shape((peers * capacity * chunks, LANES)),
        in_specs=[VMEM] * 2,
        out_specs=VMEM,
        compiler_params=params(8),
        name="rows",
    )(wanted.reshape(peers, LANES), parts)
    fetched = lax.all_to_all(
        rows_out.reshape(peers, capacity * chunks, LANES), AXES, split_axis=0, concat_axis=0, tiled=True
    )

    inner, own, fields = pl.pallas_call(
        main_kernel,
        out_shape=(
            shape(vec.shape),
            shape((blocks, NODE, LANES), BF16),
            shape((blocks, NODE, LANES), BF16),
        ),
        in_specs=[HBM] * 5 + [VMEM] * 2,
        out_specs=(VMEM,) * 3,
        scratch_shapes=[
            pltpu.SMEM((nnz, blocks), i32),
            pltpu.VMEM(vec.shape, F32),
            pltpu.VMEM(rec.shape, F32),
            pltpu.VMEM(active.shape, i32),
            pltpu.VMEM(stiff.shape, F32),
            pltpu.VMEM((blocks + 2 * HB, NODE, LANES), BF16),
            pltpu.VMEM((SUB, NODE, LANES), F32),
            pltpu.VMEM((SUB // 2, LANES, LANES), F32),
            pltpu.SemaphoreType.DMA((groups + 4,)),
        ],
        compiler_params=params(20),
        cost_estimate=pl.CostEstimate(
            flops=6 * blocks * nnz * NODE * NODE * NVEC, bytes_accessed=24 << 20, transcendentals=0
        ),
        name="main",
    )(*in_hbm(columns.T, vec, rec, active, stiff), before, after)

    out = pl.pallas_call(
        contact_kernel,
        out_shape=shape(vec.shape),
        in_specs=[HBM] + [VMEM] * 4,
        out_specs=VMEM,
        scratch_shapes=[
            pltpu.SMEM((cands, blocks), i32),
            pltpu.VMEM((STEP, NODE, 2 * LANES), F32),
            pltpu.VMEM((STEP // 2, NODE, 2 * LANES), F32),
            pltpu.VMEM((STEP, NODE, LANES), BF16),
            pltpu.VMEM((STEP, NODE, LANES), BF16),
            pltpu.VMEM((STEP, NODE, LANES), BF16),
            pltpu.SemaphoreType.DMA((1,)),
        ],
        compiler_params=params(16),
        cost_estimate=pl.CostEstimate(
            flops=80 * blocks * cands * NODE * NODE, bytes_accessed=4 << 20, transcendentals=2 * blocks * cands * NODE * NODE
        ),
        name="contact",
    )(*in_hbm(slot), fetched.reshape(peers * capacity, chunks, LANES), fields, own, inner)
    out = out.reshape(groups, pairs, SUB, LANES)
    return jnp.swapaxes(out, 1, 2).reshape(blocks, NODE * NVEC)


def solution(mesh):
    split_rows = P(AXES, None)
    return jax.shard_map(
        per_device,
        mesh=mesh,
        in_specs=(split_rows,) * 5 + (P(AXES, None, None),) + (split_rows,) * 2,
        out_specs=split_rows,
        check_vma=False,
    )
```

```python
import functools
import math

import jax
import jax.numpy as jnp
from jax import lax
from jax.experimental import pallas as pl
from jax.experimental.pallas import tpu as pltpu
from jax.sharding import PartitionSpec as P

NODE = 64
NVEC = 64
FIELDS = 8
HB = 2
LANES = 128
SUB = 8
AXES = ("dom", "tool")
TURN = 1.0 / (2.0 * math.pi)
REACH = math.sqrt(math.log2(math.e) / 4.0)
SHARE = math.sqrt(0.05)
FAR = -1e30
SINE = (6.283185160087854, -41.3416550310025, 81.60100404550954, -76.54978161791087, 39.53670066614222)
F32 = jnp.float32
BF16 = jnp.bfloat16
VMEM = pl.BlockSpec(memory_space=pltpu.VMEM)
SMEM = pl.BlockSpec(memory_space=pltpu.SMEM)
HBM = pl.BlockSpec(memory_space=pltpu.HBM)
ROUND = 1.5 * 2.0**23
PARTS = 3


def params(mib):
    return pltpu.CompilerParams(vmem_limit_bytes=mib << 20)


def left_half(rows):
    return lax.broadcasted_iota(jnp.int32, (rows, LANES), 1) < NODE


def swap(x):
    return pltpu.roll(x, NODE, 1)


def split(x):
    high = x.astype(BF16)
    return high, (x - high.astype(F32)).astype(BF16)


def three(x):
    high = x.astype(BF16).astype(F32)
    rest = x - high
    mid = rest.astype(BF16).astype(F32)
    return high, mid, rest - mid


def fold(out, half):
    pairs = NODE // 2
    even, odd = out[:pairs], out[pairs:]
    return jnp.where(half, even, odd) + swap(jnp.where(half, odd, even))


def flip(tiles):
    tiles = list(tiles)
    row = lax.broadcasted_iota(jnp.int32, (SUB, LANES), 0)
    for d in (4, 2, 1):
        keep = (row & d) == 0
        for i in range(SUB):
            if i & d:
                continue
            a, b = tiles[i], tiles[i + d]
            if 2 * d == SUB:
                moved = pltpu.roll(jnp.where(keep, b, a), d, 0)
                tiles[i], tiles[i + d] = jnp.where(keep, a, moved), jnp.where(keep, moved, b)
            else:
                tiles[i] = jnp.where(keep, a, pltpu.roll(b, d, 0))
                tiles[i + d] = jnp.where(keep, pltpu.roll(a, SUB - d, 0), b)
    return tiles


def flip_all(tiles):
    runs = [flip(tiles[i : i + SUB]) for i in range(0, len(tiles), SUB)]
    return [jnp.concatenate([run[j] for run in runs], axis=0) for j in range(SUB)]


def tiles_from(blocks):
    out = []
    for at in range(0, blocks[0].shape[0], SUB):
        out += flip([x[at : at + SUB] for x in blocks])
    return out


def doubled(x, half):
    other = swap(x)
    return jnp.where(half, x, other), jnp.where(half, other, x)


def high_low(x, half):
    return jnp.where(half, x, x - x.astype(BF16).astype(F32))


def copies_of(sources, targets, sems):
    made = [pltpu.make_async_copy(a, b, sems.at[i]) for i, (a, b) in enumerate(zip(sources, targets))]
    for copy in made:
        copy.start()
    return made


def pair_fields(x, y):
    quarter = left_half(x.shape[0])
    return jnp.concatenate([jnp.where(quarter, x, swap(y)), jnp.where(quarter, swap(x), y)], axis=0)


def field_rows(shape):
    row = lax.broadcasted_iota(jnp.int32, shape, 0)
    place = (row < 2) | (row == 4)
    return row, place, (row != 7) & ~place


def ranks(hits):
    n = hits.shape[1]
    upper = (
        lax.broadcasted_iota(jnp.int32, (n, n), 0) <= lax.broadcasted_iota(jnp.int32, (n, n), 1)
    ).astype(BF16)
    return jnp.dot(hits.astype(F32).astype(BF16), upper, preferred_element_type=F32)


def prep_kernel(
    peers, capacity, stride, owners_hbm, seg_hbm, vec_hbm, send_ref, slot_hbm,
    owners_ref, seg_ref, first_ref, last_ref, edge_ref, slot_ref, sems,
):
    last = vec_hbm.shape[0] - 1
    got = copies_of(
        (owners_hbm, seg_hbm, vec_hbm.at[0], vec_hbm.at[last]), (owners_ref, seg_ref, first_ref, last_ref), sems
    )
    got[0].wait()
    got[1].wait()
    cands, blocks = owners_ref.shape
    pairs = NODE // 2
    share = 2 * HB * pairs // peers
    owner_ids = lax.broadcasted_iota(jnp.int32, (peers, blocks), 0)
    lanes = lax.broadcasted_iota(jnp.int32, (peers, LANES), 1)
    send = jnp.zeros((peers, LANES), F32)
    before = jnp.zeros((peers, 1), F32)
    for k in range(cands):
        target = owners_ref[k : k + 1, :]
        hits = owner_ids == jnp.broadcast_to(target, (peers, blocks))
        places = jnp.where(hits, before + ranks(hits) - 1.0, -1.0)
        before = before + jnp.sum(hits.astype(F32), axis=1, keepdims=True)
        rank = jnp.sum(jnp.maximum(places, 0.0), axis=0, keepdims=True)
        slot_ref[k : k + 1, :] = target * stride + rank.astype(jnp.int32)
        wanted = jnp.broadcast_to(seg_ref[k : k + 1, :].astype(F32), (peers, blocks))
        for s in range(capacity):
            named = jnp.sum(jnp.where(places == float(s), wanted, 0.0), axis=1, keepdims=True)
            send = send + jnp.where(lanes == s, named, 0.0)
    slots = pltpu.make_async_copy(slot_ref, slot_hbm, sems.at[4])
    slots.start()
    send_ref[pl.ds(0, peers, stride=1 + share), :] = send
    got[2].wait()
    got[3].wait()
    for h in range(HB):
        edge_ref[h * pairs : (h + 1) * pairs, :] = first_ref[pl.ds(h, pairs, stride=SUB), :]
        edge_ref[(HB + h) * pairs : (HB + h + 1) * pairs, :] = last_ref[pl.ds(SUB - HB + h, pairs, stride=SUB), :]
    for r in range(share):
        send_ref[pl.ds(1 + r, peers, stride=1 + share), :] = edge_ref[pl.ds(r, peers, stride=share), :]
    slots.wait()


def rows_kernel(peers, capacity, stride, got_ref, part_ref, out_ref):
    segs, width = part_ref.shape[0], part_ref.shape[1] // PARTS
    chunks = width // LANES
    share = got_ref.shape[0] // peers - 1
    seg = lax.broadcasted_iota(jnp.int32, (peers, segs), 1)
    want = got_ref[pl.ds(0, peers, stride=1 + share), :].astype(jnp.int32)
    picks = jnp.concatenate([(seg == want[:, s : s + 1]).astype(F32).astype(BF16) for s in range(capacity)], axis=0)
    for c in range(chunks):
        got = None
        for p in range(PARTS):
            at = p * width + c * LANES
            term = jnp.dot(picks, part_ref[:, at : at + LANES], preferred_element_type=F32)
            got = term if got is None else got + term
        for s in range(capacity):
            out_ref[pl.ds(s * chunks + c, peers, stride=stride * chunks), :] = got[s * peers : (s + 1) * peers]
    me = lax.axis_index(AXES[0]) * lax.axis_size(AXES[1]) + lax.axis_index(AXES[1])
    peer = lax.broadcasted_iota(jnp.int32, (peers, LANES), 0)
    for r in range(share):
        edge = got_ref[pl.ds(1 + r, peers, stride=1 + share), :]
        following = jnp.where(peer == peers - 1, 0.0, pltpu.roll(edge, peers - 1, 0))
        previous = jnp.where(peer == 0, 0.0, pltpu.roll(edge, 1, 0))
        out_ref[pl.ds(capacity * chunks + r, peers, stride=stride * chunks), :] = jnp.where(
            me < peers // 2, following, previous
        )


def parts_kernel(after_prep, tool_hbm, part_ref, tool_ref, sems):
    copies_of((tool_hbm,), (tool_ref,), sems)[0].wait()
    width = tool_ref.shape[1]
    for p, part in enumerate(three(tool_ref[...])):
        part_ref[:, p * width : (p + 1) * width] = part.astype(BF16)


def ordered(row, h, m, l, order):
    out = jnp.zeros(row.shape, F32)
    for value, name in ((h, "h"), (m, "m"), (l, "l")):
        for i, at in enumerate(order):
            if at == name:
                out = jnp.where(row == i, value, out)
    return out


def main_kernel(
    columns_hbm, vec_hbm, rec_hbm, act_hbm, stiff_hbm, out_ref, own_ref, field_ref, edge_ref, rest_ref,
    columns_ref, vec_ref, rec_ref, act_ref, stiff_ref, wide_ref, left_ref, last_ref, sems,
):
    nnz, groups = stiff_ref.shape[:2]
    blocks = groups * SUB
    pairs = NODE // 2
    even_count = nnz // 2 * 2
    half = left_half(SUB)
    half_rows = left_half(pairs)
    got = copies_of(
        (columns_hbm, vec_hbm, rec_hbm, act_hbm) + tuple(stiff_hbm.at[:, g] for g in range(groups)),
        (columns_ref, vec_ref, rec_ref, act_ref) + tuple(stiff_ref.at[:, g] for g in range(groups)),
        sems,
    )
    zero = jnp.zeros((NODE, LANES), BF16)
    for h in range(HB):
        wide_ref[h] = zero
        wide_ref[blocks + HB + h] = zero

    def tile(m):
        return pl.ds(m * SUB, SUB)

    def spread(g):
        for at in range(0, pairs, 2 * SUB):
            evens, odds = [], []
            for m in range(at, at + 2 * SUB):
                even, odd = doubled(vec_ref[g, tile(m), :], half)
                evens.append(high_low(even, half))
                odds.append(high_low(odd, half))
            for q, values in enumerate((evens, odds)):
                for j, x in enumerate(flip_all(values)):
                    own_ref[g * SUB + j, q * pairs + at : q * pairs + at + 2 * SUB, :] = x.astype(BF16)
            mixed = [x for both in zip(evens, odds) for x in both]
            for j, x in enumerate(flip_all(mixed)):
                wide_ref[HB + g * SUB + j, 2 * at : 2 * at + 4 * SUB, :] = x.astype(BF16)

    row, place, _ = field_rows((SUB, LANES))
    scale = jnp.where(place, REACH, 1.0)
    lane = lax.broadcasted_iota(jnp.int32, (SUB, LANES), 1)
    turn = lane // NODE * NODE + lane % pairs * 2 + lane % NODE // pairs

    def evens_first(x):
        return jnp.take_along_axis(x, turn, axis=1, mode="promise_in_bounds")

    def fields(g):
        for j in range(0, SUB, 2):
            x = rec_ref[g, pl.ds(j, FIELDS // 2, stride=SUB), :]
            y = rec_ref[g, pl.ds(j + 1, FIELDS // 2, stride=SUB), :]
            part = pair_fields(x, y) * scale
            norm = -0.5 * jnp.sum(jnp.where(place, part * part, 0.0), axis=0, keepdims=True)
            at = g * SUB + j
            flags = jnp.concatenate([act_ref[pl.ds(at, 1), :], act_ref[pl.ds(at + 1, 1), :]], axis=1)
            norm = jnp.where(flags == 0, FAR, norm)
            h, m, l = three(evens_first(part))
            extra = ordered(row, *three(evens_first(jnp.broadcast_to(norm, (SUB, LANES)))), "hml")
            extra = jnp.where((row > 2) & (row < 6), 1.0, extra)
            slip = ordered(row, h[7:8], m[7:8], l[7:8], "hhmhlm")
            none = jnp.zeros((LANES - 9 * SUB, LANES), F32)
            stack = jnp.concatenate([slip, swap(slip), h, h, m, h, l, m, extra, none], axis=0).T.astype(BF16)
            field_ref[at] = stack[:NODE]
            field_ref[at + 1] = stack[NODE:]

    def prepare(g):
        for at in range(0, pairs, 2 * SUB):
            for e in range(0, nnz, 2):
                evens, odds = [], []
                for m in range(at, at + 2 * SUB):
                    x = stiff_ref[e, g, tile(m), :]
                    if e < even_count:
                        y = stiff_ref[e + 1, g, tile(m), :]
                        evens.append(jnp.where(half, x, swap(y)))
                        odds.append(jnp.where(half, swap(x), y))
                    else:
                        even, odd = doubled(x, half)
                        evens.append(high_low(even, half))
                        odds.append(high_low(odd, half))
                for q, values in enumerate((evens, odds)):
                    rows = slice(q * pairs + at, q * pairs + at + 2 * SUB)
                    for j, x in enumerate(flip_all(values)):
                        if e < even_count:
                            high, low = split(x)
                            cols = slice(e * NODE, (e + 2) * NODE)
                            left_ref[j, rows, cols] = high
                            left_ref[j, NODE + rows.start : NODE + rows.stop, cols] = low
                        else:
                            last_ref[j, rows, :] = x.astype(BF16)

    def product(g):
        folded = []
        for j in range(SUB):
            cols = [wide_ref[columns_ref[e, g * SUB + j]] for e in range(nnz)]
            folded.append(fold(times(left_ref[j], last_ref[j], cols), half_rows))
        for m, x in enumerate(tiles_from(folded)):
            out_ref[g, m * SUB : (m + 1) * SUB, :] = x

    got[1].wait()
    spread(0)
    spread(1)
    got[4].wait()
    prepare(0)
    for h in range(HB):
        edge_ref[h] = left_ref[h]
        rest_ref[h] = last_ref[h]
    got[0].wait()
    got[2].wait()
    got[3].wait()

    def body(g, carry):
        pltpu.make_async_copy(stiff_hbm.at[:, g + 1], stiff_ref.at[:, g + 1], sems.at[5 + g]).wait()
        product(g)
        prepare(g + 1)
        spread(jnp.minimum(g + 2, groups - 1))
        fields(g)
        return carry

    lax.fori_loop(0, groups - 1, body, 0)
    product(groups - 1)
    fields(groups - 1)
    for h in range(HB):
        edge_ref[HB + h] = left_ref[SUB - HB + h]
        rest_ref[HB + h] = last_ref[SUB - HB + h]


def times(left, last, cols):
    even_count = left.shape[1] // NODE
    out = jnp.dot(left, jnp.concatenate(cols[:even_count], axis=0), preferred_element_type=F32)
    out = out[:NODE] + out[NODE:]
    if len(cols) > even_count:
        out = out + jnp.dot(last, jnp.concatenate([cols[-1], cols[-1]], axis=0), preferred_element_type=F32)
    return out


def contact_kernel(
    capacity, stride, peers, slot_hbm, columns_hbm, rows_ref, field_ref, own_ref, inner_ref, edge_ref, rest_ref, out_ref,
    slot_ref, columns_ref, high_ref, low_ref, gram_ref, halo_ref, wide_ref, hold_ref, sems,
):
    got = copies_of((slot_hbm, columns_hbm), (slot_ref, columns_ref), sems)
    nnz, blocks = columns_ref.shape
    groups = blocks // SUB
    pairs = NODE // 2
    half = left_half(pairs)
    full = left_half(NODE)
    row, place, angle = field_rows((SUB, LANES))
    scale = jnp.where(place, REACH, jnp.where(row == 3, TURN, jnp.where(angle, 3.0 * TURN, 1.0)))
    none = jnp.zeros((SUB, LANES), F32)
    idle = jnp.zeros((NODE, LANES), BF16)

    def tile_of(reach, phase, slip):
        turn = 0.25 - jnp.abs(phase - ((phase + ROUND) - ROUND))
        square = turn * turn
        wave = SINE[4]
        for c in SINE[3::-1]:
            wave = wave * square + c
        return jnp.exp2(reach) * (wave * turn) * (SHARE + (0.5 * SHARE) * jnp.tanh(slip))

    def tiles(g):
        raws, slips = [], []
        for j in range(SUB):
            b = g * SUB + j
            tool = pair_fields(rows_ref[slot_ref[0, b]], rows_ref[slot_ref[1, b]]) * scale
            norm = -0.5 * jnp.sum(jnp.where(place, tool * tool, 0.0), axis=0, keepdims=True)
            h, m, l = three(tool)
            extra = jnp.where(row < 3, 1.0, 0.0) + ordered(row, *three(norm), "---hml")
            right = []
            for mask, more in ((place, extra), (angle, none)):
                hm, mm, lm = (jnp.where(mask, v, 0.0) for v in (h, m, l))
                right.append(jnp.concatenate([none, none, hm, mm, hm, lm, hm, mm, more, none], axis=0).astype(BF16))
            right = jnp.concatenate(right, axis=1)
            raws.append(jnp.dot(field_ref[b][:, : right.shape[0]], right, preferred_element_type=F32))
            slips.append(ordered(row, h[7:8], m[7:8], l[7:8], "hmhlhm"))
            if j % 2:
                right = jnp.concatenate(
                    [jnp.concatenate([slips[j - 1], none], axis=1), jnp.concatenate([none, slips[j]], axis=1)], axis=0
                ).astype(BF16)
                slide = jnp.dot(field_ref[b - 1][:, : 2 * SUB], right, preferred_element_type=F32)
                for i in range(2):
                    raw = raws[j - 1 + i]
                    high_ref[j - 1 + i], low_ref[j - 1 + i] = split(
                        tile_of(raw[:, :LANES], raw[:, LANES:], slide[:, i * LANES : (i + 1) * LANES])
                    )

    def grams(g):
        for j in range(SUB):
            high, low = high_ref[j], low_ref[j]
            left = jnp.concatenate([high, low], axis=1)
            right = jnp.concatenate(
                [jnp.concatenate([low, high], axis=1), jnp.concatenate([high, idle], axis=1)], axis=0
            )
            gram = lax.dot_general(left, right, (((1,), (1,)), ((), ())), preferred_element_type=F32)
            gram_ref[j] = high_low(gram + swap(gram), full).astype(BF16)

    def apply(g):
        folded = []
        for j in range(SUB):
            own = own_ref[g * SUB + j]
            out = jnp.dot(gram_ref[j], jnp.concatenate([own, own], axis=0), preferred_element_type=F32)
            folded.append(fold(out, half))
        for m, x in enumerate(tiles_from(folded)):
            spot = slice(m * SUB, (m + 1) * SUB)
            out_ref[g, spot, :] = inner_ref[g, spot, :] + x

    def halo():
        share = 2 * HB * pairs // peers
        step = min(share, rows_ref.shape[1])
        for at in range(0, 2 * HB * pairs, step):
            p, r = at // share, at % share
            halo_ref[at : at + step, :] = rows_ref[p * stride + capacity + r // step][:step]
        for h in range(2 * HB):
            even, odd = doubled(halo_ref[h * pairs : (h + 1) * pairs, :], half)
            hold_ref[h, pl.ds(0, pairs, stride=2), :] = even
            hold_ref[h, pl.ds(1, pairs, stride=2), :] = odd
            wide_ref[h] = high_low(hold_ref[h], full).astype(BF16)
        wide_ref[2 * HB] = idle
        deltas = []
        for i in range(2 * HB):
            b = i if i < HB else blocks - 2 * HB + i
            cols = []
            for e in range(nnz):
                c = columns_ref[e, b]
                ahead, behind = c - blocks - HB, c + HB
                cols.append(wide_ref[jnp.where(c < HB, behind, jnp.where(ahead >= 0, ahead, 2 * HB))])
            deltas.append(fold(times(edge_ref[i], rest_ref[i], cols), half))
        return deltas

    for copy in got:
        copy.wait()
    tiles(0)
    grams(0)
    tiles(1)

    def body(g, carry):
        apply(g - 2)
        grams(g - 1)
        tiles(g)
        return carry

    lax.fori_loop(2, groups, body, 0)
    deltas = halo()
    apply(groups - 2)
    grams(groups - 1)
    apply(groups - 1)
    for i, delta in enumerate(deltas):
        g, j = (0, i) if i < HB else (groups - 1, SUB - 2 * HB + i)
        spot = pl.ds(j, pairs, stride=SUB)
        out_ref[g, spot, :] = out_ref[g, spot, :] + delta


def per_device(records, tool_data, owners, local_seg, active, stiffness, columns, vectors):
    peers = lax.axis_size(AXES)
    blocks, cands = owners.shape
    nnz = columns.shape[1]
    segs, width = tool_data.shape
    capacity = max(2, (3 * blocks * cands + 2 * peers - 1) // (2 * peers))
    groups = blocks // SUB
    pairs = NODE // 2
    chunks = width // LANES
    i32 = jnp.int32

    def shape(dims, dtype=F32):
        return jax.ShapeDtypeStruct(dims, dtype)

    def tiles_of(x, rows):
        lead = x.shape[:-2]
        n = len(lead)
        x = x.reshape(lead + (rows // SUB, SUB, x.shape[-1] // LANES, LANES))
        x = jnp.swapaxes(x, n + 1, n + 2)
        return x.reshape(lead + (rows // SUB, -1, LANES))

    vec = tiles_of(vectors, blocks)
    rec = tiles_of(records, blocks)
    stiff = tiles_of(jnp.swapaxes(stiffness, 0, 1), blocks)
    share = 2 * HB * pairs // peers
    stride = capacity + -(-share // chunks)

    def in_hbm(*arrays):
        return [pltpu.with_memory_space_constraint(x, pltpu.HBM) for x in arrays]

    send, slot = pl.pallas_call(
        functools.partial(prep_kernel, peers, capacity, stride),
        out_shape=(shape((peers * (1 + share), LANES)), pltpu.HBM((cands, blocks), i32)),
        in_specs=[HBM] * 3,
        out_specs=(VMEM, HBM),
        scratch_shapes=[
            pltpu.VMEM((cands, blocks), i32),
            pltpu.VMEM((cands, blocks), i32),
            pltpu.VMEM(vec.shape[1:], F32),
            pltpu.VMEM(vec.shape[1:], F32),
            pltpu.VMEM((2 * HB * pairs, LANES), F32),
            pltpu.VMEM((cands, blocks), i32),
            pltpu.SemaphoreType.DMA((5,)),
        ],
        compiler_params=params(8),
        name="prep",
    )(*in_hbm(owners.T, local_seg.T, vec))

    wanted = lax.all_to_all(send.reshape(peers, 1 + share, 1, LANES), AXES, split_axis=0, concat_axis=0, tiled=True)

    parts = pl.pallas_call(
        parts_kernel,
        out_shape=shape((segs, PARTS * width), BF16),
        in_specs=[HBM] * 2,
        out_specs=VMEM,
        scratch_shapes=[pltpu.VMEM(tool_data.shape, F32), pltpu.SemaphoreType.DMA((1,))],
        compiler_params=params(8),
        cost_estimate=pl.CostEstimate(flops=1 << 20, bytes_accessed=4 << 20, transcendentals=0),
        name="parts",
    )(*in_hbm(slot, tool_data))

    rows_out = pl.pallas_call(
        functools.partial(rows_kernel, peers, capacity, stride),
        out_shape=shape((peers * stride * chunks, LANES)),
        in_specs=[VMEM] * 2,
        out_specs=VMEM,
        compiler_params=params(8),
        name="rows",
    )(wanted.reshape(peers * (1 + share), LANES), parts)
    fetched = lax.all_to_all(
        rows_out.reshape(peers, stride, chunks, LANES), AXES, split_axis=0, concat_axis=0, tiled=True
    )

    wide = (blocks, NODE, LANES)
    left = (2 * NODE, nnz // 2 * 2 * NODE)
    inner, own, fields, edges, rests = pl.pallas_call(
        main_kernel,
        out_shape=(
            shape(vec.shape),
            shape(wide, BF16),
            shape(wide, BF16),
            shape((2 * HB,) + left, BF16),
            shape((2 * HB, NODE, LANES), BF16),
        ),
        in_specs=[HBM] * 5,
        out_specs=(VMEM,) * 5,
        scratch_shapes=[
            pltpu.SMEM((nnz, blocks), i32),
            pltpu.VMEM(vec.shape, F32),
            pltpu.VMEM(rec.shape, F32),
            pltpu.VMEM(active.shape, i32),
            pltpu.VMEM(stiff.shape, F32),
            pltpu.VMEM((blocks + 2 * HB, NODE, LANES), BF16),
            pltpu.VMEM((SUB,) + left, BF16),
            pltpu.VMEM((SUB, NODE, LANES), BF16),
            pltpu.SemaphoreType.DMA((groups + 4,)),
        ],
        compiler_params=params(20),
        cost_estimate=pl.CostEstimate(
            flops=6 * blocks * nnz * NODE * NODE * NVEC, bytes_accessed=24 << 20, transcendentals=0
        ),
        name="main",
    )(*in_hbm(columns.T, vec, rec, active, stiff))

    out = pl.pallas_call(
        functools.partial(contact_kernel, capacity, stride, peers),
        out_shape=shape(vec.shape),
        in_specs=[HBM] * 2 + [VMEM] * 6,
        out_specs=VMEM,
        scratch_shapes=[
            pltpu.SMEM((cands, blocks), i32),
            pltpu.SMEM((nnz, blocks), i32),
            pltpu.VMEM((SUB, NODE, LANES), BF16),
            pltpu.VMEM((SUB, NODE, LANES), BF16),
            pltpu.VMEM((SUB, NODE, LANES), BF16),
            pltpu.VMEM((2 * HB * pairs, LANES), F32),
            pltpu.VMEM((2 * HB + 1, NODE, LANES), BF16),
            pltpu.VMEM((2 * HB, NODE, LANES), F32),
            pltpu.SemaphoreType.DMA((2,)),
        ],
        compiler_params=params(16),
        cost_estimate=pl.CostEstimate(
            flops=80 * blocks * cands * NODE * NODE, bytes_accessed=4 << 20, transcendentals=2 * blocks * cands * NODE * NODE
        ),
        name="contact",
    )(*in_hbm(slot, columns.T), fetched.reshape(peers * stride, chunks, LANES), fields, own, inner, edges, rests)
    out = out.reshape(groups, pairs, SUB, LANES)
    return jnp.swapaxes(out, 1, 2).reshape(blocks, NODE * NVEC)


def solution(mesh):
    split_rows = P(AXES, None)
    return jax.shard_map(
        per_device,
        mesh=mesh,
        in_specs=(split_rows,) * 5 + (P(AXES, None, None),) + (split_rows,) * 2,
        out_specs=split_rows,
        check_vma=False,
    )
```

```python
import functools
import math

import jax
import jax.numpy as jnp
from jax import lax
from jax.experimental import pallas as pl
from jax.experimental.pallas import tpu as pltpu
from jax.sharding import PartitionSpec as P

NODE = 64
NVEC = 64
FIELDS = 8
HB = 2
LANES = 128
SUB = 8
AXES = ("dom", "tool")
TURN = 1.0 / (2.0 * math.pi)
REACH = math.sqrt(math.log2(math.e) / 4.0)
SHARE = math.sqrt(0.05)
FAR = -1e30
SINE = (6.283164044071425, -41.33714233428813, 81.34076747811504, -70.99341826772617)
LIFT = math.log2(-SINE[3] * SHARE * 0.5)
F32 = jnp.float32
BF16 = jnp.bfloat16
VMEM = pl.BlockSpec(memory_space=pltpu.VMEM)
SMEM = pl.BlockSpec(memory_space=pltpu.SMEM)
HBM = pl.BlockSpec(memory_space=pltpu.HBM)
ROUND = 1.5 * 2.0**23
PARTS = 3


def params(mib):
    return pltpu.CompilerParams(vmem_limit_bytes=mib << 20)


def left_half(rows):
    return lax.broadcasted_iota(jnp.int32, (rows, LANES), 1) < NODE


def swap(x):
    return pltpu.roll(x, NODE, 1)


def split(x):
    high = x.astype(BF16)
    return high, (x - high.astype(F32)).astype(BF16)


def three(x):
    high = x.astype(BF16).astype(F32)
    rest = x - high
    mid = rest.astype(BF16).astype(F32)
    return high, mid, rest - mid


def fold(out, half):
    pairs = NODE // 2
    even, odd = out[:pairs], out[pairs:]
    return jnp.where(half, even, odd) + swap(jnp.where(half, odd, even))


def flip(tiles):
    tiles = list(tiles)
    row = lax.broadcasted_iota(jnp.int32, (SUB, LANES), 0)
    for d in (4, 2, 1):
        keep = (row & d) == 0
        for i in range(SUB):
            if i & d:
                continue
            a, b = tiles[i], tiles[i + d]
            if 2 * d == SUB:
                moved = pltpu.roll(jnp.where(keep, b, a), d, 0)
                tiles[i], tiles[i + d] = jnp.where(keep, a, moved), jnp.where(keep, moved, b)
            else:
                tiles[i] = jnp.where(keep, a, pltpu.roll(b, d, 0))
                tiles[i + d] = jnp.where(keep, pltpu.roll(a, SUB - d, 0), b)
    return tiles


def flip_all(tiles):
    runs = [flip(tiles[i : i + SUB]) for i in range(0, len(tiles), SUB)]
    return [jnp.concatenate([run[j] for run in runs], axis=0) for j in range(SUB)]


def tiles_from(blocks):
    out = []
    for at in range(0, blocks[0].shape[0], SUB):
        out += flip([x[at : at + SUB] for x in blocks])
    return out


def doubled(x, half):
    other = swap(x)
    return jnp.where(half, x, other), jnp.where(half, other, x)


def high_low(x, half):
    return jnp.where(half, x, x - x.astype(BF16).astype(F32))


def copies_of(sources, targets, sems):
    made = [pltpu.make_async_copy(a, b, sems.at[i]) for i, (a, b) in enumerate(zip(sources, targets))]
    for copy in made:
        copy.start()
    return made


def pair_fields(x, y):
    quarter = left_half(x.shape[0])
    return jnp.concatenate([jnp.where(quarter, x, swap(y)), jnp.where(quarter, swap(x), y)], axis=0)


def field_rows(shape):
    row = lax.broadcasted_iota(jnp.int32, shape, 0)
    place = (row < 2) | (row == 4)
    return row, place, (row != 7) & ~place


def ranks(hits):
    n = hits.shape[1]
    upper = (
        lax.broadcasted_iota(jnp.int32, (n, n), 0) <= lax.broadcasted_iota(jnp.int32, (n, n), 1)
    ).astype(BF16)
    return jnp.dot(hits.astype(F32).astype(BF16), upper, preferred_element_type=F32)


def prep_kernel(
    doms, peers, capacity, stride, owners_hbm, seg_hbm, vec_hbm, send_ref, slot_hbm,
    owners_ref, seg_ref, first_ref, last_ref, edge_ref, slot_ref, sems,
):
    last = vec_hbm.shape[0] - 1
    got = copies_of(
        (owners_hbm, seg_hbm, vec_hbm.at[0], vec_hbm.at[last]), (owners_ref, seg_ref, first_ref, last_ref), sems
    )
    got[0].wait()
    got[1].wait()
    cands, blocks = owners_ref.shape
    pairs = NODE // 2
    share = 2 * HB * pairs // peers
    place = lax.broadcasted_iota(jnp.int32, (peers, blocks), 0)
    owner_ids = place % doms * (peers // doms) + place // doms
    lanes = lax.broadcasted_iota(jnp.int32, (peers, LANES), 1)
    send = jnp.zeros((peers, LANES), F32)
    before = jnp.zeros((peers, 1), F32)
    for k in range(cands):
        target = owners_ref[k : k + 1, :]
        hits = owner_ids == jnp.broadcast_to(target, (peers, blocks))
        places = jnp.where(hits, before + ranks(hits) - 1.0, -1.0)
        before = before + jnp.sum(hits.astype(F32), axis=1, keepdims=True)
        rank = jnp.sum(jnp.maximum(places, 0.0), axis=0, keepdims=True)
        slot_ref[k : k + 1, :] = target * stride + rank.astype(jnp.int32)
        wanted = jnp.broadcast_to(seg_ref[k : k + 1, :].astype(F32), (peers, blocks))
        for s in range(capacity):
            named = jnp.sum(jnp.where(places == float(s), wanted, 0.0), axis=1, keepdims=True)
            send = send + jnp.where(lanes == s, named, 0.0)
    slots = pltpu.make_async_copy(slot_ref, slot_hbm, sems.at[4])
    slots.start()
    send_ref[pl.ds(0, peers, stride=1 + share), :] = send
    got[2].wait()
    got[3].wait()
    for h in range(HB):
        edge_ref[h * pairs : (h + 1) * pairs, :] = first_ref[pl.ds(h, pairs, stride=SUB), :]
        edge_ref[(HB + h) * pairs : (HB + h + 1) * pairs, :] = last_ref[pl.ds(SUB - HB + h, pairs, stride=SUB), :]
    for r in range(share):
        send_ref[pl.ds(1 + r, peers, stride=1 + share), :] = edge_ref[pl.ds(r, peers, stride=share), :]
    slots.wait()


def turn_kernel(doms, tools, in_ref, out_ref):
    rows = in_ref.shape[0] // (doms * tools)
    for t in range(tools):
        for d in range(doms):
            source, target = (t * doms + d) * rows, (d * tools + t) * rows
            out_ref[target : target + rows, :] = in_ref[source : source + rows, :]


def rows_kernel(peers, capacity, stride, got_ref, part_ref, out_ref):
    segs, width = part_ref.shape[0], part_ref.shape[1] // PARTS
    chunks = width // LANES
    share = got_ref.shape[0] // peers - 1
    seg = lax.broadcasted_iota(jnp.int32, (peers, segs), 1)
    want = got_ref[pl.ds(0, peers, stride=1 + share), :].astype(jnp.int32)
    picks = jnp.concatenate([(seg == want[:, s : s + 1]).astype(F32).astype(BF16) for s in range(capacity)], axis=0)
    for c in range(chunks):
        got = None
        for p in range(PARTS):
            at = p * width + c * LANES
            term = jnp.dot(picks, part_ref[:, at : at + LANES], preferred_element_type=F32)
            got = term if got is None else got + term
        for s in range(capacity):
            out_ref[pl.ds(s * chunks + c, peers, stride=stride * chunks), :] = got[s * peers : (s + 1) * peers]
    me = lax.axis_index(AXES[1]) * lax.axis_size(AXES[0]) + lax.axis_index(AXES[0])
    peer = lax.broadcasted_iota(jnp.int32, (peers, LANES), 0)
    for r in range(share):
        edge = got_ref[pl.ds(1 + r, peers, stride=1 + share), :]
        following = jnp.where(peer == peers - 1, 0.0, pltpu.roll(edge, peers - 1, 0))
        previous = jnp.where(peer == 0, 0.0, pltpu.roll(edge, 1, 0))
        out_ref[pl.ds(capacity * chunks + r, peers, stride=stride * chunks), :] = jnp.where(
            me < peers // 2, following, previous
        )


def parts_kernel(after_prep, tool_hbm, part_ref, tool_ref, sems):
    copies_of((tool_hbm,), (tool_ref,), sems)[0].wait()
    width = tool_ref.shape[1]
    for p, part in enumerate(three(tool_ref[...])):
        part_ref[:, p * width : (p + 1) * width] = part.astype(BF16)


def ordered(row, h, m, l, order):
    out = jnp.zeros(row.shape, F32)
    for value, name in ((h, "h"), (m, "m"), (l, "l")):
        for i, at in enumerate(order):
            if at == name:
                out = jnp.where(row == i, value, out)
    return out


def main_kernel(
    columns_hbm, vec_hbm, rec_hbm, act_hbm, stiff_hbm, out_hbm, own_hbm, field_ref, slip_ref, edge_ref, rest_ref,
    columns_ref, vec_ref, rec_ref, act_ref, stiff_ref, wide_ref, left_ref, last_ref, out_ref, own_ref, sems, out_sems,
):
    nnz, groups = stiff_ref.shape[:2]
    blocks = groups * SUB
    pairs = NODE // 2
    even_count = nnz // 2 * 2
    half = left_half(SUB)
    half_rows = left_half(pairs)
    got = copies_of(
        (columns_hbm, vec_hbm, rec_hbm, act_hbm) + tuple(stiff_hbm.at[:, g] for g in range(groups)),
        (columns_ref, vec_ref, rec_ref, act_ref) + tuple(stiff_ref.at[:, g] for g in range(groups)),
        sems,
    )
    zero = jnp.zeros((NODE, LANES), BF16)
    for h in range(HB):
        wide_ref[h] = zero
        wide_ref[blocks + HB + h] = zero

    def tile(m):
        return pl.ds(m * SUB, SUB)

    def spread(g):
        for at in range(0, pairs, 2 * SUB):
            evens, odds = [], []
            for m in range(at, at + 2 * SUB):
                even, odd = doubled(vec_ref[g, tile(m), :], half)
                evens.append(high_low(even, half))
                odds.append(high_low(odd, half))
            for q, values in enumerate((evens, odds)):
                for j, x in enumerate(flip_all(values)):
                    own_ref[g * SUB + j, q * pairs + at : q * pairs + at + 2 * SUB, :] = x.astype(BF16)
            mixed = [x for both in zip(evens, odds) for x in both]
            for j, x in enumerate(flip_all(mixed)):
                wide_ref[HB + g * SUB + j, 2 * at : 2 * at + 4 * SUB, :] = x.astype(BF16)

    row, place, _ = field_rows((SUB, LANES))
    scale = jnp.where(place, REACH, 1.0)
    lane = lax.broadcasted_iota(jnp.int32, (SUB, LANES), 1)
    turn = lane // NODE * NODE + lane % pairs * 2 + lane % NODE // pairs

    def evens_first(x):
        return jnp.take_along_axis(x, turn, axis=1, mode="promise_in_bounds")

    def fields(g):
        for j in range(0, SUB, 2):
            x = rec_ref[g, pl.ds(j, FIELDS // 2, stride=SUB), :]
            y = rec_ref[g, pl.ds(j + 1, FIELDS // 2, stride=SUB), :]
            part = pair_fields(x, y) * scale
            norm = -0.5 * jnp.sum(jnp.where(place, part * part, 0.0), axis=0, keepdims=True)
            at = g * SUB + j
            flags = jnp.concatenate([act_ref[pl.ds(at, 1), :], act_ref[pl.ds(at + 1, 1), :]], axis=1)
            norm = jnp.where(flags == 0, FAR, norm)
            h, m, l = three(evens_first(part))
            extra = ordered(row, *three(evens_first(jnp.broadcast_to(norm, (SUB, LANES)))), "hml")
            extra = jnp.where((row > 2) & (row < 6), 1.0, extra)
            slip = ordered(row, h[7:8], m[7:8], l[7:8], "hhmhlm")
            none = jnp.zeros((SUB, LANES), F32)
            more = jnp.zeros((LANES - 10 * SUB, LANES), F32)
            stack = jnp.concatenate([h, h, m, h, l, m, extra, none, slip, swap(slip), more], axis=0).T
            field_ref[at] = stack[:NODE].astype(BF16)
            field_ref[at + 1] = stack[NODE:].astype(BF16)
            slip_ref[at // 2] = swap(stack[:NODE]).astype(BF16)

    def prepare(g):
        for at in range(0, pairs, 2 * SUB):
            for e in range(0, nnz, 2):
                evens, odds = [], []
                for m in range(at, at + 2 * SUB):
                    x = stiff_ref[e, g, tile(m), :]
                    if e < even_count:
                        y = stiff_ref[e + 1, g, tile(m), :]
                        evens.append(jnp.where(half, x, swap(y)))
                        odds.append(jnp.where(half, swap(x), y))
                    else:
                        even, odd = doubled(x, half)
                        evens.append(high_low(even, half))
                        odds.append(high_low(odd, half))
                for q, values in enumerate((evens, odds)):
                    rows = slice(q * pairs + at, q * pairs + at + 2 * SUB)
                    for j, x in enumerate(flip_all(values)):
                        if e < even_count:
                            high, low = split(x)
                            cols = slice(e * NODE, (e + 2) * NODE)
                            left_ref[j, rows, cols] = high
                            left_ref[j, NODE + rows.start : NODE + rows.stop, cols] = low
                        else:
                            last_ref[j, rows, :] = x.astype(BF16)

    def product(g):
        folded = []
        for j in range(SUB):
            cols = [wide_ref[columns_ref[e, g * SUB + j]] for e in range(nnz)]
            folded.append(fold(times(left_ref[j], last_ref[j], cols), half_rows))
        for m, x in enumerate(tiles_from(folded)):
            out_ref[g, m * SUB : (m + 1) * SUB, :] = x

    got[1].wait()
    spread(0)
    spread(1)
    got[4].wait()
    prepare(0)
    for h in range(HB):
        edge_ref[h] = left_ref[h]
        rest_ref[h] = last_ref[h]
    got[0].wait()
    got[2].wait()
    got[3].wait()

    def body(g, carry):
        pltpu.make_async_copy(stiff_hbm.at[:, g + 1], stiff_ref.at[:, g + 1], sems.at[5 + g]).wait()
        product(g)
        prepare(g + 1)
        spread(jnp.minimum(g + 2, groups - 1))
        fields(g)
        return carry

    lax.fori_loop(0, groups - 1, body, 0)
    owns = pltpu.make_async_copy(own_ref, own_hbm, out_sems.at[0])
    owns.start()
    product(groups - 1)
    inners = pltpu.make_async_copy(out_ref, out_hbm, out_sems.at[1])
    inners.start()
    fields(groups - 1)
    for h in range(HB):
        edge_ref[HB + h] = left_ref[SUB - HB + h]
        rest_ref[HB + h] = last_ref[SUB - HB + h]
    owns.wait()
    inners.wait()


def times(left, last, cols):
    even_count = left.shape[1] // NODE
    out = jnp.dot(left, jnp.concatenate(cols[:even_count], axis=0), preferred_element_type=F32)
    out = out[:NODE] + out[NODE:]
    if len(cols) > even_count:
        out = out + jnp.dot(last, jnp.concatenate([cols[-1], cols[-1]], axis=0), preferred_element_type=F32)
    return out


def contact_kernel(
    doms, tools, capacity, stride,
    slot_hbm, columns_hbm, own_hbm, inner_hbm, rows_ref, field_ref, slip_ref, edge_ref, rest_ref, out_ref,
    slot_ref, columns_ref, own_ref, inner_ref, tall_ref, gram_ref, halo_ref, wide_ref, hold_ref, delta_ref, sems, own_sems, inner_sems,
):
    got = copies_of((columns_hbm, slot_hbm), (columns_ref, slot_ref), sems)
    nnz, blocks = columns_ref.shape
    groups = blocks // SUB
    peers = doms * tools

    def own_copy(g):
        spot = pl.ds(g * SUB, SUB)
        return pltpu.make_async_copy(own_hbm.at[spot], own_ref.at[spot], own_sems.at[g])

    def inner_copy(g):
        return pltpu.make_async_copy(inner_hbm.at[g], inner_ref.at[g], inner_sems.at[g])

    for g in range(groups):
        own_copy(g).start()
        inner_copy(g).start()
    pairs = NODE // 2
    half = left_half(pairs)
    full = left_half(NODE)
    row, place, angle = field_rows((SUB, LANES))
    scale = jnp.where(place, REACH, jnp.where(row == 3, TURN, jnp.where(angle, 3.0 * TURN, 1.0)))
    none = jnp.zeros((SUB, LANES), F32)

    def tile_of(reach, phase, slip):
        turn = jnp.abs(phase - ((phase + ROUND) - ROUND)) - 0.25
        square = turn * turn
        wave = square + SINE[2] / SINE[3]
        wave = wave * square + SINE[1] / SINE[3]
        wave = wave * square + SINE[0] / SINE[3]
        return jnp.exp2(reach) * (wave * turn) * (2.0 + jnp.tanh(slip))

    def tiles(g):
        raws, slips = [], []
        for j in range(SUB):
            b = g * SUB + j
            tool = pair_fields(rows_ref[slot_ref[0, b]], rows_ref[slot_ref[1, b]]) * scale
            norm = LIFT - 0.5 * jnp.sum(jnp.where(place, tool * tool, 0.0), axis=0, keepdims=True)
            h, m, l = three(tool)
            extra = jnp.where(row < 3, 1.0, 0.0) + ordered(row, *three(norm), "---hml")
            right = []
            for mask, more in ((place, extra), (angle, none)):
                hm, mm, lm = (jnp.where(mask, v, 0.0) for v in (h, m, l))
                right.append(jnp.concatenate([hm, mm, hm, lm, hm, mm, more, none], axis=0).astype(BF16))
            right = jnp.concatenate(right, axis=1)
            raws.append(jnp.dot(field_ref[b][:, : right.shape[0]], right, preferred_element_type=F32))
            slips.append(ordered(row, h[7:8], m[7:8], l[7:8], "hmhlhm"))
            if j % 2:
                right = jnp.concatenate(
                    [jnp.concatenate([slips[j - 1], none], axis=1), jnp.concatenate([none, slips[j]], axis=1)], axis=0
                ).astype(BF16)
                slide = jnp.dot(slip_ref[b // 2][:, : 2 * SUB], right, preferred_element_type=F32)
                for i in range(2):
                    raw = raws[j - 1 + i]
                    high, low = split(tile_of(raw[:, :LANES], raw[:, LANES:], slide[:, i * LANES : (i + 1) * LANES]))
                    tall_ref[j - 1 + i, :NODE, :] = high
                    tall_ref[j - 1 + i, NODE:, :] = low

    def grams(g):
        for j in range(SUB):
            tall = tall_ref[j]
            gram = lax.dot_general(tall, tall, (((1,), (1,)), ((), ())), preferred_element_type=F32)
            gram = gram[:NODE] + gram[NODE:]
            gram_ref[j] = high_low(gram + swap(gram), full).astype(BF16)

    def apply(g):
        own_copy(g).wait()
        inner_copy(g).wait()
        folded = []
        for j in range(SUB):
            own = own_ref[g * SUB + j]
            out = jnp.dot(gram_ref[j], jnp.concatenate([own, own], axis=0), preferred_element_type=F32)
            folded.append(fold(out, half))
        for m, x in enumerate(tiles_from(folded)):
            spot = slice(m * SUB, (m + 1) * SUB)
            out_ref[g, spot, :] = inner_ref[g, spot, :] + x

    def halo():
        share = 2 * HB * pairs // peers
        step = min(share, rows_ref.shape[1])
        for at in range(0, 2 * HB * pairs, step):
            q, r = at // share, at % share
            p = q % doms * tools + q // doms
            halo_ref[at : at + step, :] = rows_ref[p * stride + capacity + r // step][:step]
        for h in range(2 * HB):
            even, odd = doubled(halo_ref[h * pairs : (h + 1) * pairs, :], half)
            hold_ref[h, pl.ds(0, pairs, stride=2), :] = even
            hold_ref[h, pl.ds(1, pairs, stride=2), :] = odd
            wide_ref[h] = high_low(hold_ref[h], full).astype(BF16)
        wide_ref[2 * HB] = jnp.zeros((NODE, LANES), BF16)
        got[0].wait()
        deltas = []
        for i in range(2 * HB):
            b = i if i < HB else blocks - 2 * HB + i
            cols = []
            for e in range(nnz):
                c = columns_ref[e, b]
                ahead, behind = c - blocks - HB, c + HB
                cols.append(wide_ref[jnp.where(c < HB, behind, jnp.where(ahead >= 0, ahead, 2 * HB))])
            deltas.append(fold(times(edge_ref[i], rest_ref[i], cols), half))
        return deltas

    deltas = halo()
    for i, delta in enumerate(deltas):
        delta_ref[i] = delta
    got[1].wait()
    tiles(0)
    grams(0)
    tiles(1)

    def body(g, carry):
        apply(g - 2)
        grams(g - 1)
        tiles(g)
        return carry

    lax.fori_loop(2, groups, body, 0)
    apply(groups - 2)
    grams(groups - 1)
    apply(groups - 1)
    for i in range(2 * HB):
        g, j = (0, i) if i < HB else (groups - 1, SUB - 2 * HB + i)
        spot = pl.ds(j, pairs, stride=SUB)
        out_ref[g, spot, :] = out_ref[g, spot, :] + delta_ref[i]


def per_device(records, tool_data, owners, local_seg, active, stiffness, columns, vectors):
    doms, tools = (lax.axis_size(axis) for axis in AXES)
    peers = doms * tools
    blocks, cands = owners.shape
    nnz = columns.shape[1]
    segs, width = tool_data.shape
    capacity = max(2, (3 * blocks * cands + 2 * peers - 1) // (2 * peers))
    groups = blocks // SUB
    pairs = NODE // 2
    chunks = width // LANES
    i32 = jnp.int32

    def shape(dims, dtype=F32):
        return jax.ShapeDtypeStruct(dims, dtype)

    def tiles_of(x, rows):
        lead = x.shape[:-2]
        n = len(lead)
        x = x.reshape(lead + (rows // SUB, SUB, x.shape[-1] // LANES, LANES))
        x = jnp.swapaxes(x, n + 1, n + 2)
        return x.reshape(lead + (rows // SUB, -1, LANES))

    vec = tiles_of(vectors, blocks)
    rec = tiles_of(records, blocks)
    stiff = tiles_of(jnp.swapaxes(stiffness, 0, 1), blocks)
    share = 2 * HB * pairs // peers
    stride = capacity + -(-share // chunks)

    def in_hbm(*arrays):
        return [pltpu.with_memory_space_constraint(x, pltpu.HBM) for x in arrays]

    send, slot = pl.pallas_call(
        functools.partial(prep_kernel, doms, peers, capacity, stride),
        out_shape=(shape((peers * (1 + share), LANES)), pltpu.HBM((cands, blocks), i32)),
        in_specs=[HBM] * 3,
        out_specs=(VMEM, HBM),
        scratch_shapes=[
            pltpu.VMEM((cands, blocks), i32),
            pltpu.VMEM((cands, blocks), i32),
            pltpu.VMEM(vec.shape[1:], F32),
            pltpu.VMEM(vec.shape[1:], F32),
            pltpu.VMEM((2 * HB * pairs, LANES), F32),
            pltpu.VMEM((cands, blocks), i32),
            pltpu.SemaphoreType.DMA((5,)),
        ],
        compiler_params=params(8),
        name="prep",
    )(*in_hbm(owners.T, local_seg.T, vec))

    def exchange(x, axis, size):
        x = x.reshape(size, peers // size * (1 + share), 1, LANES)
        x = lax.all_to_all(x, axis, split_axis=0, concat_axis=0, tiled=True)
        return x.reshape(peers * (1 + share), LANES)

    halfway = exchange(send, AXES[1], tools)
    halfway = pl.pallas_call(
        functools.partial(turn_kernel, doms, tools),
        out_shape=shape(halfway.shape),
        in_specs=[VMEM],
        out_specs=VMEM,
        compiler_params=params(4),
        name="turn",
    )(halfway)
    wanted = exchange(halfway, AXES[0], doms)

    parts = pl.pallas_call(
        parts_kernel,
        out_shape=shape((segs, PARTS * width), BF16),
        in_specs=[HBM] * 2,
        out_specs=VMEM,
        scratch_shapes=[pltpu.VMEM(tool_data.shape, F32), pltpu.SemaphoreType.DMA((1,))],
        compiler_params=params(8),
        cost_estimate=pl.CostEstimate(flops=1 << 20, bytes_accessed=4 << 20, transcendentals=0),
        name="parts",
    )(*in_hbm(slot, tool_data))

    rows_out = pl.pallas_call(
        functools.partial(rows_kernel, peers, capacity, stride),
        out_shape=shape((peers * stride * chunks, LANES)),
        in_specs=[VMEM] * 2,
        out_specs=VMEM,
        compiler_params=params(8),
        name="rows",
    )(wanted, parts)
    fetched = lax.all_to_all(
        rows_out.reshape(peers, stride, chunks, LANES), AXES, split_axis=0, concat_axis=0, tiled=True
    )

    wide = (blocks, NODE, LANES)
    left = (2 * NODE, nnz // 2 * 2 * NODE)
    inner, own, fields, slips, edges, rests = pl.pallas_call(
        main_kernel,
        out_shape=(
            pltpu.HBM(vec.shape, F32),
            pltpu.HBM(wide, BF16),
            shape(wide, BF16),
            shape((blocks // 2, NODE, LANES), BF16),
            shape((2 * HB,) + left, BF16),
            shape((2 * HB, NODE, LANES), BF16),
        ),
        in_specs=[HBM] * 5,
        out_specs=(HBM,) * 2 + (VMEM,) * 4,
        scratch_shapes=[
            pltpu.SMEM((nnz, blocks), i32),
            pltpu.VMEM(vec.shape, F32),
            pltpu.VMEM(rec.shape, F32),
            pltpu.VMEM(active.shape, i32),
            pltpu.VMEM(stiff.shape, F32),
            pltpu.VMEM((blocks + 2 * HB, NODE, LANES), BF16),
            pltpu.VMEM((SUB,) + left, BF16),
            pltpu.VMEM((SUB, NODE, LANES), BF16),
            pltpu.VMEM(vec.shape, F32),
            pltpu.VMEM(wide, BF16),
            pltpu.SemaphoreType.DMA((groups + 4,)),
            pltpu.SemaphoreType.DMA((2,)),
        ],
        compiler_params=params(20),
        cost_estimate=pl.CostEstimate(
            flops=6 * blocks * nnz * NODE * NODE * NVEC, bytes_accessed=24 << 20, transcendentals=0
        ),
        name="main",
    )(*in_hbm(columns.T, vec, rec, active, stiff))

    out = pl.pallas_call(
        functools.partial(contact_kernel, doms, tools, capacity, stride),
        out_shape=shape(vec.shape),
        in_specs=[HBM] * 4 + [VMEM] * 5,
        out_specs=VMEM,
        scratch_shapes=[
            pltpu.SMEM((cands, blocks), i32),
            pltpu.SMEM((nnz, blocks), i32),
            pltpu.VMEM(wide, BF16),
            pltpu.VMEM(vec.shape, F32),
            pltpu.VMEM((SUB, 2 * NODE, LANES), BF16),
            pltpu.VMEM((SUB, NODE, LANES), BF16),
            pltpu.VMEM((2 * HB * pairs, LANES), F32),
            pltpu.VMEM((2 * HB + 1, NODE, LANES), BF16),
            pltpu.VMEM((2 * HB, NODE, LANES), F32),
            pltpu.VMEM((2 * HB, pairs, LANES), F32),
            pltpu.SemaphoreType.DMA((2,)),
            pltpu.SemaphoreType.DMA((groups,)),
            pltpu.SemaphoreType.DMA((groups,)),
        ],
        compiler_params=params(16),
        cost_estimate=pl.CostEstimate(
            flops=80 * blocks * cands * NODE * NODE, bytes_accessed=4 << 20, transcendentals=2 * blocks * cands * NODE * NODE
        ),
        name="contact",
    )(*in_hbm(slot, columns.T, own, inner), fetched.reshape(peers * stride, chunks, LANES), fields, slips, edges, rests)
    out = out.reshape(groups, pairs, SUB, LANES)
    return jnp.swapaxes(out, 1, 2).reshape(blocks, NODE * NVEC)


def solution(mesh):
    split_rows = P(AXES, None)
    return jax.shard_map(
        per_device,
        mesh=mesh,
        in_specs=(split_rows,) * 5 + (P(AXES, None, None),) + (split_rows,) * 2,
        out_specs=split_rows,
        check_vma=False,
    )
```

```python
import functools
import math

import jax
import jax.numpy as jnp
from jax import lax
from jax.experimental import pallas as pl
from jax.experimental.pallas import tpu as pltpu
from jax.sharding import PartitionSpec as P

NODE = 64
NVEC = 64
FIELDS = 8
HB = 2
LANES = 128
SUB = 8
AXES = ("dom", "tool")
TURN = 1.0 / (2.0 * math.pi)
REACH = math.sqrt(math.log2(math.e) / 4.0)
SHARE = math.sqrt(0.05)
FAR = -1e30
SINE = (6.283164044071425, -41.33714233428813, 81.34076747811504, -70.99341826772617)
LIFT = math.log2(-SINE[3] * SHARE * 0.5)
F32 = jnp.float32
BF16 = jnp.bfloat16
VMEM = pl.BlockSpec(memory_space=pltpu.VMEM)
SMEM = pl.BlockSpec(memory_space=pltpu.SMEM)
HBM = pl.BlockSpec(memory_space=pltpu.HBM)
ROUND = 1.5 * 2.0**23
PARTS = 3


def params(mib):
    return pltpu.CompilerParams(vmem_limit_bytes=mib << 20)


def left_half(rows):
    return lax.broadcasted_iota(jnp.int32, (rows, LANES), 1) < NODE


def swap(x):
    return pltpu.roll(x, NODE, 1)


def split(x):
    high = x.astype(BF16)
    return high, (x - high.astype(F32)).astype(BF16)


def three(x):
    high = x.astype(BF16).astype(F32)
    rest = x - high
    mid = rest.astype(BF16).astype(F32)
    return high, mid, rest - mid


def fold(out, half):
    pairs = NODE // 2
    even, odd = out[:pairs], out[pairs:]
    return jnp.where(half, even, odd) + swap(jnp.where(half, odd, even))


def flip(tiles):
    tiles = list(tiles)
    row = lax.broadcasted_iota(jnp.int32, (SUB, LANES), 0)
    for d in (4, 2, 1):
        keep = (row & d) == 0
        for i in range(SUB):
            if i & d:
                continue
            a, b = tiles[i], tiles[i + d]
            if 2 * d == SUB:
                moved = pltpu.roll(jnp.where(keep, b, a), d, 0)
                tiles[i], tiles[i + d] = jnp.where(keep, a, moved), jnp.where(keep, moved, b)
            else:
                tiles[i] = jnp.where(keep, a, pltpu.roll(b, d, 0))
                tiles[i + d] = jnp.where(keep, pltpu.roll(a, SUB - d, 0), b)
    return tiles


def flip_all(tiles):
    runs = [flip(tiles[i : i + SUB]) for i in range(0, len(tiles), SUB)]
    return [jnp.concatenate([run[j] for run in runs], axis=0) for j in range(SUB)]


def tiles_from(blocks):
    out = []
    for at in range(0, blocks[0].shape[0], SUB):
        out += flip([x[at : at + SUB] for x in blocks])
    return out


def doubled(x, half):
    other = swap(x)
    return jnp.where(half, x, other), jnp.where(half, other, x)


def high_low(x, half):
    return jnp.where(half, x, x - x.astype(BF16).astype(F32))


def copies_of(sources, targets, sems):
    made = [pltpu.make_async_copy(a, b, sems.at[i]) for i, (a, b) in enumerate(zip(sources, targets))]
    for copy in made:
        copy.start()
    return made


def pair_fields(x, y):
    quarter = left_half(x.shape[0])
    return jnp.concatenate([jnp.where(quarter, x, swap(y)), jnp.where(quarter, swap(x), y)], axis=0)


def field_rows(shape):
    row = lax.broadcasted_iota(jnp.int32, shape, 0)
    place = (row < 2) | (row == 4)
    return row, place, (row != 7) & ~place


def ranks(hits):
    n = hits.shape[1]
    upper = (
        lax.broadcasted_iota(jnp.int32, (n, n), 0) <= lax.broadcasted_iota(jnp.int32, (n, n), 1)
    ).astype(BF16)
    return jnp.dot(hits.astype(F32).astype(BF16), upper, preferred_element_type=F32)


def prep_kernel(
    doms, peers, capacity, stride, owners_hbm, seg_hbm, vec_hbm, send_ref, slot_hbm,
    owners_ref, seg_ref, first_ref, last_ref, edge_ref, slot_ref, sems,
):
    last = vec_hbm.shape[0] - 1
    got = copies_of(
        (owners_hbm, seg_hbm, vec_hbm.at[0], vec_hbm.at[last]), (owners_ref, seg_ref, first_ref, last_ref), sems
    )
    got[0].wait()
    got[1].wait()
    cands, blocks = owners_ref.shape
    pairs = NODE // 2
    share = 2 * HB * pairs // peers
    place = lax.broadcasted_iota(jnp.int32, (peers, blocks), 0)
    owner_ids = place % doms * (peers // doms) + place // doms
    lanes = lax.broadcasted_iota(jnp.int32, (peers, LANES), 1)
    send = jnp.zeros((peers, LANES), F32)
    before = jnp.zeros((peers, 1), F32)
    for k in range(cands):
        target = owners_ref[k : k + 1, :]
        hits = owner_ids == jnp.broadcast_to(target, (peers, blocks))
        places = jnp.where(hits, before + ranks(hits) - 1.0, -1.0)
        before = before + jnp.sum(hits.astype(F32), axis=1, keepdims=True)
        rank = jnp.sum(jnp.maximum(places, 0.0), axis=0, keepdims=True)
        tools = peers // doms
        slot_ref[k : k + 1, :] = (target % tools * doms + target // tools) * stride + rank.astype(jnp.int32)
        wanted = jnp.broadcast_to(seg_ref[k : k + 1, :].astype(F32), (peers, blocks))
        for s in range(capacity):
            named = jnp.sum(jnp.where(places == float(s), wanted, 0.0), axis=1, keepdims=True)
            send = send + jnp.where(lanes == s, named, 0.0)
    slots = pltpu.make_async_copy(slot_ref, slot_hbm, sems.at[4])
    slots.start()
    send_ref[pl.ds(0, peers, stride=1 + share), :] = send
    got[2].wait()
    got[3].wait()
    for h in range(HB):
        edge_ref[h * pairs : (h + 1) * pairs, :] = first_ref[pl.ds(h, pairs, stride=SUB), :]
        edge_ref[(HB + h) * pairs : (HB + h + 1) * pairs, :] = last_ref[pl.ds(SUB - HB + h, pairs, stride=SUB), :]
    for r in range(share):
        send_ref[pl.ds(1 + r, peers, stride=1 + share), :] = edge_ref[pl.ds(r, peers, stride=share), :]
    slots.wait()


def rows_kernel(doms, peers, capacity, stride, got_ref, part_ref, out_ref):
    segs, width = part_ref.shape[0], part_ref.shape[1] // PARTS
    chunks = width // LANES
    share = got_ref.shape[0] // peers - 1
    seg = lax.broadcasted_iota(jnp.int32, (peers, segs), 1)
    want = got_ref[pl.ds(0, peers, stride=1 + share), :].astype(jnp.int32)
    picks = jnp.concatenate([(seg == want[:, s : s + 1]).astype(F32).astype(BF16) for s in range(capacity)], axis=0)
    for c in range(chunks):
        got = None
        for p in range(PARTS):
            at = p * width + c * LANES
            term = jnp.dot(picks, part_ref[:, at : at + LANES], preferred_element_type=F32)
            got = term if got is None else got + term
        for s in range(capacity):
            out_ref[pl.ds(s * chunks + c, peers, stride=stride * chunks), :] = got[s * peers : (s + 1) * peers]
    me = lax.axis_index(AXES[1]) * lax.axis_size(AXES[0]) + lax.axis_index(AXES[0])
    peer = lax.broadcasted_iota(jnp.int32, (peers, LANES), 0)
    for r in range(share):
        edge = got_ref[pl.ds(1 + r, peers, stride=1 + share), :]
        following = jnp.where(
            peer < peers - doms, pltpu.roll(edge, peers - doms, 0), pltpu.roll(edge, peers - doms - 1, 0)
        )
        following = jnp.where(peer == peers - 1, 0.0, following)
        previous = jnp.where(peer >= doms, pltpu.roll(edge, doms, 0), pltpu.roll(edge, doms + 1, 0))
        previous = jnp.where(peer == 0, 0.0, previous)
        out_ref[pl.ds(capacity * chunks + r, peers, stride=stride * chunks), :] = jnp.where(
            me < peers // 2, following, previous
        )


def parts_kernel(after_prep, tool_hbm, part_ref, tool_ref, sems):
    copies_of((tool_hbm,), (tool_ref,), sems)[0].wait()
    width = tool_ref.shape[1]
    for p, part in enumerate(three(tool_ref[...])):
        part_ref[:, p * width : (p + 1) * width] = part.astype(BF16)


def ordered(row, h, m, l, order):
    out = jnp.zeros(row.shape, F32)
    for value, name in ((h, "h"), (m, "m"), (l, "l")):
        for i, at in enumerate(order):
            if at == name:
                out = jnp.where(row == i, value, out)
    return out


def main_kernel(
    columns_hbm, vec_hbm, rec_hbm, act_hbm, stiff_hbm, out_hbm, own_hbm, field_ref, slip_ref, edge_ref, rest_ref,
    columns_ref, vec_ref, rec_ref, act_ref, stiff_ref, wide_ref, left_ref, last_ref, out_ref, own_ref, sems, out_sems,
):
    nnz, groups = stiff_ref.shape[:2]
    blocks = groups * SUB
    pairs = NODE // 2
    even_count = nnz // 2 * 2
    half = left_half(SUB)
    half_rows = left_half(pairs)
    got = copies_of(
        (columns_hbm, vec_hbm, rec_hbm, act_hbm) + tuple(stiff_hbm.at[:, g] for g in range(groups)),
        (columns_ref, vec_ref, rec_ref, act_ref) + tuple(stiff_ref.at[:, g] for g in range(groups)),
        sems,
    )
    zero = jnp.zeros((NODE, LANES), BF16)
    for h in range(HB):
        wide_ref[h] = zero
        wide_ref[blocks + HB + h] = zero

    def tile(m):
        return pl.ds(m * SUB, SUB)

    def spread(g):
        for at in range(0, pairs, 2 * SUB):
            evens, odds = [], []
            for m in range(at, at + 2 * SUB):
                even, odd = doubled(vec_ref[g, tile(m), :], half)
                evens.append(high_low(even, half))
                odds.append(high_low(odd, half))
            for q, values in enumerate((evens, odds)):
                for j, x in enumerate(flip_all(values)):
                    own_ref[g * SUB + j, q * pairs + at : q * pairs + at + 2 * SUB, :] = x.astype(BF16)
            mixed = [x for both in zip(evens, odds) for x in both]
            for j, x in enumerate(flip_all(mixed)):
                wide_ref[HB + g * SUB + j, 2 * at : 2 * at + 4 * SUB, :] = x.astype(BF16)

    row, place, _ = field_rows((SUB, LANES))
    scale = jnp.where(place, REACH, 1.0)
    lane = lax.broadcasted_iota(jnp.int32, (SUB, LANES), 1)
    turn = lane // NODE * NODE + lane % pairs * 2 + lane % NODE // pairs

    def evens_first(x):
        return jnp.take_along_axis(x, turn, axis=1, mode="promise_in_bounds")

    def fields(g):
        for j in range(0, SUB, 2):
            x = rec_ref[g, pl.ds(j, FIELDS // 2, stride=SUB), :]
            y = rec_ref[g, pl.ds(j + 1, FIELDS // 2, stride=SUB), :]
            part = pair_fields(x, y) * scale
            norm = -0.5 * jnp.sum(jnp.where(place, part * part, 0.0), axis=0, keepdims=True)
            at = g * SUB + j
            flags = jnp.concatenate([act_ref[pl.ds(at, 1), :], act_ref[pl.ds(at + 1, 1), :]], axis=1)
            norm = jnp.where(flags == 0, FAR, norm)
            h, m, l = three(evens_first(part))
            extra = ordered(row, *three(evens_first(jnp.broadcast_to(norm, (SUB, LANES)))), "hml")
            extra = jnp.where((row > 2) & (row < 6), 1.0, extra)
            slip = ordered(row, h[7:8], m[7:8], l[7:8], "hhmhlm")
            none = jnp.zeros((SUB, LANES), F32)
            more = jnp.zeros((LANES - 10 * SUB, LANES), F32)
            stack = jnp.concatenate([h, h, m, h, l, m, extra, none, slip, swap(slip), more], axis=0).T
            field_ref[at] = stack[:NODE].astype(BF16)
            field_ref[at + 1] = stack[NODE:].astype(BF16)
            slip_ref[at // 2] = swap(stack[:NODE]).astype(BF16)

    def prepare(g):
        for at in range(0, pairs, 2 * SUB):
            for e in range(0, nnz, 2):
                evens, odds = [], []
                for m in range(at, at + 2 * SUB):
                    x = stiff_ref[e, g, tile(m), :]
                    if e < even_count:
                        y = stiff_ref[e + 1, g, tile(m), :]
                        evens.append(jnp.where(half, x, swap(y)))
                        odds.append(jnp.where(half, swap(x), y))
                    else:
                        even, odd = doubled(x, half)
                        evens.append(high_low(even, half))
                        odds.append(high_low(odd, half))
                for q, values in enumerate((evens, odds)):
                    rows = slice(q * pairs + at, q * pairs + at + 2 * SUB)
                    for j, x in enumerate(flip_all(values)):
                        if e < even_count:
                            high, low = split(x)
                            cols = slice(e * NODE, (e + 2) * NODE)
                            left_ref[j, rows, cols] = high
                            left_ref[j, NODE + rows.start : NODE + rows.stop, cols] = low
                        else:
                            last_ref[j, rows, :] = x.astype(BF16)

    def product(g):
        folded = []
        for j in range(SUB):
            cols = [wide_ref[columns_ref[e, g * SUB + j]] for e in range(nnz)]
            folded.append(fold(times(left_ref[j], last_ref[j], cols), half_rows))
        for m, x in enumerate(tiles_from(folded)):
            out_ref[g, m * SUB : (m + 1) * SUB, :] = x

    got[1].wait()
    spread(0)
    spread(1)
    got[4].wait()
    prepare(0)
    for h in range(HB):
        edge_ref[h] = left_ref[h]
        rest_ref[h] = last_ref[h]
    got[0].wait()
    got[2].wait()
    got[3].wait()

    def body(g, carry):
        pltpu.make_async_copy(stiff_hbm.at[:, g + 1], stiff_ref.at[:, g + 1], sems.at[5 + g]).wait()
        product(g)
        prepare(g + 1)
        spread(jnp.minimum(g + 2, groups - 1))
        fields(g)
        return carry

    lax.fori_loop(0, groups - 1, body, 0)
    owns = pltpu.make_async_copy(own_ref, own_hbm, out_sems.at[0])
    owns.start()
    product(groups - 1)
    inners = pltpu.make_async_copy(out_ref, out_hbm, out_sems.at[1])
    inners.start()
    fields(groups - 1)
    for h in range(HB):
        edge_ref[HB + h] = left_ref[SUB - HB + h]
        rest_ref[HB + h] = last_ref[SUB - HB + h]
    owns.wait()
    inners.wait()


def times(left, last, cols):
    even_count = left.shape[1] // NODE
    out = jnp.dot(left, jnp.concatenate(cols[:even_count], axis=0), preferred_element_type=F32)
    out = out[:NODE] + out[NODE:]
    if len(cols) > even_count:
        out = out + jnp.dot(last, jnp.concatenate([cols[-1], cols[-1]], axis=0), preferred_element_type=F32)
    return out


def contact_kernel(
    peers, capacity, stride,
    slot_hbm, columns_hbm, own_hbm, inner_hbm, rows_ref, field_ref, slip_ref, edge_ref, rest_ref, out_ref,
    slot_ref, columns_ref, own_ref, inner_ref, tall_ref, gram_ref, halo_ref, wide_ref, hold_ref, delta_ref, sems, own_sems, inner_sems,
):
    got = copies_of((columns_hbm, slot_hbm), (columns_ref, slot_ref), sems)
    nnz, blocks = columns_ref.shape
    groups = blocks // SUB

    def own_copy(g):
        spot = pl.ds(g * SUB, SUB)
        return pltpu.make_async_copy(own_hbm.at[spot], own_ref.at[spot], own_sems.at[g])

    def inner_copy(g):
        return pltpu.make_async_copy(inner_hbm.at[g], inner_ref.at[g], inner_sems.at[g])

    for g in range(groups):
        own_copy(g).start()
        inner_copy(g).start()
    pairs = NODE // 2
    half = left_half(pairs)
    full = left_half(NODE)
    row, place, angle = field_rows((SUB, LANES))
    scale = jnp.where(place, REACH, jnp.where(row == 3, TURN, jnp.where(angle, 3.0 * TURN, 1.0)))
    none = jnp.zeros((SUB, LANES), F32)

    def tile_of(reach, phase, slip):
        turn = jnp.abs(phase - ((phase + ROUND) - ROUND)) - 0.25
        square = turn * turn
        wave = square + SINE[2] / SINE[3]
        wave = wave * square + SINE[1] / SINE[3]
        wave = wave * square + SINE[0] / SINE[3]
        return jnp.exp2(reach) * (wave * turn) * (2.0 + jnp.tanh(slip))

    def tiles(g):
        raws, slips = [], []
        for j in range(SUB):
            b = g * SUB + j
            tool = pair_fields(rows_ref[slot_ref[0, b]], rows_ref[slot_ref[1, b]]) * scale
            norm = LIFT - 0.5 * jnp.sum(jnp.where(place, tool * tool, 0.0), axis=0, keepdims=True)
            h, m, l = three(tool)
            extra = jnp.where(row < 3, 1.0, 0.0) + ordered(row, *three(norm), "---hml")
            right = []
            for mask, more in ((place, extra), (angle, none)):
                hm, mm, lm = (jnp.where(mask, v, 0.0) for v in (h, m, l))
                right.append(jnp.concatenate([hm, mm, hm, lm, hm, mm, more, none], axis=0).astype(BF16))
            right = jnp.concatenate(right, axis=1)
            raws.append(jnp.dot(field_ref[b][:, : right.shape[0]], right, preferred_element_type=F32))
            slips.append(ordered(row, h[7:8], m[7:8], l[7:8], "hmhlhm"))
            if j % 2:
                right = jnp.concatenate(
                    [jnp.concatenate([slips[j - 1], none], axis=1), jnp.concatenate([none, slips[j]], axis=1)], axis=0
                ).astype(BF16)
                slide = jnp.dot(slip_ref[b // 2][:, : 2 * SUB], right, preferred_element_type=F32)
                for i in range(2):
                    raw = raws[j - 1 + i]
                    high, low = split(tile_of(raw[:, :LANES], raw[:, LANES:], slide[:, i * LANES : (i + 1) * LANES]))
                    tall_ref[j - 1 + i, :NODE, :] = high
                    tall_ref[j - 1 + i, NODE:, :] = low

    def grams(g):
        for j in range(SUB):
            tall = tall_ref[j]
            gram = lax.dot_general(tall, tall, (((1,), (1,)), ((), ())), preferred_element_type=F32)
            gram = gram[:NODE] + gram[NODE:]
            gram_ref[j] = high_low(gram + swap(gram), full).astype(BF16)

    def apply(g):
        own_copy(g).wait()
        inner_copy(g).wait()
        folded = []
        for j in range(SUB):
            own = own_ref[g * SUB + j]
            out = jnp.dot(gram_ref[j], jnp.concatenate([own, own], axis=0), preferred_element_type=F32)
            folded.append(fold(out, half))
        for m, x in enumerate(tiles_from(folded)):
            spot = slice(m * SUB, (m + 1) * SUB)
            out_ref[g, spot, :] = inner_ref[g, spot, :] + x

    def halo():
        share = 2 * HB * pairs // peers
        step = min(share, rows_ref.shape[1])
        for at in range(0, 2 * HB * pairs, step):
            q, r = at // share, at % share
            halo_ref[at : at + step, :] = rows_ref[q * stride + capacity + r // step][:step]
        for h in range(2 * HB):
            even, odd = doubled(halo_ref[h * pairs : (h + 1) * pairs, :], half)
            hold_ref[h, pl.ds(0, pairs, stride=2), :] = even
            hold_ref[h, pl.ds(1, pairs, stride=2), :] = odd
            wide_ref[h] = high_low(hold_ref[h], full).astype(BF16)
        wide_ref[2 * HB] = jnp.zeros((NODE, LANES), BF16)
        got[0].wait()
        deltas = []
        for i in range(2 * HB):
            b = i if i < HB else blocks - 2 * HB + i
            cols = []
            for e in range(nnz):
                c = columns_ref[e, b]
                ahead, behind = c - blocks - HB, c + HB
                cols.append(wide_ref[jnp.where(c < HB, behind, jnp.where(ahead >= 0, ahead, 2 * HB))])
            deltas.append(fold(times(edge_ref[i], rest_ref[i], cols), half))
        return deltas

    deltas = halo()
    for i, delta in enumerate(deltas):
        delta_ref[i] = delta
    got[1].wait()
    tiles(0)
    grams(0)
    tiles(1)

    def body(g, carry):
        apply(g - 2)
        grams(g - 1)
        tiles(g)
        return carry

    lax.fori_loop(2, groups, body, 0)
    apply(groups - 2)
    grams(groups - 1)
    apply(groups - 1)
    for i in range(2 * HB):
        g, j = (0, i) if i < HB else (groups - 1, SUB - 2 * HB + i)
        spot = pl.ds(j, pairs, stride=SUB)
        out_ref[g, spot, :] = out_ref[g, spot, :] + delta_ref[i]


def per_device(records, tool_data, owners, local_seg, active, stiffness, columns, vectors):
    doms, tools = (lax.axis_size(axis) for axis in AXES)
    peers = doms * tools
    blocks, cands = owners.shape
    nnz = columns.shape[1]
    segs, width = tool_data.shape
    capacity = max(2, (3 * blocks * cands + 2 * peers - 1) // (2 * peers))
    groups = blocks // SUB
    pairs = NODE // 2
    chunks = width // LANES
    i32 = jnp.int32

    def shape(dims, dtype=F32):
        return jax.ShapeDtypeStruct(dims, dtype)

    def tiles_of(x, rows):
        lead = x.shape[:-2]
        n = len(lead)
        x = x.reshape(lead + (rows // SUB, SUB, x.shape[-1] // LANES, LANES))
        x = jnp.swapaxes(x, n + 1, n + 2)
        return x.reshape(lead + (rows // SUB, -1, LANES))

    vec = tiles_of(vectors, blocks)
    rec = tiles_of(records, blocks)
    stiff = tiles_of(jnp.swapaxes(stiffness, 0, 1), blocks)
    share = 2 * HB * pairs // peers
    stride = capacity + -(-share // chunks)

    def in_hbm(*arrays):
        return [pltpu.with_memory_space_constraint(x, pltpu.HBM) for x in arrays]

    send, slot = pl.pallas_call(
        functools.partial(prep_kernel, doms, peers, capacity, stride),
        out_shape=(shape((peers * (1 + share), LANES)), pltpu.HBM((cands, blocks), i32)),
        in_specs=[HBM] * 3,
        out_specs=(VMEM, HBM),
        scratch_shapes=[
            pltpu.VMEM((cands, blocks), i32),
            pltpu.VMEM((cands, blocks), i32),
            pltpu.VMEM(vec.shape[1:], F32),
            pltpu.VMEM(vec.shape[1:], F32),
            pltpu.VMEM((2 * HB * pairs, LANES), F32),
            pltpu.VMEM((cands, blocks), i32),
            pltpu.SemaphoreType.DMA((5,)),
        ],
        compiler_params=params(8),
        name="prep",
    )(*in_hbm(owners.T, local_seg.T, vec))

    members = AXES[::-1]
    wanted = lax.all_to_all(send.reshape(peers, 1 + share, 1, LANES), members, split_axis=0, concat_axis=0, tiled=True)
    wanted = wanted.reshape(peers * (1 + share), LANES)

    parts = pl.pallas_call(
        parts_kernel,
        out_shape=shape((segs, PARTS * width), BF16),
        in_specs=[HBM] * 2,
        out_specs=VMEM,
        scratch_shapes=[pltpu.VMEM(tool_data.shape, F32), pltpu.SemaphoreType.DMA((1,))],
        compiler_params=params(8),
        cost_estimate=pl.CostEstimate(flops=1 << 20, bytes_accessed=4 << 20, transcendentals=0),
        name="parts",
    )(*in_hbm(slot, tool_data))

    rows_out = pl.pallas_call(
        functools.partial(rows_kernel, doms, peers, capacity, stride),
        out_shape=shape((peers * stride * chunks, LANES)),
        in_specs=[VMEM] * 2,
        out_specs=VMEM,
        compiler_params=params(8),
        name="rows",
    )(wanted, parts)
    fetched = lax.all_to_all(
        rows_out.reshape(peers, stride, chunks, LANES), members, split_axis=0, concat_axis=0, tiled=True
    )

    wide = (blocks, NODE, LANES)
    left = (2 * NODE, nnz // 2 * 2 * NODE)
    inner, own, fields, slips, edges, rests = pl.pallas_call(
        main_kernel,
        out_shape=(
            pltpu.HBM(vec.shape, F32),
            pltpu.HBM(wide, BF16),
            shape(wide, BF16),
            shape((blocks // 2, NODE, LANES), BF16),
            shape((2 * HB,) + left, BF16),
            shape((2 * HB, NODE, LANES), BF16),
        ),
        in_specs=[HBM] * 5,
        out_specs=(HBM,) * 2 + (VMEM,) * 4,
        scratch_shapes=[
            pltpu.SMEM((nnz, blocks), i32),
            pltpu.VMEM(vec.shape, F32),
            pltpu.VMEM(rec.shape, F32),
            pltpu.VMEM(active.shape, i32),
            pltpu.VMEM(stiff.shape, F32),
            pltpu.VMEM((blocks + 2 * HB, NODE, LANES), BF16),
            pltpu.VMEM((SUB,) + left, BF16),
            pltpu.VMEM((SUB, NODE, LANES), BF16),
            pltpu.VMEM(vec.shape, F32),
            pltpu.VMEM(wide, BF16),
            pltpu.SemaphoreType.DMA((groups + 4,)),
            pltpu.SemaphoreType.DMA((2,)),
        ],
        compiler_params=params(20),
        cost_estimate=pl.CostEstimate(
            flops=6 * blocks * nnz * NODE * NODE * NVEC, bytes_accessed=24 << 20, transcendentals=0
        ),
        name="main",
    )(*in_hbm(columns.T, vec, rec, active, stiff))

    out = pl.pallas_call(
        functools.partial(contact_kernel, peers, capacity, stride),
        out_shape=shape(vec.shape),
        in_specs=[HBM] * 4 + [VMEM] * 5,
        out_specs=VMEM,
        scratch_shapes=[
            pltpu.SMEM((cands, blocks), i32),
            pltpu.SMEM((nnz, blocks), i32),
            pltpu.VMEM(wide, BF16),
            pltpu.VMEM(vec.shape, F32),
            pltpu.VMEM((SUB, 2 * NODE, LANES), BF16),
            pltpu.VMEM((SUB, NODE, LANES), BF16),
            pltpu.VMEM((2 * HB * pairs, LANES), F32),
            pltpu.VMEM((2 * HB + 1, NODE, LANES), BF16),
            pltpu.VMEM((2 * HB, NODE, LANES), F32),
            pltpu.VMEM((2 * HB, pairs, LANES), F32),
            pltpu.SemaphoreType.DMA((2,)),
            pltpu.SemaphoreType.DMA((groups,)),
            pltpu.SemaphoreType.DMA((groups,)),
        ],
        compiler_params=params(16),
        cost_estimate=pl.CostEstimate(
            flops=80 * blocks * cands * NODE * NODE, bytes_accessed=4 << 20, transcendentals=2 * blocks * cands * NODE * NODE
        ),
        name="contact",
    )(*in_hbm(slot, columns.T, own, inner), fetched.reshape(peers * stride, chunks, LANES), fields, slips, edges, rests)
    out = out.reshape(groups, pairs, SUB, LANES)
    return jnp.swapaxes(out, 1, 2).reshape(blocks, NODE * NVEC)


def solution(mesh):
    split_rows = P(AXES, None)
    return jax.shard_map(
        per_device,
        mesh=mesh,
        in_specs=(split_rows,) * 5 + (P(AXES, None, None),) + (split_rows,) * 2,
        out_specs=split_rows,
        check_vma=False,
    )
```

```python
import functools
import math

import jax
import jax.numpy as jnp
from jax import lax
from jax.experimental import pallas as pl
from jax.experimental.pallas import tpu as pltpu
from jax.sharding import PartitionSpec as P

NODE = 64
NVEC = 64
FIELDS = 8
HB = 2
LANES = 128
SUB = 8
AXES = ("dom", "tool")
TURN = 1.0 / (2.0 * math.pi)
REACH = math.sqrt(math.log2(math.e) / 4.0)
SHARE = math.sqrt(0.05)
FAR = -1e30
SINE = (6.283164044071425, -41.33714233428813, 81.34076747811504, -70.99341826772617)
LIFT = math.log2(-SINE[3] * SHARE * 0.5)
F32 = jnp.float32
BF16 = jnp.bfloat16
VMEM = pl.BlockSpec(memory_space=pltpu.VMEM)
SMEM = pl.BlockSpec(memory_space=pltpu.SMEM)
HBM = pl.BlockSpec(memory_space=pltpu.HBM)
ROUND = 1.5 * 2.0**23
PARTS = 3


def params(mib):
    return pltpu.CompilerParams(vmem_limit_bytes=mib << 20)


def left_half(rows):
    return lax.broadcasted_iota(jnp.int32, (rows, LANES), 1) < NODE


def swap(x):
    return pltpu.roll(x, NODE, 1)


def split(x):
    high = x.astype(BF16)
    return high, (x - high.astype(F32)).astype(BF16)


def three(x):
    high = x.astype(BF16).astype(F32)
    rest = x - high
    mid = rest.astype(BF16).astype(F32)
    return high, mid, rest - mid


def fold(out, half):
    pairs = NODE // 2
    even, odd = out[:pairs], out[pairs:]
    return jnp.where(half, even, odd) + swap(jnp.where(half, odd, even))


def flip(tiles):
    tiles = list(tiles)
    row = lax.broadcasted_iota(jnp.int32, (SUB, LANES), 0)
    for d in (4, 2, 1):
        keep = (row & d) == 0
        for i in range(SUB):
            if i & d:
                continue
            a, b = tiles[i], tiles[i + d]
            if 2 * d == SUB:
                moved = pltpu.roll(jnp.where(keep, b, a), d, 0)
                tiles[i], tiles[i + d] = jnp.where(keep, a, moved), jnp.where(keep, moved, b)
            else:
                tiles[i] = jnp.where(keep, a, pltpu.roll(b, d, 0))
                tiles[i + d] = jnp.where(keep, pltpu.roll(a, SUB - d, 0), b)
    return tiles


def flip_all(tiles):
    runs = [flip(tiles[i : i + SUB]) for i in range(0, len(tiles), SUB)]
    return [jnp.concatenate([run[j] for run in runs], axis=0) for j in range(SUB)]


def tiles_from(blocks):
    out = []
    for at in range(0, blocks[0].shape[0], SUB):
        out += flip([x[at : at + SUB] for x in blocks])
    return out


def doubled(x, half):
    other = swap(x)
    return jnp.where(half, x, other), jnp.where(half, other, x)


def high_low(x, half):
    return jnp.where(half, x, x - x.astype(BF16).astype(F32))


def copies_of(sources, targets, sems):
    made = [pltpu.make_async_copy(a, b, sems.at[i]) for i, (a, b) in enumerate(zip(sources, targets))]
    for copy in made:
        copy.start()
    return made


def pair_fields(x, y):
    quarter = left_half(x.shape[0])
    return jnp.concatenate([jnp.where(quarter, x, swap(y)), jnp.where(quarter, swap(x), y)], axis=0)


def field_rows(shape):
    row = lax.broadcasted_iota(jnp.int32, shape, 0)
    place = (row < 2) | (row == 4)
    return row, place, (row != 7) & ~place


def ranks(hits):
    n = hits.shape[1]
    upper = (
        lax.broadcasted_iota(jnp.int32, (n, n), 0) <= lax.broadcasted_iota(jnp.int32, (n, n), 1)
    ).astype(BF16)
    return jnp.dot(hits.astype(F32).astype(BF16), upper, preferred_element_type=F32)


def prep_kernel(
    peers, segs, owners_hbm, seg_hbm, vec_hbm, send_ref, owners_ref, seg_ref, first_ref, last_ref, edge_ref, sems
):
    last = vec_hbm.shape[0] - 1
    got = copies_of(
        (owners_hbm, seg_hbm, vec_hbm.at[0], vec_hbm.at[last]), (owners_ref, seg_ref, first_ref, last_ref), sems
    )
    cands = owners_ref.shape[0]
    pairs = NODE // 2
    share = 2 * HB * pairs // peers
    got[0].wait()
    got[1].wait()
    wanted = [owners_ref[k : k + 1, :] * segs + seg_ref[k : k + 1, :] for k in range(cands)]
    wanted = jnp.concatenate(wanted, axis=1).astype(F32)
    send_ref[pl.ds(0, peers, stride=1 + share), :] = jnp.broadcast_to(wanted, (peers, LANES))
    got[2].wait()
    got[3].wait()
    for h in range(HB):
        edge_ref[h * pairs : (h + 1) * pairs, :] = first_ref[pl.ds(h, pairs, stride=SUB), :]
        edge_ref[(HB + h) * pairs : (HB + h + 1) * pairs, :] = last_ref[pl.ds(SUB - HB + h, pairs, stride=SUB), :]
    for r in range(share):
        send_ref[pl.ds(1 + r, peers, stride=1 + share), :] = edge_ref[pl.ds(r, peers, stride=share), :]


def rows_kernel(peers, capacity, stride, got_ref, part_ref, out_ref):
    segs, width = part_ref.shape[0], part_ref.shape[1] // PARTS
    chunks = width // LANES
    share = got_ref.shape[0] // peers - 1
    doms, tools = (lax.axis_size(axis) for axis in AXES)
    at_dom, at_tool = (lax.axis_index(axis) for axis in AXES)
    seg = lax.broadcasted_iota(jnp.int32, (peers, segs), 1).astype(F32)
    local = got_ref[pl.ds(0, peers, stride=1 + share), :] - ((at_dom * tools + at_tool) * segs).astype(F32)
    hits = (local >= 0.0) & (local < float(segs))
    rank = ranks(hits)
    picks = []
    for s in range(capacity):
        row = jnp.sum(jnp.where(hits & (rank == s + 1.0), local, 0.0), axis=1, keepdims=True)
        picks.append((seg == row).astype(F32).astype(BF16))
    picks = jnp.concatenate(picks, axis=0)
    for c in range(0, chunks, 2):
        got = None
        for p in range(PARTS):
            at = p * width + c * LANES
            term = jnp.dot(picks, part_ref[:, at : at + 2 * LANES], preferred_element_type=F32)
            got = term if got is None else got + term
        for s in range(capacity):
            for i in range(2):
                out_ref[pl.ds(s * chunks + c + i, peers, stride=stride * chunks), :] = got[
                    s * peers : (s + 1) * peers, i * LANES : (i + 1) * LANES
                ]
    me = at_tool * doms + at_dom
    peer = lax.broadcasted_iota(jnp.int32, (peers, LANES), 0)
    for r in range(share):
        edge = got_ref[pl.ds(1 + r, peers, stride=1 + share), :]
        following = jnp.where(
            peer < peers - doms, pltpu.roll(edge, peers - doms, 0), pltpu.roll(edge, peers - doms - 1, 0)
        )
        following = jnp.where(peer == peers - 1, 0.0, following)
        previous = jnp.where(peer >= doms, pltpu.roll(edge, doms, 0), pltpu.roll(edge, doms + 1, 0))
        previous = jnp.where(peer == 0, 0.0, previous)
        out_ref[pl.ds(capacity * chunks + r, peers, stride=stride * chunks), :] = jnp.where(
            me < peers // 2, following, previous
        )


def parts_kernel(after_prep, tool_hbm, part_ref, tool_ref, sems):
    copies_of((tool_hbm,), (tool_ref,), sems)[0].wait()
    width = tool_ref.shape[1]
    for p, part in enumerate(three(tool_ref[...])):
        part_ref[:, p * width : (p + 1) * width] = part.astype(BF16)


def ordered(row, h, m, l, order):
    out = jnp.zeros(row.shape, F32)
    for value, name in ((h, "h"), (m, "m"), (l, "l")):
        for i, at in enumerate(order):
            if at == name:
                out = jnp.where(row == i, value, out)
    return out


def main_kernel(
    doms, peers, capacity, stride,
    columns_hbm, vec_hbm, rec_hbm, act_hbm, owners_hbm, stiff_hbm, out_hbm, slot_hbm, own_ref, field_ref, edge_ref,
    columns_ref, vec_ref, rec_ref, act_ref, owners_ref, stiff_ref,
    wide_ref, left_ref, last_ref, out_ref, slot_ref, sems, out_sems,
):
    nnz, groups = stiff_ref.shape[:2]
    blocks = groups * SUB
    pairs = NODE // 2
    even_count = nnz // 2 * 2
    half = left_half(SUB)
    half_rows = left_half(pairs)
    got = copies_of(
        (columns_hbm, vec_hbm, rec_hbm, act_hbm, owners_hbm) + tuple(stiff_hbm.at[:, g] for g in range(groups)),
        (columns_ref, vec_ref, rec_ref, act_ref, owners_ref) + tuple(stiff_ref.at[:, g] for g in range(groups)),
        sems,
    )
    zero = jnp.zeros((NODE, LANES), BF16)
    for h in range(HB):
        wide_ref[h] = zero
        wide_ref[blocks + HB + h] = zero

    def tile(m):
        return pl.ds(m * SUB, SUB)

    def spread(g):
        for at in range(0, pairs, 2 * SUB):
            evens, odds = [], []
            for m in range(at, at + 2 * SUB):
                even, odd = doubled(vec_ref[g, tile(m), :], half)
                evens.append(high_low(even, half))
                odds.append(high_low(odd, half))
            for q, values in enumerate((evens, odds)):
                for j, x in enumerate(flip_all(values)):
                    own_ref[g * SUB + j, q * pairs + at : q * pairs + at + 2 * SUB, :] = x.astype(BF16)
            mixed = [x for both in zip(evens, odds) for x in both]
            for j, x in enumerate(flip_all(mixed)):
                wide_ref[HB + g * SUB + j, 2 * at : 2 * at + 4 * SUB, :] = x.astype(BF16)

    row, place, _ = field_rows((SUB, LANES))
    scale = jnp.where(place, REACH, 1.0)
    lane = lax.broadcasted_iota(jnp.int32, (SUB, LANES), 1)
    turn = lane // NODE * NODE + lane % pairs * 2 + lane % NODE // pairs

    def evens_first(x):
        return jnp.take_along_axis(x, turn, axis=1, mode="promise_in_bounds")

    def fields(g):
        for j in range(0, SUB, 2):
            x = rec_ref[g, pl.ds(j, FIELDS // 2, stride=SUB), :]
            y = rec_ref[g, pl.ds(j + 1, FIELDS // 2, stride=SUB), :]
            part = pair_fields(x, y) * scale
            norm = -0.5 * jnp.sum(jnp.where(place, part * part, 0.0), axis=0, keepdims=True)
            at = g * SUB + j
            flags = jnp.concatenate([act_ref[pl.ds(at, 1), :], act_ref[pl.ds(at + 1, 1), :]], axis=1)
            norm = jnp.where(flags == 0, FAR, norm)
            h, m, l = three(evens_first(part))
            norms = three(evens_first(jnp.broadcast_to(norm, (SUB, LANES))))
            slip = ordered(row, h[7:8], m[7:8], l[7:8], "hhmhlm")
            lists = [jnp.where(row == 7, n, v) for n, v in zip(norms + (1.0, 1.0, 1.0), (h, h, m, h, l, m))]
            more = jnp.zeros((LANES - 8 * SUB, LANES), F32)
            stack = jnp.concatenate(lists + [slip, swap(slip), more], axis=0).T.astype(BF16)
            field_ref[at] = stack[:NODE]
            field_ref[at + 1] = stack[NODE:]

    def prepare(g):
        for at in range(0, pairs, 2 * SUB):
            for e in range(0, nnz, 2):
                evens, odds = [], []
                for m in range(at, at + 2 * SUB):
                    x = stiff_ref[e, g, tile(m), :]
                    if e < even_count:
                        y = stiff_ref[e + 1, g, tile(m), :]
                        evens.append(jnp.where(half, x, swap(y)))
                        odds.append(jnp.where(half, swap(x), y))
                    else:
                        even, odd = doubled(x, half)
                        evens.append(high_low(even, half))
                        odds.append(high_low(odd, half))
                for q, values in enumerate((evens, odds)):
                    rows = slice(q * pairs + at, q * pairs + at + 2 * SUB)
                    for j, x in enumerate(flip_all(values)):
                        if e < even_count:
                            high, low = split(x)
                            cols = slice(e * NODE, (e + 2) * NODE)
                            left_ref[j, rows, cols] = high
                            left_ref[j, NODE + rows.start : NODE + rows.stop, cols] = low
                        else:
                            last_ref[j, rows, :] = x.astype(BF16)

    def product(g):
        folded = []
        for j in range(SUB):
            cols = [wide_ref[columns_ref[e, g * SUB + j]] for e in range(nnz)]
            folded.append(fold(times(left_ref[j], last_ref[j], cols), half_rows))
        for m, x in enumerate(tiles_from(folded)):
            out_ref[g, m * SUB : (m + 1) * SUB, :] = x

    def edges(side, g, first):
        for i in range(HB):
            j = first + i
            sums = []
            for h in range(HB):
                total = jnp.zeros((pairs, LANES), F32)
                for e in range(nnz):
                    here = columns_ref[e, g * SUB + j] == side * (blocks + HB) + h
                    total = total + jnp.where(here, stiff_ref[e, g, pl.ds(j, pairs, stride=SUB), :], 0.0)
                sums.append(total)
            x, y = sums
            left = jnp.concatenate([jnp.where(half_rows, x, swap(y)), jnp.where(half_rows, swap(x), y)], axis=0)
            high, low = split(left)
            edge_ref[side, i * 2 * NODE : i * 2 * NODE + NODE, :] = high
            edge_ref[side, i * 2 * NODE + NODE : (i + 1) * 2 * NODE, :] = low

    got[1].wait()
    spread(0)
    spread(1)
    got[5].wait()
    prepare(0)
    got[0].wait()
    edges(0, 0, 0)
    got[2].wait()
    got[3].wait()
    got[4].wait()
    cands = owners_ref.shape[0]
    owner_ids = lax.broadcasted_iota(jnp.int32, (peers, blocks), 0)
    before = jnp.zeros((peers, 1), F32)
    for k in range(cands):
        target = owners_ref[k : k + 1, :]
        hits = owner_ids == jnp.broadcast_to(target, (peers, blocks))
        places = jnp.where(hits, before + ranks(hits) - 1.0, 0.0)
        before = before + jnp.sum(hits.astype(F32), axis=1, keepdims=True)
        rank = jnp.sum(places, axis=0, keepdims=True)
        tools = peers // doms
        slot_ref[k : k + 1, :] = (target % tools * doms + target // tools) * stride + rank.astype(jnp.int32)
    slots = pltpu.make_async_copy(slot_ref, slot_hbm, out_sems.at[0])
    slots.start()

    def body(g, carry):
        pltpu.make_async_copy(stiff_hbm.at[:, g + 1], stiff_ref.at[:, g + 1], sems.at[6 + g]).wait()
        product(g)
        prepare(g + 1)
        spread(jnp.minimum(g + 2, groups - 1))
        fields(g)
        return carry

    lax.fori_loop(0, groups - 1, body, 0)
    product(groups - 1)
    inners = pltpu.make_async_copy(out_ref, out_hbm, out_sems.at[1])
    inners.start()
    fields(groups - 1)
    edges(1, groups - 1, SUB - HB)
    slots.wait()
    inners.wait()


def times(left, last, cols):
    even_count = left.shape[1] // NODE
    out = jnp.dot(left, jnp.concatenate(cols[:even_count], axis=0), preferred_element_type=F32)
    out = out[:NODE] + out[NODE:]
    if len(cols) > even_count:
        out = out + jnp.dot(last, jnp.concatenate([cols[-1], cols[-1]], axis=0), preferred_element_type=F32)
    return out


def contact_kernel(
    peers, capacity, stride, slot_hbm, inner_hbm, rows_ref, field_ref, own_ref, edge_ref, out_hbm,
    slot_ref, inner_ref, out_ref, tall_ref, gram_ref, halo_ref, wide_ref, hold_ref, delta_ref, sems, out_sems,
):
    got = copies_of((slot_hbm, inner_hbm), (slot_ref, inner_ref), sems)
    blocks = slot_ref.shape[1]
    groups = blocks // SUB
    pairs = NODE // 2
    half = left_half(pairs)
    full = left_half(NODE)
    row, place, angle = field_rows((SUB, LANES))
    scale = jnp.where(place, REACH, jnp.where(row == 3, TURN, jnp.where(angle, 3.0 * TURN, 1.0)))
    none = jnp.zeros((SUB, LANES), F32)
    tail = row == 7

    def tile_of(reach, phase, slip):
        turn = jnp.abs(phase - ((phase + ROUND) - ROUND)) - 0.25
        square = turn * turn
        wave = square + SINE[2] / SINE[3]
        wave = wave * square + SINE[1] / SINE[3]
        wave = wave * square + SINE[0] / SINE[3]
        return jnp.exp2(reach) * (wave * turn) * (2.0 + jnp.tanh(slip))

    def tiles(g):
        raws, slips = [], []
        for j in range(SUB):
            b = g * SUB + j
            tool = pair_fields(rows_ref[slot_ref[0, b]], rows_ref[slot_ref[1, b]]) * scale
            norm = LIFT - 0.5 * jnp.sum(jnp.where(place, tool * tool, 0.0), axis=0, keepdims=True)
            h, m, l = three(tool)
            nh, nm, nl = three(norm)
            ones = jnp.where(tail, 1.0, 0.0)
            hp, mp, lp = (jnp.where(place, v, 0.0) for v in (h, m, l))
            ha, ma, la = (jnp.where(angle, v, 0.0) for v in (h, m, l))
            reach = [hp + ones, mp + ones, hp + ones, jnp.where(tail, nh, lp), jnp.where(tail, nm, hp), jnp.where(tail, nl, mp)]
            right = jnp.concatenate(
                [jnp.concatenate(x, axis=0).astype(BF16) for x in (reach, [ha, ma, ha, la, ha, ma])], axis=1
            )
            raws.append(jnp.dot(field_ref[b][:, : 6 * SUB], right, preferred_element_type=F32))
            slips.append(ordered(row, h[7:8], m[7:8], l[7:8], "hmhlhm"))
            if j % 2:
                right = jnp.concatenate(
                    [jnp.concatenate([slips[j - 1], none], axis=1), jnp.concatenate([none, slips[j]], axis=1)], axis=0
                ).astype(BF16)
                slide = jnp.dot(field_ref[b - 1][:, 6 * SUB : 8 * SUB], right, preferred_element_type=F32)
                for i in range(2):
                    raw = raws[j - 1 + i]
                    high, low = split(tile_of(raw[:, :LANES], raw[:, LANES:], slide[:, i * LANES : (i + 1) * LANES]))
                    tall_ref[j - 1 + i, :NODE, :] = high
                    tall_ref[j - 1 + i, NODE:, :] = low

    def grams(g):
        for j in range(SUB):
            tall = tall_ref[j]
            gram = lax.dot_general(tall, tall, (((1,), (1,)), ((), ())), preferred_element_type=F32)
            gram = gram[:NODE] + gram[NODE:]
            gram_ref[j] = high_low(gram + swap(gram), full).astype(BF16)

    def out_copy(g):
        return pltpu.make_async_copy(out_ref.at[g], out_hbm.at[g], out_sems.at[g])

    def apply(g):
        folded = []
        for j in range(SUB):
            own = own_ref[g * SUB + j]
            out = jnp.dot(gram_ref[j], jnp.concatenate([own, own], axis=0), preferred_element_type=F32)
            folded.append(fold(out, half))
        for m, x in enumerate(tiles_from(folded)):
            spot = slice(m * SUB, (m + 1) * SUB)
            out_ref[g, spot, :] = inner_ref[g, spot, :] + x
        out_copy(g).start()

    share = 2 * HB * pairs // peers
    step = min(share, rows_ref.shape[1])
    for at in range(0, 2 * HB * pairs, step):
        q, r = at // share, at % share
        halo_ref[at : at + step, :] = rows_ref[q * stride + capacity + r // step][:step]
    for side in range(2):
        for h in range(HB):
            at = ((1 - side) * HB + h) * pairs
            even, odd = doubled(halo_ref[at : at + pairs, :], half)
            hold_ref[h, pl.ds(0, pairs, stride=2), :] = even
            hold_ref[h, pl.ds(1, pairs, stride=2), :] = odd
            wide_ref[side, h * NODE : (h + 1) * NODE, :] = high_low(hold_ref[h], full).astype(BF16)
        out = jnp.dot(edge_ref[side], wide_ref[side], preferred_element_type=F32)
        for i in range(HB):
            at = i * 2 * NODE
            delta_ref[side * HB + i] = fold(out[at : at + NODE] + out[at + NODE : at + 2 * NODE], half)
    got[0].wait()
    tiles(0)
    grams(0)
    tiles(1)
    got[1].wait()
    for i in range(2 * HB):
        g, j = (0, i) if i < HB else (groups - 1, SUB - 2 * HB + i)
        spot = pl.ds(j, pairs, stride=SUB)
        inner_ref[g, spot, :] = inner_ref[g, spot, :] + delta_ref[i]

    def body(g, carry):
        apply(g - 2)
        grams(g - 1)
        tiles(g)
        return carry

    lax.fori_loop(2, groups, body, 0)
    apply(groups - 2)
    grams(groups - 1)
    apply(groups - 1)
    for g in range(groups):
        out_copy(g).wait()


def per_device(records, tool_data, owners, local_seg, active, stiffness, columns, vectors):
    doms, tools = (lax.axis_size(axis) for axis in AXES)
    peers = doms * tools
    blocks, cands = owners.shape
    nnz = columns.shape[1]
    segs, width = tool_data.shape
    capacity = max(2, (3 * blocks * cands + 2 * peers - 1) // (2 * peers))
    groups = blocks // SUB
    pairs = NODE // 2
    chunks = width // LANES
    i32 = jnp.int32

    def shape(dims, dtype=F32):
        return jax.ShapeDtypeStruct(dims, dtype)

    def tiles_of(x, rows):
        lead = x.shape[:-2]
        n = len(lead)
        x = x.reshape(lead + (rows // SUB, SUB, x.shape[-1] // LANES, LANES))
        x = jnp.swapaxes(x, n + 1, n + 2)
        return x.reshape(lead + (rows // SUB, -1, LANES))

    vec = tiles_of(vectors, blocks)
    rec = tiles_of(records, blocks)
    stiff = tiles_of(jnp.swapaxes(stiffness, 0, 1), blocks)
    share = 2 * HB * pairs // peers
    stride = capacity + -(-share // chunks)

    def in_hbm(*arrays):
        return [pltpu.with_memory_space_constraint(x, pltpu.HBM) for x in arrays]

    send = pl.pallas_call(
        functools.partial(prep_kernel, peers, segs),
        out_shape=shape((peers * (1 + share), LANES)),
        in_specs=[HBM] * 3,
        out_specs=VMEM,
        scratch_shapes=[
            pltpu.VMEM((cands, blocks), i32),
            pltpu.VMEM((cands, blocks), i32),
            pltpu.VMEM(vec.shape[1:], F32),
            pltpu.VMEM(vec.shape[1:], F32),
            pltpu.VMEM((2 * HB * pairs, LANES), F32),
            pltpu.SemaphoreType.DMA((4,)),
        ],
        compiler_params=params(8),
        name="prep",
    )(*in_hbm(owners.T, local_seg.T, vec))

    members = AXES[::-1]
    wanted = lax.all_to_all(send.reshape(peers, 1 + share, 1, LANES), members, split_axis=0, concat_axis=0, tiled=True)
    wanted = wanted.reshape(peers * (1 + share), LANES)

    parts = pl.pallas_call(
        parts_kernel,
        out_shape=shape((segs, PARTS * width), BF16),
        in_specs=[HBM] * 2,
        out_specs=VMEM,
        scratch_shapes=[pltpu.VMEM(tool_data.shape, F32), pltpu.SemaphoreType.DMA((1,))],
        compiler_params=params(8),
        cost_estimate=pl.CostEstimate(flops=1 << 20, bytes_accessed=4 << 20, transcendentals=0),
        name="parts",
    )(*in_hbm(send, tool_data))

    rows_out = pl.pallas_call(
        functools.partial(rows_kernel, peers, capacity, stride),
        out_shape=shape((peers * stride * chunks, LANES)),
        in_specs=[VMEM] * 2,
        out_specs=VMEM,
        compiler_params=params(8),
        name="rows",
    )(wanted, parts)
    fetched = lax.all_to_all(
        rows_out.reshape(peers, stride, chunks, LANES), members, split_axis=0, concat_axis=0, tiled=True
    )

    wide = (blocks, NODE, LANES)
    left = (2 * NODE, nnz // 2 * 2 * NODE)
    inner, slot, own, fields, edges = pl.pallas_call(
        functools.partial(main_kernel, doms, peers, capacity, stride),
        out_shape=(
            pltpu.HBM(vec.shape, F32),
            pltpu.HBM((cands, blocks), i32),
            shape(wide, BF16),
            shape(wide, BF16),
            shape((2, HB * 2 * NODE, LANES), BF16),
        ),
        in_specs=[HBM] * 6,
        out_specs=(HBM,) * 2 + (VMEM,) * 3,
        scratch_shapes=[
            pltpu.SMEM((nnz, blocks), i32),
            pltpu.VMEM(vec.shape, F32),
            pltpu.VMEM(rec.shape, F32),
            pltpu.VMEM(active.shape, i32),
            pltpu.VMEM((cands, blocks), i32),
            pltpu.VMEM(stiff.shape, F32),
            pltpu.VMEM((blocks + 2 * HB, NODE, LANES), BF16),
            pltpu.VMEM((SUB,) + left, BF16),
            pltpu.VMEM((SUB, NODE, LANES), BF16),
            pltpu.VMEM(vec.shape, F32),
            pltpu.VMEM((cands, blocks), i32),
            pltpu.SemaphoreType.DMA((groups + 5,)),
            pltpu.SemaphoreType.DMA((2,)),
        ],
        compiler_params=params(20),
        cost_estimate=pl.CostEstimate(
            flops=6 * blocks * nnz * NODE * NODE * NVEC, bytes_accessed=24 << 20, transcendentals=0
        ),
        name="main",
    )(*in_hbm(columns.T, vec, rec, active, owners.T, stiff))

    out = pl.pallas_call(
        functools.partial(contact_kernel, peers, capacity, stride),
        out_shape=pltpu.HBM(vec.shape, F32),
        in_specs=[HBM] * 2 + [VMEM] * 4,
        out_specs=HBM,
        scratch_shapes=[
            pltpu.SMEM((cands, blocks), i32),
            pltpu.VMEM(vec.shape, F32),
            pltpu.VMEM(vec.shape, F32),
            pltpu.VMEM((SUB, 2 * NODE, LANES), BF16),
            pltpu.VMEM((SUB, NODE, LANES), BF16),
            pltpu.VMEM((2 * HB * pairs, LANES), F32),
            pltpu.VMEM((2, HB * NODE, LANES), BF16),
            pltpu.VMEM((HB, NODE, LANES), F32),
            pltpu.VMEM((2 * HB, pairs, LANES), F32),
            pltpu.SemaphoreType.DMA((2,)),
            pltpu.SemaphoreType.DMA((groups,)),
        ],
        compiler_params=params(16),
        cost_estimate=pl.CostEstimate(
            flops=80 * blocks * cands * NODE * NODE, bytes_accessed=4 << 20, transcendentals=2 * blocks * cands * NODE * NODE
        ),
        name="contact",
    )(*in_hbm(slot, inner), fetched.reshape(peers * stride, chunks, LANES), fields, own, edges)
    out = out.reshape(groups, pairs, SUB, LANES)
    return jnp.swapaxes(out, 1, 2).reshape(blocks, NODE * NVEC)


def solution(mesh):
    split_rows = P(AXES, None)
    return jax.shard_map(
        per_device,
        mesh=mesh,
        in_specs=(split_rows,) * 5 + (P(AXES, None, None),) + (split_rows,) * 2,
        out_specs=split_rows,
        check_vma=False,
    )
```

```python
import functools
import math

import jax
import jax.numpy as jnp
from jax import lax
from jax.experimental import pallas as pl
from jax.experimental.pallas import tpu as pltpu
from jax.sharding import PartitionSpec as P

NODE = 64
NVEC = 64
FIELDS = 8
HB = 2
LANES = 128
SUB = 8
AXES = ("dom", "tool")
TURN = 1.0 / (2.0 * math.pi)
REACH = math.sqrt(math.log2(math.e) / 4.0)
SHARE = math.sqrt(0.05)
FAR = -1e30
SINE = (6.283164044071425, -41.33714233428813, 81.34076747811504, -70.99341826772617)
LIFT = math.log2(-SINE[3] * SHARE * 0.5)
F32 = jnp.float32
BF16 = jnp.bfloat16
VMEM = pl.BlockSpec(memory_space=pltpu.VMEM)
SMEM = pl.BlockSpec(memory_space=pltpu.SMEM)
HBM = pl.BlockSpec(memory_space=pltpu.HBM)
ROUND = 1.5 * 2.0**23
PARTS = 3


def params(mib):
    return pltpu.CompilerParams(vmem_limit_bytes=mib << 20)


def left_half(rows):
    return lax.broadcasted_iota(jnp.int32, (rows, LANES), 1) < NODE


def swap(x):
    return pltpu.roll(x, NODE, 1)


def split(x):
    high = x.astype(BF16)
    return high, (x - high.astype(F32)).astype(BF16)


def three(x):
    high = x.astype(BF16).astype(F32)
    rest = x - high
    mid = rest.astype(BF16).astype(F32)
    return high, mid, rest - mid


def fold(out, half):
    pairs = NODE // 2
    even, odd = out[:pairs], out[pairs:]
    return jnp.where(half, even, odd) + swap(jnp.where(half, odd, even))


def flip(tiles):
    tiles = list(tiles)
    row = lax.broadcasted_iota(jnp.int32, (SUB, LANES), 0)
    for d in (4, 2, 1):
        keep = (row & d) == 0
        for i in range(SUB):
            if i & d:
                continue
            a, b = tiles[i], tiles[i + d]
            if 2 * d == SUB:
                moved = pltpu.roll(jnp.where(keep, b, a), d, 0)
                tiles[i], tiles[i + d] = jnp.where(keep, a, moved), jnp.where(keep, moved, b)
            else:
                tiles[i] = jnp.where(keep, a, pltpu.roll(b, d, 0))
                tiles[i + d] = jnp.where(keep, pltpu.roll(a, SUB - d, 0), b)
    return tiles


def flip_all(tiles):
    runs = [flip(tiles[i : i + SUB]) for i in range(0, len(tiles), SUB)]
    return [jnp.concatenate([run[j] for run in runs], axis=0) for j in range(SUB)]


def tiles_from(blocks):
    out = []
    for at in range(0, blocks[0].shape[0], SUB):
        out += flip([x[at : at + SUB] for x in blocks])
    return out


def doubled(x, half):
    other = swap(x)
    return jnp.where(half, x, other), jnp.where(half, other, x)


def high_low(x, half):
    return jnp.where(half, x, x - x.astype(BF16).astype(F32))


def copies_of(sources, targets, sems):
    made = [pltpu.make_async_copy(a, b, sems.at[i]) for i, (a, b) in enumerate(zip(sources, targets))]
    for copy in made:
        copy.start()
    return made


def pair_fields(x, y):
    quarter = left_half(x.shape[0])
    return jnp.concatenate([jnp.where(quarter, x, swap(y)), jnp.where(quarter, swap(x), y)], axis=0)


def field_rows(shape):
    row = lax.broadcasted_iota(jnp.int32, shape, 0)
    place = (row < 2) | (row == 4)
    return row, place, (row != 7) & ~place


def ranks(hits):
    n = hits.shape[1]
    upper = (
        lax.broadcasted_iota(jnp.int32, (n, n), 0) <= lax.broadcasted_iota(jnp.int32, (n, n), 1)
    ).astype(BF16)
    return jnp.dot(hits.astype(F32).astype(BF16), upper, preferred_element_type=F32)


def prep_kernel(
    peers, segs, owners_hbm, seg_hbm, vec_hbm, send_ref, owners_ref, seg_ref, first_ref, last_ref, edge_ref, sems
):
    last = vec_hbm.shape[0] - 1
    got = copies_of(
        (owners_hbm, seg_hbm, vec_hbm.at[0], vec_hbm.at[last]), (owners_ref, seg_ref, first_ref, last_ref), sems
    )
    cands = owners_ref.shape[0]
    pairs = NODE // 2
    share = 2 * HB * pairs // peers
    got[0].wait()
    got[1].wait()
    wanted = [owners_ref[k : k + 1, :] * segs + seg_ref[k : k + 1, :] for k in range(cands)]
    wanted = jnp.concatenate(wanted, axis=1).astype(F32)
    send_ref[pl.ds(0, peers, stride=1 + share), :] = jnp.broadcast_to(wanted, (peers, LANES))
    got[2].wait()
    got[3].wait()
    for h in range(HB):
        edge_ref[h * pairs : (h + 1) * pairs, :] = first_ref[pl.ds(h, pairs, stride=SUB), :]
        edge_ref[(HB + h) * pairs : (HB + h + 1) * pairs, :] = last_ref[pl.ds(SUB - HB + h, pairs, stride=SUB), :]
    for r in range(share):
        send_ref[pl.ds(1 + r, peers, stride=1 + share), :] = edge_ref[pl.ds(r, peers, stride=share), :]


def rows_kernel(peers, capacity, stride, got_ref, part_ref, out_ref):
    segs, width = part_ref.shape[0], part_ref.shape[1] // PARTS
    chunks = width // LANES
    share = got_ref.shape[0] // peers - 1
    doms, tools = (lax.axis_size(axis) for axis in AXES)
    at_dom, at_tool = (lax.axis_index(axis) for axis in AXES)
    seg = lax.broadcasted_iota(jnp.int32, (peers, segs), 1).astype(F32)
    local = got_ref[pl.ds(0, peers, stride=1 + share), :] - ((at_dom * tools + at_tool) * segs).astype(F32)
    hits = (local >= 0.0) & (local < float(segs))
    rank = ranks(hits)
    picks = []
    for s in range(capacity):
        row = jnp.sum(jnp.where(hits & (rank == s + 1.0), local, 0.0), axis=1, keepdims=True)
        picks.append((seg == row).astype(F32).astype(BF16))
    picks = jnp.concatenate(picks, axis=0)
    for c in range(0, chunks, 2):
        got = None
        for p in range(PARTS):
            at = p * width + c * LANES
            term = jnp.dot(picks, part_ref[:, at : at + 2 * LANES], preferred_element_type=F32)
            got = term if got is None else got + term
        for s in range(capacity):
            for i in range(2):
                out_ref[pl.ds(s * chunks + c + i, peers, stride=stride * chunks), :] = got[
                    s * peers : (s + 1) * peers, i * LANES : (i + 1) * LANES
                ]
    me = at_tool * doms + at_dom
    peer = lax.broadcasted_iota(jnp.int32, (peers, LANES), 0)
    for r in range(share):
        edge = got_ref[pl.ds(1 + r, peers, stride=1 + share), :]
        following = jnp.where(
            peer < peers - doms, pltpu.roll(edge, peers - doms, 0), pltpu.roll(edge, peers - doms - 1, 0)
        )
        following = jnp.where(peer == peers - 1, 0.0, following)
        previous = jnp.where(peer >= doms, pltpu.roll(edge, doms, 0), pltpu.roll(edge, doms + 1, 0))
        previous = jnp.where(peer == 0, 0.0, previous)
        out_ref[pl.ds(capacity * chunks + r, peers, stride=stride * chunks), :] = jnp.where(
            me < peers // 2, following, previous
        )


def parts_kernel(after_prep, tool_hbm, part_ref, tool_ref, sems):
    copies_of((tool_hbm,), (tool_ref,), sems)[0].wait()
    width = tool_ref.shape[1]
    for p, part in enumerate(three(tool_ref[...])):
        part_ref[:, p * width : (p + 1) * width] = part.astype(BF16)


def ordered(row, h, m, l, order):
    out = jnp.zeros(row.shape, F32)
    for value, name in ((h, "h"), (m, "m"), (l, "l")):
        for i, at in enumerate(order):
            if at == name:
                out = jnp.where(row == i, value, out)
    return out


def main_kernel(
    doms, peers, capacity, stride,
    columns_hbm, vec_hbm, rec_hbm, act_hbm, owners_hbm, stiff_hbm, out_hbm, slot_ref, own_ref, field_ref, edge_ref,
    columns_ref, vec_ref, rec_ref, act_ref, owners_ref, stiff_ref,
    wide_ref, left_ref, last_ref, out_ref, sems, out_sem,
):
    nnz, groups = stiff_ref.shape[:2]
    blocks = groups * SUB
    pairs = NODE // 2
    even_count = nnz // 2 * 2
    half = left_half(SUB)
    half_rows = left_half(pairs)
    got = copies_of(
        (columns_hbm, vec_hbm, rec_hbm, act_hbm, owners_hbm) + tuple(stiff_hbm.at[:, g] for g in range(groups)),
        (columns_ref, vec_ref, rec_ref, act_ref, owners_ref) + tuple(stiff_ref.at[:, g] for g in range(groups)),
        sems,
    )
    zero = jnp.zeros((NODE, LANES), BF16)
    for h in range(HB):
        wide_ref[h] = zero
        wide_ref[blocks + HB + h] = zero

    def tile(m):
        return pl.ds(m * SUB, SUB)

    def spread(g):
        for at in range(0, pairs, 2 * SUB):
            evens, odds = [], []
            for m in range(at, at + 2 * SUB):
                even, odd = doubled(vec_ref[g, tile(m), :], half)
                evens.append(high_low(even, half))
                odds.append(high_low(odd, half))
            for q, values in enumerate((evens, odds)):
                for j, x in enumerate(flip_all(values)):
                    own_ref[g * SUB + j, q * pairs + at : q * pairs + at + 2 * SUB, :] = x.astype(BF16)
            mixed = [x for both in zip(evens, odds) for x in both]
            for j, x in enumerate(flip_all(mixed)):
                wide_ref[HB + g * SUB + j, 2 * at : 2 * at + 4 * SUB, :] = x.astype(BF16)

    row, place, _ = field_rows((SUB, LANES))
    scale = jnp.where(place, REACH, 1.0)
    lane = lax.broadcasted_iota(jnp.int32, (SUB, LANES), 1)
    turn = lane // NODE * NODE + lane % pairs * 2 + lane % NODE // pairs

    def evens_first(x):
        return jnp.take_along_axis(x, turn, axis=1, mode="promise_in_bounds")

    def fields(g):
        for j in range(0, SUB, 2):
            x = rec_ref[g, pl.ds(j, FIELDS // 2, stride=SUB), :]
            y = rec_ref[g, pl.ds(j + 1, FIELDS // 2, stride=SUB), :]
            part = pair_fields(x, y) * scale
            norm = -0.5 * jnp.sum(jnp.where(place, part * part, 0.0), axis=0, keepdims=True)
            at = g * SUB + j
            flags = jnp.concatenate([act_ref[pl.ds(at, 1), :], act_ref[pl.ds(at + 1, 1), :]], axis=1)
            norm = jnp.where(flags == 0, FAR, norm)
            h, m, l = three(evens_first(part))
            norms = three(evens_first(jnp.broadcast_to(norm, (SUB, LANES))))
            slip = ordered(row, h[7:8], m[7:8], l[7:8], "hhmhlm")
            lists = [jnp.where(row == 7, n, v) for n, v in zip(norms + (1.0, 1.0, 1.0), (h, h, m, h, l, m))]
            more = jnp.zeros((LANES - 8 * SUB, LANES), F32)
            stack = jnp.concatenate(lists + [slip, swap(slip), more], axis=0).T.astype(BF16)
            field_ref[at] = stack[:NODE]
            field_ref[at + 1] = stack[NODE:]

    def prepare(g):
        for at in range(0, pairs, 2 * SUB):
            for e in range(0, nnz, 2):
                evens, odds = [], []
                for m in range(at, at + 2 * SUB):
                    x = stiff_ref[e, g, tile(m), :]
                    if e < even_count:
                        y = stiff_ref[e + 1, g, tile(m), :]
                        evens.append(jnp.where(half, x, swap(y)))
                        odds.append(jnp.where(half, swap(x), y))
                    else:
                        even, odd = doubled(x, half)
                        evens.append(high_low(even, half))
                        odds.append(high_low(odd, half))
                for q, values in enumerate((evens, odds)):
                    rows = slice(q * pairs + at, q * pairs + at + 2 * SUB)
                    for j, x in enumerate(flip_all(values)):
                        if e < even_count:
                            high, low = split(x)
                            cols = slice(e * NODE, (e + 2) * NODE)
                            left_ref[j, rows, cols] = high
                            left_ref[j, NODE + rows.start : NODE + rows.stop, cols] = low
                        else:
                            last_ref[j, rows, :] = x.astype(BF16)

    def product(g):
        folded = []
        for j in range(SUB):
            cols = [wide_ref[columns_ref[e, g * SUB + j]] for e in range(nnz)]
            folded.append(fold(times(left_ref[j], last_ref[j], cols), half_rows))
        for m, x in enumerate(tiles_from(folded)):
            out_ref[g, m * SUB : (m + 1) * SUB, :] = x

    def edges(side, g, first):
        for i in range(HB):
            j = first + i
            sums = []
            for h in range(HB):
                total = jnp.zeros((pairs, LANES), F32)
                for e in range(nnz):
                    here = columns_ref[e, g * SUB + j] == side * (blocks + HB) + h
                    total = total + jnp.where(here, stiff_ref[e, g, pl.ds(j, pairs, stride=SUB), :], 0.0)
                sums.append(total)
            x, y = sums
            left = jnp.concatenate([jnp.where(half_rows, x, swap(y)), jnp.where(half_rows, swap(x), y)], axis=0)
            high, low = split(left)
            edge_ref[side, i * 2 * NODE : i * 2 * NODE + NODE, :] = high
            edge_ref[side, i * 2 * NODE + NODE : (i + 1) * 2 * NODE, :] = low

    got[1].wait()
    spread(0)
    spread(1)
    got[5].wait()
    prepare(0)
    got[0].wait()
    edges(0, 0, 0)
    got[2].wait()
    got[3].wait()
    got[4].wait()
    cands = owners_ref.shape[0]
    owner_ids = lax.broadcasted_iota(jnp.int32, (peers, blocks), 0)
    before = jnp.zeros((peers, 1), F32)
    for k in range(cands):
        target = owners_ref[k : k + 1, :]
        hits = owner_ids == jnp.broadcast_to(target, (peers, blocks))
        places = jnp.where(hits, before + ranks(hits) - 1.0, 0.0)
        before = before + jnp.sum(hits.astype(F32), axis=1, keepdims=True)
        rank = jnp.sum(places, axis=0, keepdims=True)
        tools = peers // doms
        slot_ref[k : k + 1, :] = (target % tools * doms + target // tools) * stride + rank.astype(jnp.int32)

    def body(g, carry):
        pltpu.make_async_copy(stiff_hbm.at[:, g + 1], stiff_ref.at[:, g + 1], sems.at[6 + g]).wait()
        product(g)
        prepare(g + 1)
        spread(jnp.minimum(g + 2, groups - 1))
        fields(g)
        return carry

    lax.fori_loop(0, groups - 1, body, 0)
    product(groups - 1)
    inners = pltpu.make_async_copy(out_ref, out_hbm, out_sem)
    inners.start()
    fields(groups - 1)
    edges(1, groups - 1, SUB - HB)
    inners.wait()


def times(left, last, cols):
    even_count = left.shape[1] // NODE
    out = jnp.dot(left, jnp.concatenate(cols[:even_count], axis=0), preferred_element_type=F32)
    out = out[:NODE] + out[NODE:]
    if len(cols) > even_count:
        out = out + jnp.dot(last, jnp.concatenate([cols[-1], cols[-1]], axis=0), preferred_element_type=F32)
    return out


def contact_kernel(
    peers, capacity, stride, inner_hbm, slots_ref, rows_ref, field_ref, own_ref, edge_ref, out_hbm,
    slot_ref, inner_ref, out_ref, tall_ref, gram_ref, halo_ref, wide_ref, hold_ref, delta_ref, sems, out_sems,
):
    got = copies_of((slots_ref, inner_hbm), (slot_ref, inner_ref), sems)
    blocks = slot_ref.shape[1]
    groups = blocks // SUB
    pairs = NODE // 2
    half = left_half(pairs)
    full = left_half(NODE)
    row, place, angle = field_rows((SUB, LANES))
    scale = jnp.where(place, REACH, jnp.where(row == 3, TURN, jnp.where(angle, 3.0 * TURN, 1.0)))
    none = jnp.zeros((SUB, LANES), F32)
    tail = row == 7

    def tile_of(reach, phase, slip):
        turn = jnp.abs(phase - ((phase + ROUND) - ROUND)) - 0.25
        square = turn * turn
        wave = square + SINE[2] / SINE[3]
        wave = wave * square + SINE[1] / SINE[3]
        wave = wave * square + SINE[0] / SINE[3]
        return jnp.exp2(reach) * (wave * turn) * (2.0 + jnp.tanh(slip))

    def tiles(g):
        raws, slips = [], []
        for j in range(SUB):
            b = g * SUB + j
            tool = pair_fields(rows_ref[slot_ref[0, b]], rows_ref[slot_ref[1, b]]) * scale
            norm = LIFT - 0.5 * jnp.sum(jnp.where(place, tool * tool, 0.0), axis=0, keepdims=True)
            h, m, l = three(tool)
            nh, nm, nl = three(norm)
            ones = jnp.where(tail, 1.0, 0.0)
            hp, mp, lp = (jnp.where(place, v, 0.0) for v in (h, m, l))
            ha, ma, la = (jnp.where(angle, v, 0.0) for v in (h, m, l))
            reach = [hp + ones, mp + ones, hp + ones, jnp.where(tail, nh, lp), jnp.where(tail, nm, hp), jnp.where(tail, nl, mp)]
            right = jnp.concatenate(
                [jnp.concatenate(x, axis=0).astype(BF16) for x in (reach, [ha, ma, ha, la, ha, ma])], axis=1
            )
            raws.append(jnp.dot(field_ref[b][:, : 6 * SUB], right, preferred_element_type=F32))
            slips.append(ordered(row, h[7:8], m[7:8], l[7:8], "hmhlhm"))
            if j % 2:
                right = jnp.concatenate(
                    [jnp.concatenate([slips[j - 1], none], axis=1), jnp.concatenate([none, slips[j]], axis=1)], axis=0
                ).astype(BF16)
                slide = jnp.dot(field_ref[b - 1][:, 6 * SUB : 8 * SUB], right, preferred_element_type=F32)
                for i in range(2):
                    raw = raws[j - 1 + i]
                    high, low = split(tile_of(raw[:, :LANES], raw[:, LANES:], slide[:, i * LANES : (i + 1) * LANES]))
                    tall_ref[j - 1 + i, :NODE, :] = high
                    tall_ref[j - 1 + i, NODE:, :] = low

    def grams(g):
        for j in range(SUB):
            tall = tall_ref[j]
            gram = lax.dot_general(tall[:NODE], tall, (((1,), (1,)), ((), ())), preferred_element_type=F32)
            other = swap(gram)
            cross = other[:, :NODE]
            gram = gram + other + jnp.concatenate([cross, cross], axis=0).T
            gram_ref[j] = high_low(gram, full).astype(BF16)

    def out_copy(g):
        return pltpu.make_async_copy(out_ref.at[g], out_hbm.at[g], out_sems.at[g])

    def apply(g):
        folded = []
        for j in range(SUB):
            own = own_ref[g * SUB + j]
            out = jnp.dot(gram_ref[j], jnp.concatenate([own, own], axis=0), preferred_element_type=F32)
            folded.append(fold(out, half))
        for m, x in enumerate(tiles_from(folded)):
            spot = slice(m * SUB, (m + 1) * SUB)
            out_ref[g, spot, :] = inner_ref[g, spot, :] + x
        out_copy(g).start()

    share = 2 * HB * pairs // peers
    step = min(share, rows_ref.shape[1])
    for at in range(0, 2 * HB * pairs, step):
        q, r = at // share, at % share
        halo_ref[at : at + step, :] = rows_ref[q * stride + capacity + r // step][:step]
    for side in range(2):
        for h in range(HB):
            at = ((1 - side) * HB + h) * pairs
            even, odd = doubled(halo_ref[at : at + pairs, :], half)
            hold_ref[h, pl.ds(0, pairs, stride=2), :] = even
            hold_ref[h, pl.ds(1, pairs, stride=2), :] = odd
            wide_ref[side, h * NODE : (h + 1) * NODE, :] = high_low(hold_ref[h], full).astype(BF16)
        out = jnp.dot(edge_ref[side], wide_ref[side], preferred_element_type=F32)
        for i in range(HB):
            at = i * 2 * NODE
            delta_ref[side * HB + i] = fold(out[at : at + NODE] + out[at + NODE : at + 2 * NODE], half)
    got[0].wait()
    tiles(0)
    got[1].wait()
    for i in range(2 * HB):
        g, j = (0, i) if i < HB else (groups - 1, SUB - 2 * HB + i)
        spot = pl.ds(j, pairs, stride=SUB)
        inner_ref[g, spot, :] = inner_ref[g, spot, :] + delta_ref[i]

    def body(g, carry):
        grams(g - 1)
        apply(g - 1)
        tiles(g)
        return carry

    lax.fori_loop(1, groups, body, 0)
    grams(groups - 1)
    apply(groups - 1)
    for g in range(groups):
        out_copy(g).wait()


def per_device(records, tool_data, owners, local_seg, active, stiffness, columns, vectors):
    doms, tools = (lax.axis_size(axis) for axis in AXES)
    peers = doms * tools
    blocks, cands = owners.shape
    nnz = columns.shape[1]
    segs, width = tool_data.shape
    capacity = max(2, (3 * blocks * cands + 2 * peers - 1) // (2 * peers))
    groups = blocks // SUB
    pairs = NODE // 2
    chunks = width // LANES
    i32 = jnp.int32

    def shape(dims, dtype=F32):
        return jax.ShapeDtypeStruct(dims, dtype)

    def tiles_of(x, rows):
        lead = x.shape[:-2]
        n = len(lead)
        x = x.reshape(lead + (rows // SUB, SUB, x.shape[-1] // LANES, LANES))
        x = jnp.swapaxes(x, n + 1, n + 2)
        return x.reshape(lead + (rows // SUB, -1, LANES))

    vec = tiles_of(vectors, blocks)
    rec = tiles_of(records, blocks)
    stiff = tiles_of(jnp.swapaxes(stiffness, 0, 1), blocks)
    share = 2 * HB * pairs // peers
    stride = capacity + -(-share // chunks)

    def in_hbm(*arrays):
        return [pltpu.with_memory_space_constraint(x, pltpu.HBM) for x in arrays]

    send = pl.pallas_call(
        functools.partial(prep_kernel, peers, segs),
        out_shape=shape((peers * (1 + share), LANES)),
        in_specs=[HBM] * 3,
        out_specs=VMEM,
        scratch_shapes=[
            pltpu.VMEM((cands, blocks), i32),
            pltpu.VMEM((cands, blocks), i32),
            pltpu.VMEM(vec.shape[1:], F32),
            pltpu.VMEM(vec.shape[1:], F32),
            pltpu.VMEM((2 * HB * pairs, LANES), F32),
            pltpu.SemaphoreType.DMA((4,)),
        ],
        compiler_params=params(8),
        name="prep",
    )(*in_hbm(owners.T, local_seg.T, vec))

    members = AXES[::-1]
    wanted = lax.all_to_all(send.reshape(peers, 1 + share, 1, LANES), members, split_axis=0, concat_axis=0, tiled=True)
    wanted = wanted.reshape(peers * (1 + share), LANES)

    parts = pl.pallas_call(
        parts_kernel,
        out_shape=shape((segs, PARTS * width), BF16),
        in_specs=[HBM] * 2,
        out_specs=VMEM,
        scratch_shapes=[pltpu.VMEM(tool_data.shape, F32), pltpu.SemaphoreType.DMA((1,))],
        compiler_params=params(8),
        cost_estimate=pl.CostEstimate(flops=1 << 20, bytes_accessed=4 << 20, transcendentals=0),
        name="parts",
    )(*in_hbm(send, tool_data))

    rows_out = pl.pallas_call(
        functools.partial(rows_kernel, peers, capacity, stride),
        out_shape=shape((peers * stride * chunks, LANES)),
        in_specs=[VMEM] * 2,
        out_specs=VMEM,
        compiler_params=params(8),
        name="rows",
    )(wanted, parts)
    fetched = lax.all_to_all(
        rows_out.reshape(peers, stride, chunks, LANES), members, split_axis=0, concat_axis=0, tiled=True
    )

    wide = (blocks, NODE, LANES)
    left = (2 * NODE, nnz // 2 * 2 * NODE)
    inner, slot, own, fields, edges = pl.pallas_call(
        functools.partial(main_kernel, doms, peers, capacity, stride),
        out_shape=(
            pltpu.HBM(vec.shape, F32),
            shape((cands, blocks), i32),
            shape(wide, BF16),
            shape(wide, BF16),
            shape((2, HB * 2 * NODE, LANES), BF16),
        ),
        in_specs=[HBM] * 6,
        out_specs=(HBM,) + (VMEM,) * 4,
        scratch_shapes=[
            pltpu.SMEM((nnz, blocks), i32),
            pltpu.VMEM(vec.shape, F32),
            pltpu.VMEM(rec.shape, F32),
            pltpu.VMEM(active.shape, i32),
            pltpu.VMEM((cands, blocks), i32),
            pltpu.VMEM(stiff.shape, F32),
            pltpu.VMEM((blocks + 2 * HB, NODE, LANES), BF16),
            pltpu.VMEM((SUB,) + left, BF16),
            pltpu.VMEM((SUB, NODE, LANES), BF16),
            pltpu.VMEM(vec.shape, F32),
            pltpu.SemaphoreType.DMA((groups + 5,)),
            pltpu.SemaphoreType.DMA,
        ],
        compiler_params=params(20),
        cost_estimate=pl.CostEstimate(
            flops=6 * blocks * nnz * NODE * NODE * NVEC, bytes_accessed=24 << 20, transcendentals=0
        ),
        name="main",
    )(*in_hbm(columns.T, vec, rec, active, owners.T, stiff))

    out = pl.pallas_call(
        functools.partial(contact_kernel, peers, capacity, stride),
        out_shape=pltpu.HBM(vec.shape, F32),
        in_specs=[HBM] + [VMEM] * 5,
        out_specs=HBM,
        scratch_shapes=[
            pltpu.SMEM((cands, blocks), i32),
            pltpu.VMEM(vec.shape, F32),
            pltpu.VMEM(vec.shape, F32),
            pltpu.VMEM((SUB, 2 * NODE, LANES), BF16),
            pltpu.VMEM((SUB, NODE, LANES), BF16),
            pltpu.VMEM((2 * HB * pairs, LANES), F32),
            pltpu.VMEM((2, HB * NODE, LANES), BF16),
            pltpu.VMEM((HB, NODE, LANES), F32),
            pltpu.VMEM((2 * HB, pairs, LANES), F32),
            pltpu.SemaphoreType.DMA((2,)),
            pltpu.SemaphoreType.DMA((groups,)),
        ],
        compiler_params=params(16),
        cost_estimate=pl.CostEstimate(
            flops=80 * blocks * cands * NODE * NODE, bytes_accessed=4 << 20, transcendentals=2 * blocks * cands * NODE * NODE
        ),
        name="contact",
    )(*in_hbm(inner), slot, fetched.reshape(peers * stride, chunks, LANES), fields, own, edges)
    out = out.reshape(groups, pairs, SUB, LANES)
    return jnp.swapaxes(out, 1, 2).reshape(blocks, NODE * NVEC)


def solution(mesh):
    split_rows = P(AXES, None)
    return jax.shard_map(
        per_device,
        mesh=mesh,
        in_specs=(split_rows,) * 5 + (P(AXES, None, None),) + (split_rows,) * 2,
        out_specs=split_rows,
        check_vma=False,
    )
```

```python
import functools
import math

import jax
import jax.numpy as jnp
from jax import lax
from jax.experimental import pallas as pl
from jax.experimental.pallas import tpu as pltpu
from jax.sharding import PartitionSpec as P

NODE = 64
NVEC = 64
FIELDS = 8
HB = 2
LANES = 128
SUB = 8
AXES = ("dom", "tool")
TURN = 1.0 / (2.0 * math.pi)
REACH = math.sqrt(math.log2(math.e) / 4.0)
SHARE = math.sqrt(0.05)
FAR = -1e30
SINE = (6.283164044071425, -41.33714233428813, 81.34076747811504, -70.99341826772617)
LIFT = math.log2(-SINE[3] * SHARE * 0.5)
F32 = jnp.float32
BF16 = jnp.bfloat16
VMEM = pl.BlockSpec(memory_space=pltpu.VMEM)
SMEM = pl.BlockSpec(memory_space=pltpu.SMEM)
HBM = pl.BlockSpec(memory_space=pltpu.HBM)
ROUND = 1.5 * 2.0**23
PARTS = 3


def params(mib):
    return pltpu.CompilerParams(vmem_limit_bytes=mib << 20)


def left_half(rows):
    return lax.broadcasted_iota(jnp.int32, (rows, LANES), 1) < NODE


def swap(x):
    return pltpu.roll(x, NODE, 1)


def split(x):
    high = x.astype(BF16)
    return high, (x - high.astype(F32)).astype(BF16)


def three(x):
    high = x.astype(BF16).astype(F32)
    rest = x - high
    mid = rest.astype(BF16).astype(F32)
    return high, mid, rest - mid


def fold(out, half):
    pairs = NODE // 2
    even, odd = out[:pairs], out[pairs:]
    return jnp.where(half, even, odd) + swap(jnp.where(half, odd, even))


def flip(tiles):
    tiles = list(tiles)
    row = lax.broadcasted_iota(jnp.int32, (SUB, LANES), 0)
    for d in (4, 2, 1):
        keep = (row & d) == 0
        for i in range(SUB):
            if i & d:
                continue
            a, b = tiles[i], tiles[i + d]
            if 2 * d == SUB:
                moved = pltpu.roll(jnp.where(keep, b, a), d, 0)
                tiles[i], tiles[i + d] = jnp.where(keep, a, moved), jnp.where(keep, moved, b)
            else:
                tiles[i] = jnp.where(keep, a, pltpu.roll(b, d, 0))
                tiles[i + d] = jnp.where(keep, pltpu.roll(a, SUB - d, 0), b)
    return tiles


def flip_all(tiles):
    runs = [flip(tiles[i : i + SUB]) for i in range(0, len(tiles), SUB)]
    return [jnp.concatenate([run[j] for run in runs], axis=0) for j in range(SUB)]


def tiles_from(blocks):
    out = []
    for at in range(0, blocks[0].shape[0], SUB):
        out += flip([x[at : at + SUB] for x in blocks])
    return out


def doubled(x, half):
    other = swap(x)
    return jnp.where(half, x, other), jnp.where(half, other, x)


def high_low(x, half):
    return jnp.where(half, x, x - x.astype(BF16).astype(F32))


def copies_of(sources, targets, sems):
    made = [pltpu.make_async_copy(a, b, sems.at[i]) for i, (a, b) in enumerate(zip(sources, targets))]
    for copy in made:
        copy.start()
    return made


def pair_fields(x, y):
    quarter = left_half(x.shape[0])
    return jnp.concatenate([jnp.where(quarter, x, swap(y)), jnp.where(quarter, swap(x), y)], axis=0)


def field_rows(shape):
    row = lax.broadcasted_iota(jnp.int32, shape, 0)
    place = (row < 2) | (row == 4)
    return row, place, (row != 7) & ~place


def ranks(hits):
    n = hits.shape[1]
    upper = (
        lax.broadcasted_iota(jnp.int32, (n, n), 0) <= lax.broadcasted_iota(jnp.int32, (n, n), 1)
    ).astype(BF16)
    return jnp.dot(hits.astype(F32).astype(BF16), upper, preferred_element_type=F32)


def prep_kernel(segs, owners_hbm, seg_hbm, vec_hbm, send_hbm, owners_ref, seg_ref, row_ref, sems):
    got = copies_of((owners_hbm, seg_hbm), (owners_ref, seg_ref), sems)
    cands = owners_ref.shape[0]
    groups, runs = vec_hbm.shape[:2]
    sent = []
    for h in range(2 * HB):
        g, j = (0, h) if h < HB else (groups - 1, SUB - 2 * HB + h)
        sent.append(
            pltpu.make_async_copy(
                vec_hbm.at[g, :, :, j], send_hbm.at[pl.ds(h * runs, runs), pl.ds(1, vec_hbm.shape[2])], sems.at[2 + h]
            )
        )
        sent[-1].start()
    for copy in got:
        copy.wait()
    wanted = [owners_ref[k : k + 1, :] * segs + seg_ref[k : k + 1, :] for k in range(cands)]
    wanted = jnp.concatenate(wanted, axis=1).astype(F32)
    row_ref[...] = jnp.broadcast_to(wanted.reshape(1, 1, 1, LANES), row_ref.shape)
    sent.append(pltpu.make_async_copy(row_ref, send_hbm.at[:, pl.ds(0, 1)], sems.at[2 + 2 * HB]))
    sent[-1].start()
    for copy in sent:
        copy.wait()


def rows_kernel(peers, capacity, stride, got_ref, part_ref, out_ref):
    segs, width = part_ref.shape[0], part_ref.shape[1] // PARTS
    chunks = width // LANES
    share = got_ref.shape[0] // peers - 1
    doms, tools = (lax.axis_size(axis) for axis in AXES)
    at_dom, at_tool = (lax.axis_index(axis) for axis in AXES)
    seg = lax.broadcasted_iota(jnp.int32, (peers, segs), 1).astype(F32)
    local = got_ref[pl.ds(0, peers, stride=1 + share), :] - ((at_dom * tools + at_tool) * segs).astype(F32)
    hits = (local >= 0.0) & (local < float(segs))
    rank = ranks(hits)
    picks = []
    for s in range(capacity):
        row = jnp.sum(jnp.where(hits & (rank == s + 1.0), local, 0.0), axis=1, keepdims=True)
        picks.append((seg == row).astype(F32).astype(BF16))
    picks = jnp.concatenate(picks, axis=0)
    for c in range(0, chunks, 2):
        got = None
        for p in range(PARTS):
            at = p * width + c * LANES
            term = jnp.dot(picks, part_ref[:, at : at + 2 * LANES], preferred_element_type=F32)
            got = term if got is None else got + term
        for s in range(capacity):
            for i in range(2):
                out_ref[pl.ds(s * chunks + c + i, peers, stride=stride * chunks), :] = got[
                    s * peers : (s + 1) * peers, i * LANES : (i + 1) * LANES
                ]
    me = at_tool * doms + at_dom
    peer = lax.broadcasted_iota(jnp.int32, (peers, LANES), 0)
    for r in range(share):
        edge = got_ref[pl.ds(1 + r, peers, stride=1 + share), :]
        following = jnp.where(
            peer < peers - doms, pltpu.roll(edge, peers - doms, 0), pltpu.roll(edge, peers - doms - 1, 0)
        )
        following = jnp.where(peer == peers - 1, 0.0, following)
        previous = jnp.where(peer >= doms, pltpu.roll(edge, doms, 0), pltpu.roll(edge, doms + 1, 0))
        previous = jnp.where(peer == 0, 0.0, previous)
        out_ref[pl.ds(capacity * chunks + r, peers, stride=stride * chunks), :] = jnp.where(
            me < peers // 2, following, previous
        )


def parts_kernel(after_prep, tool_hbm, part_ref, tool_ref, sems):
    copies_of((tool_hbm,), (tool_ref,), sems)[0].wait()
    width = tool_ref.shape[1]
    for p, part in enumerate(three(tool_ref[...])):
        part_ref[:, p * width : (p + 1) * width] = part.astype(BF16)


def ordered(row, h, m, l, order):
    out = jnp.zeros(row.shape, F32)
    for value, name in ((h, "h"), (m, "m"), (l, "l")):
        for i, at in enumerate(order):
            if at == name:
                out = jnp.where(row == i, value, out)
    return out


def main_kernel(
    doms, peers, capacity, stride,
    columns_hbm, vec_hbm, rec_hbm, act_hbm, owners_hbm, stiff_hbm, out_hbm, slot_ref, own_ref, field_ref, edge_ref,
    columns_ref, vec_ref, rec_ref, act_ref, owners_ref, stiff_ref,
    wide_ref, left_ref, last_ref, out_ref, sems, out_sem,
):
    nnz, groups = stiff_ref.shape[:2]
    blocks = groups * SUB
    pairs = NODE // 2
    even_count = nnz // 2 * 2
    half = left_half(SUB)
    half_rows = left_half(pairs)
    got = copies_of(
        (columns_hbm, vec_hbm, rec_hbm, act_hbm, owners_hbm) + tuple(stiff_hbm.at[:, g] for g in range(groups)),
        (columns_ref, vec_ref, rec_ref, act_ref, owners_ref) + tuple(stiff_ref.at[:, g] for g in range(groups)),
        sems,
    )
    zero = jnp.zeros((NODE, LANES), BF16)
    for h in range(HB):
        wide_ref[h] = zero
        wide_ref[blocks + HB + h] = zero

    def tile(m):
        return pl.ds(m * SUB, SUB)

    def spread(g):
        for at in range(0, pairs, 2 * SUB):
            evens, odds = [], []
            for m in range(at, at + 2 * SUB):
                even, odd = doubled(vec_ref[g, tile(m), :], half)
                evens.append(high_low(even, half))
                odds.append(high_low(odd, half))
            for q, values in enumerate((evens, odds)):
                for j, x in enumerate(flip_all(values)):
                    own_ref[g * SUB + j, q * pairs + at : q * pairs + at + 2 * SUB, :] = x.astype(BF16)
            mixed = [x for both in zip(evens, odds) for x in both]
            for j, x in enumerate(flip_all(mixed)):
                wide_ref[HB + g * SUB + j, 2 * at : 2 * at + 4 * SUB, :] = x.astype(BF16)

    row, place, _ = field_rows((SUB, LANES))
    scale = jnp.where(place, REACH, 1.0)
    lane = lax.broadcasted_iota(jnp.int32, (SUB, LANES), 1)
    turn = lane // NODE * NODE + lane % pairs * 2 + lane % NODE // pairs

    def evens_first(x):
        return jnp.take_along_axis(x, turn, axis=1, mode="promise_in_bounds")

    def fields(g):
        for j in range(0, SUB, 2):
            x = rec_ref[g, pl.ds(j, FIELDS // 2, stride=SUB), :]
            y = rec_ref[g, pl.ds(j + 1, FIELDS // 2, stride=SUB), :]
            part = pair_fields(x, y) * scale
            norm = -0.5 * jnp.sum(jnp.where(place, part * part, 0.0), axis=0, keepdims=True)
            at = g * SUB + j
            flags = jnp.concatenate([act_ref[pl.ds(at, 1), :], act_ref[pl.ds(at + 1, 1), :]], axis=1)
            norm = jnp.where(flags == 0, FAR, norm)
            h, m, l = three(evens_first(part))
            norms = three(evens_first(jnp.broadcast_to(norm, (SUB, LANES))))
            slip = ordered(row, h[7:8], m[7:8], l[7:8], "hhmhlm")
            lists = [jnp.where(row == 7, n, v) for n, v in zip(norms + (1.0, 1.0, 1.0), (h, h, m, h, l, m))]
            more = jnp.zeros((LANES - 8 * SUB, LANES), F32)
            stack = jnp.concatenate(lists + [slip, swap(slip), more], axis=0).T.astype(BF16)
            field_ref[at] = stack[:NODE]
            field_ref[at + 1] = stack[NODE:]

    def prepare(g):
        for at in range(0, pairs, 2 * SUB):
            for e in range(0, nnz, 2):
                evens, odds = [], []
                for m in range(at, at + 2 * SUB):
                    x = stiff_ref[e, g, tile(m), :]
                    if e < even_count:
                        y = stiff_ref[e + 1, g, tile(m), :]
                        evens.append(jnp.where(half, x, swap(y)))
                        odds.append(jnp.where(half, swap(x), y))
                    else:
                        even, odd = doubled(x, half)
                        evens.append(high_low(even, half))
                        odds.append(high_low(odd, half))
                for q, values in enumerate((evens, odds)):
                    rows = slice(q * pairs + at, q * pairs + at + 2 * SUB)
                    for j, x in enumerate(flip_all(values)):
                        if e < even_count:
                            high, low = split(x)
                            cols = slice(e * NODE, (e + 2) * NODE)
                            left_ref[j, rows, cols] = high
                            left_ref[j, NODE + rows.start : NODE + rows.stop, cols] = low
                        else:
                            last_ref[j, rows, :] = x.astype(BF16)

    def product(g):
        folded = []
        for j in range(SUB):
            cols = [wide_ref[columns_ref[e, g * SUB + j]] for e in range(nnz)]
            folded.append(fold(times(left_ref[j], last_ref[j], cols), half_rows))
        for m, x in enumerate(tiles_from(folded)):
            out_ref[g, m * SUB : (m + 1) * SUB, :] = x

    def edges(side, g, first):
        for i in range(HB):
            j = first + i
            sums = []
            for h in range(HB):
                total = jnp.zeros((pairs, LANES), F32)
                for e in range(nnz):
                    here = columns_ref[e, g * SUB + j] == side * (blocks + HB) + h
                    total = total + jnp.where(here, stiff_ref[e, g, pl.ds(j, pairs, stride=SUB), :], 0.0)
                sums.append(total)
            x, y = sums
            left = jnp.concatenate([jnp.where(half_rows, x, swap(y)), jnp.where(half_rows, swap(x), y)], axis=0)
            high, low = split(left)
            edge_ref[side, i * 2 * NODE : i * 2 * NODE + NODE, :] = high
            edge_ref[side, i * 2 * NODE + NODE : (i + 1) * 2 * NODE, :] = low

    got[1].wait()
    spread(0)
    spread(1)
    got[5].wait()
    prepare(0)
    got[0].wait()
    edges(0, 0, 0)
    got[2].wait()
    got[3].wait()
    got[4].wait()
    cands = owners_ref.shape[0]
    owner_ids = lax.broadcasted_iota(jnp.int32, (peers, blocks), 0)
    before = jnp.zeros((peers, 1), F32)
    for k in range(cands):
        target = owners_ref[k : k + 1, :]
        hits = owner_ids == jnp.broadcast_to(target, (peers, blocks))
        places = jnp.where(hits, before + ranks(hits) - 1.0, 0.0)
        before = before + jnp.sum(hits.astype(F32), axis=1, keepdims=True)
        rank = jnp.sum(places, axis=0, keepdims=True)
        tools = peers // doms
        slot_ref[k : k + 1, :] = (target % tools * doms + target // tools) * stride + rank.astype(jnp.int32)

    def body(g, carry):
        pltpu.make_async_copy(stiff_hbm.at[:, g + 1], stiff_ref.at[:, g + 1], sems.at[6 + g]).wait()
        product(g)
        prepare(g + 1)
        spread(jnp.minimum(g + 2, groups - 1))
        fields(g)
        return carry

    lax.fori_loop(0, groups - 1, body, 0)
    product(groups - 1)
    inners = pltpu.make_async_copy(out_ref, out_hbm, out_sem)
    inners.start()
    fields(groups - 1)
    edges(1, groups - 1, SUB - HB)
    inners.wait()


def times(left, last, cols):
    even_count = left.shape[1] // NODE
    out = jnp.dot(left, jnp.concatenate(cols[:even_count], axis=0), preferred_element_type=F32)
    out = out[:NODE] + out[NODE:]
    if len(cols) > even_count:
        out = out + jnp.dot(last, jnp.concatenate([cols[-1], cols[-1]], axis=0), preferred_element_type=F32)
    return out


def contact_kernel(
    peers, capacity, stride, inner_hbm, slots_ref, rows_ref, field_ref, own_ref, edge_ref, out_hbm,
    slot_ref, inner_ref, out_ref, tall_ref, gram_ref, halo_ref, wide_ref, hold_ref, delta_ref, sems, out_sems,
):
    got = copies_of((slots_ref, inner_hbm), (slot_ref, inner_ref), sems)
    blocks = slot_ref.shape[1]
    groups = blocks // SUB
    pairs = NODE // 2
    half = left_half(pairs)
    full = left_half(NODE)
    row, place, angle = field_rows((SUB, LANES))
    scale = jnp.where(place, REACH, jnp.where(row == 3, TURN, jnp.where(angle, 3.0 * TURN, 1.0)))
    none = jnp.zeros((SUB, LANES), F32)
    tail = row == 7

    def tile_of(reach, phase, slip):
        turn = jnp.abs(phase - ((phase + ROUND) - ROUND)) - 0.25
        square = turn * turn
        wave = square + SINE[2] / SINE[3]
        wave = wave * square + SINE[1] / SINE[3]
        wave = wave * square + SINE[0] / SINE[3]
        return jnp.exp2(reach) * (wave * turn) * (2.0 + jnp.tanh(slip))

    def tiles(g):
        raws, slips = [], []
        for j in range(SUB):
            b = g * SUB + j
            tool = pair_fields(rows_ref[slot_ref[0, b]], rows_ref[slot_ref[1, b]]) * scale
            norm = LIFT - 0.5 * jnp.sum(jnp.where(place, tool * tool, 0.0), axis=0, keepdims=True)
            h, m, l = three(tool)
            nh, nm, nl = three(norm)
            ones = jnp.where(tail, 1.0, 0.0)
            hp, mp, lp = (jnp.where(place, v, 0.0) for v in (h, m, l))
            ha, ma, la = (jnp.where(angle, v, 0.0) for v in (h, m, l))
            reach = [hp + ones, mp + ones, hp + ones, jnp.where(tail, nh, lp), jnp.where(tail, nm, hp), jnp.where(tail, nl, mp)]
            right = jnp.concatenate(
                [jnp.concatenate(x, axis=0).astype(BF16) for x in (reach, [ha, ma, ha, la, ha, ma])], axis=1
            )
            raws.append(jnp.dot(field_ref[b][:, : 6 * SUB], right, preferred_element_type=F32))
            slips.append(ordered(row, h[7:8], m[7:8], l[7:8], "hmhlhm"))
            if j % 2:
                right = jnp.concatenate(
                    [jnp.concatenate([slips[j - 1], none], axis=1), jnp.concatenate([none, slips[j]], axis=1)], axis=0
                ).astype(BF16)
                slide = jnp.dot(field_ref[b - 1][:, 6 * SUB : 8 * SUB], right, preferred_element_type=F32)
                for i in range(2):
                    raw = raws[j - 1 + i]
                    high, low = split(tile_of(raw[:, :LANES], raw[:, LANES:], slide[:, i * LANES : (i + 1) * LANES]))
                    tall_ref[j - 1 + i, :NODE, :] = high
                    tall_ref[j - 1 + i, NODE:, :] = low

    def grams(g):
        for j in range(SUB):
            tall = tall_ref[j]
            gram = lax.dot_general(tall, tall, (((1,), (1,)), ((), ())), preferred_element_type=F32)
            gram = gram[:NODE] + gram[NODE:]
            gram_ref[j] = high_low(gram + swap(gram), full).astype(BF16)

    def out_copy(g):
        return pltpu.make_async_copy(out_ref.at[g], out_hbm.at[g], out_sems.at[g])

    def apply(g):
        folded = []
        for j in range(SUB):
            own = own_ref[g * SUB + j]
            out = jnp.dot(gram_ref[j], jnp.concatenate([own, own], axis=0), preferred_element_type=F32)
            folded.append(fold(out, half))
        for m, x in enumerate(tiles_from(folded)):
            spot = slice(m * SUB, (m + 1) * SUB)
            out_ref[g, spot, :] = inner_ref[g, spot, :] + x
        out_copy(g).start()

    share = 2 * HB * pairs // peers
    step = min(share, rows_ref.shape[1])
    for at in range(0, 2 * HB * pairs, step):
        q, r = at // share, at % share
        halo_ref[at : at + step, :] = rows_ref[q * stride + capacity + r // step][:step]
    for side in range(2):
        for h in range(HB):
            at = ((1 - side) * HB + h) * pairs
            even, odd = doubled(halo_ref[at : at + pairs, :], half)
            hold_ref[h, pl.ds(0, pairs, stride=2), :] = even
            hold_ref[h, pl.ds(1, pairs, stride=2), :] = odd
            wide_ref[side, h * NODE : (h + 1) * NODE, :] = high_low(hold_ref[h], full).astype(BF16)
        out = jnp.dot(edge_ref[side], wide_ref[side], preferred_element_type=F32)
        for i in range(HB):
            at = i * 2 * NODE
            delta_ref[side * HB + i] = fold(out[at : at + NODE] + out[at + NODE : at + 2 * NODE], half)
    got[0].wait()
    tiles(0)
    grams(0)
    tiles(1)
    got[1].wait()
    for i in range(2 * HB):
        g, j = (0, i) if i < HB else (groups - 1, SUB - 2 * HB + i)
        spot = pl.ds(j, pairs, stride=SUB)
        inner_ref[g, spot, :] = inner_ref[g, spot, :] + delta_ref[i]

    def body(g, carry):
        apply(g - 2)
        grams(g - 1)
        tiles(g)
        return carry

    lax.fori_loop(2, groups, body, 0)
    apply(groups - 2)
    grams(groups - 1)
    apply(groups - 1)
    for g in range(groups):
        out_copy(g).wait()


def per_device(records, tool_data, owners, local_seg, active, stiffness, columns, vectors):
    doms, tools = (lax.axis_size(axis) for axis in AXES)
    peers = doms * tools
    blocks, cands = owners.shape
    nnz = columns.shape[1]
    segs, width = tool_data.shape
    capacity = max(2, (3 * blocks * cands + 2 * peers - 1) // (2 * peers))
    groups = blocks // SUB
    pairs = NODE // 2
    chunks = width // LANES
    i32 = jnp.int32

    def shape(dims, dtype=F32):
        return jax.ShapeDtypeStruct(dims, dtype)

    def tiles_of(x, rows):
        lead = x.shape[:-2]
        n = len(lead)
        x = x.reshape(lead + (rows // SUB, SUB, x.shape[-1] // LANES, LANES))
        x = jnp.swapaxes(x, n + 1, n + 2)
        return x.reshape(lead + (rows // SUB, -1, LANES))

    vec = tiles_of(vectors, blocks)
    rec = tiles_of(records, blocks)
    stiff = tiles_of(jnp.swapaxes(stiffness, 0, 1), blocks)
    share = 2 * HB * pairs // peers
    stride = capacity + -(-share // chunks)

    def in_hbm(*arrays):
        return [pltpu.with_memory_space_constraint(x, pltpu.HBM) for x in arrays]

    rows_of = vec.reshape(groups, pairs // share, share, SUB, 1, LANES)
    send = pl.pallas_call(
        functools.partial(prep_kernel, segs),
        out_shape=pltpu.HBM((peers, 1 + share, 1, LANES), F32),
        in_specs=[HBM] * 3,
        out_specs=HBM,
        scratch_shapes=[
            pltpu.VMEM((cands, blocks), i32),
            pltpu.VMEM((cands, blocks), i32),
            pltpu.VMEM((peers, 1, 1, LANES), F32),
            pltpu.SemaphoreType.DMA((3 + 2 * HB,)),
        ],
        compiler_params=params(8),
        name="prep",
    )(*in_hbm(owners.T, local_seg.T, rows_of))

    members = AXES[::-1]
    wanted = lax.all_to_all(send, members, split_axis=0, concat_axis=0, tiled=True)
    wanted = wanted.reshape(peers * (1 + share), LANES)

    parts = pl.pallas_call(
        parts_kernel,
        out_shape=shape((segs, PARTS * width), BF16),
        in_specs=[HBM] * 2,
        out_specs=VMEM,
        scratch_shapes=[pltpu.VMEM(tool_data.shape, F32), pltpu.SemaphoreType.DMA((1,))],
        compiler_params=params(8),
        cost_estimate=pl.CostEstimate(flops=1 << 20, bytes_accessed=4 << 20, transcendentals=0),
        name="parts",
    )(*in_hbm(send, tool_data))

    rows_out = pl.pallas_call(
        functools.partial(rows_kernel, peers, capacity, stride),
        out_shape=shape((peers * stride * chunks, LANES)),
        in_specs=[VMEM] * 2,
        out_specs=VMEM,
        compiler_params=params(8),
        name="rows",
    )(wanted, parts)
    fetched = lax.all_to_all(
        rows_out.reshape(peers, stride, chunks, LANES), members, split_axis=0, concat_axis=0, tiled=True
    )

    wide = (blocks, NODE, LANES)
    left = (2 * NODE, nnz // 2 * 2 * NODE)
    inner, slot, own, fields, edges = pl.pallas_call(
        functools.partial(main_kernel, doms, peers, capacity, stride),
        out_shape=(
            pltpu.HBM(vec.shape, F32),
            shape((cands, blocks), i32),
            shape(wide, BF16),
            shape(wide, BF16),
            shape((2, HB * 2 * NODE, LANES), BF16),
        ),
        in_specs=[HBM] * 6,
        out_specs=(HBM,) + (VMEM,) * 4,
        scratch_shapes=[
            pltpu.SMEM((nnz, blocks), i32),
            pltpu.VMEM(vec.shape, F32),
            pltpu.VMEM(rec.shape, F32),
            pltpu.VMEM(active.shape, i32),
            pltpu.VMEM((cands, blocks), i32),
            pltpu.VMEM(stiff.shape, F32),
            pltpu.VMEM((blocks + 2 * HB, NODE, LANES), BF16),
            pltpu.VMEM((SUB,) + left, BF16),
            pltpu.VMEM((SUB, NODE, LANES), BF16),
            pltpu.VMEM(vec.shape, F32),
            pltpu.SemaphoreType.DMA((groups + 5,)),
            pltpu.SemaphoreType.DMA,
        ],
        compiler_params=params(20),
        cost_estimate=pl.CostEstimate(
            flops=6 * blocks * nnz * NODE * NODE * NVEC, bytes_accessed=24 << 20, transcendentals=0
        ),
        name="main",
    )(*in_hbm(columns.T, vec, rec, active, owners.T, stiff))

    out = pl.pallas_call(
        functools.partial(contact_kernel, peers, capacity, stride),
        out_shape=pltpu.HBM(vec.shape, F32),
        in_specs=[HBM] + [VMEM] * 5,
        out_specs=HBM,
        scratch_shapes=[
            pltpu.SMEM((cands, blocks), i32),
            pltpu.VMEM(vec.shape, F32),
            pltpu.VMEM(vec.shape, F32),
            pltpu.VMEM((SUB, 2 * NODE, LANES), BF16),
            pltpu.VMEM((SUB, NODE, LANES), BF16),
            pltpu.VMEM((2 * HB * pairs, LANES), F32),
            pltpu.VMEM((2, HB * NODE, LANES), BF16),
            pltpu.VMEM((HB, NODE, LANES), F32),
            pltpu.VMEM((2 * HB, pairs, LANES), F32),
            pltpu.SemaphoreType.DMA((2,)),
            pltpu.SemaphoreType.DMA((groups,)),
        ],
        compiler_params=params(16),
        cost_estimate=pl.CostEstimate(
            flops=80 * blocks * cands * NODE * NODE, bytes_accessed=4 << 20, transcendentals=2 * blocks * cands * NODE * NODE
        ),
        name="contact",
    )(*in_hbm(inner), slot, fetched.reshape(peers * stride, chunks, LANES), fields, own, edges)
    out = out.reshape(groups, pairs, SUB, LANES)
    return jnp.swapaxes(out, 1, 2).reshape(blocks, NODE * NVEC)


def solution(mesh):
    split_rows = P(AXES, None)
    return jax.shard_map(
        per_device,
        mesh=mesh,
        in_specs=(split_rows,) * 5 + (P(AXES, None, None),) + (split_rows,) * 2,
        out_specs=split_rows,
        check_vma=False,
    )
```

```python
import functools
import math

import jax
import jax.numpy as jnp
from jax import lax
from jax.experimental import pallas as pl
from jax.experimental.pallas import tpu as pltpu
from jax.sharding import PartitionSpec as P

NODE = 64
NVEC = 64
FIELDS = 8
HB = 2
LANES = 128
SUB = 8
AXES = ("dom", "tool")
TURN = 1.0 / (2.0 * math.pi)
REACH = math.sqrt(math.log2(math.e) / 4.0)
SHARE = math.sqrt(0.05)
FAR = -1e30
SINE = (6.283164044071425, -41.33714233428813, 81.34076747811504, -70.99341826772617)
LIFT = math.log2(-SINE[3] * SHARE * 0.5)
F32 = jnp.float32
BF16 = jnp.bfloat16
VMEM = pl.BlockSpec(memory_space=pltpu.VMEM)
SMEM = pl.BlockSpec(memory_space=pltpu.SMEM)
HBM = pl.BlockSpec(memory_space=pltpu.HBM)
ROUND = 1.5 * 2.0**23
PARTS = 3


def params(mib):
    return pltpu.CompilerParams(vmem_limit_bytes=mib << 20)


def left_half(rows):
    return lax.broadcasted_iota(jnp.int32, (rows, LANES), 1) < NODE


def swap(x):
    return pltpu.roll(x, NODE, 1)


def split(x):
    high = x.astype(BF16)
    return high, (x - high.astype(F32)).astype(BF16)


def three(x):
    high = x.astype(BF16).astype(F32)
    rest = x - high
    mid = rest.astype(BF16).astype(F32)
    return high, mid, rest - mid


def fold(out, half):
    pairs = NODE // 2
    even, odd = out[:pairs], out[pairs:]
    return jnp.where(half, even, odd) + swap(jnp.where(half, odd, even))


def flip(tiles):
    tiles = list(tiles)
    row = lax.broadcasted_iota(jnp.int32, (SUB, LANES), 0)
    for d in (4, 2, 1):
        keep = (row & d) == 0
        for i in range(SUB):
            if i & d:
                continue
            a, b = tiles[i], tiles[i + d]
            if 2 * d == SUB:
                moved = pltpu.roll(jnp.where(keep, b, a), d, 0)
                tiles[i], tiles[i + d] = jnp.where(keep, a, moved), jnp.where(keep, moved, b)
            else:
                tiles[i] = jnp.where(keep, a, pltpu.roll(b, d, 0))
                tiles[i + d] = jnp.where(keep, pltpu.roll(a, SUB - d, 0), b)
    return tiles


def flip_all(tiles):
    runs = [flip(tiles[i : i + SUB]) for i in range(0, len(tiles), SUB)]
    return [jnp.concatenate([run[j] for run in runs], axis=0) for j in range(SUB)]


def tiles_from(blocks):
    out = []
    for at in range(0, blocks[0].shape[0], SUB):
        out += flip([x[at : at + SUB] for x in blocks])
    return out


def doubled(x, half):
    other = swap(x)
    return jnp.where(half, x, other), jnp.where(half, other, x)


def high_low(x, half):
    return jnp.where(half, x, x - x.astype(BF16).astype(F32))


def copies_of(sources, targets, sems):
    made = [pltpu.make_async_copy(a, b, sems.at[i]) for i, (a, b) in enumerate(zip(sources, targets))]
    for copy in made:
        copy.start()
    return made


def pair_fields(x, y):
    quarter = left_half(x.shape[0])
    return jnp.concatenate([jnp.where(quarter, x, swap(y)), jnp.where(quarter, swap(x), y)], axis=0)


def field_rows(shape):
    row = lax.broadcasted_iota(jnp.int32, shape, 0)
    place = (row < 2) | (row == 4)
    return row, place, (row != 7) & ~place


def ranks(hits):
    n = hits.shape[1]
    upper = (
        lax.broadcasted_iota(jnp.int32, (n, n), 0) <= lax.broadcasted_iota(jnp.int32, (n, n), 1)
    ).astype(BF16)
    return jnp.dot(hits.astype(F32).astype(BF16), upper, preferred_element_type=F32)


def prep_kernel(
    peers, segs, owners_hbm, seg_hbm, vec_hbm, send_ref, owners_ref, seg_ref, first_ref, last_ref, edge_ref, sems
):
    last = vec_hbm.shape[0] - 1
    got = copies_of(
        (owners_hbm, seg_hbm, vec_hbm.at[0], vec_hbm.at[last]), (owners_ref, seg_ref, first_ref, last_ref), sems
    )
    cands = owners_ref.shape[0]
    pairs = NODE // 2
    share = 2 * HB * pairs // peers
    got[0].wait()
    got[1].wait()
    wanted = [owners_ref[k : k + 1, :] * segs + seg_ref[k : k + 1, :] for k in range(cands)]
    wanted = jnp.concatenate(wanted, axis=1).astype(F32)
    send_ref[pl.ds(0, peers, stride=1 + share), :] = jnp.broadcast_to(wanted, (peers, LANES))
    got[2].wait()
    got[3].wait()
    for h in range(HB):
        edge_ref[h * pairs : (h + 1) * pairs, :] = first_ref[pl.ds(h, pairs, stride=SUB), :]
        edge_ref[(HB + h) * pairs : (HB + h + 1) * pairs, :] = last_ref[pl.ds(SUB - HB + h, pairs, stride=SUB), :]
    for r in range(share):
        send_ref[pl.ds(1 + r, peers, stride=1 + share), :] = edge_ref[pl.ds(r, peers, stride=share), :]


def rows_kernel(peers, capacity, stride, got_ref, part_ref, out_ref):
    segs, width = part_ref.shape[0], part_ref.shape[1] // PARTS
    chunks = width // LANES
    share = got_ref.shape[0] // peers - 1
    doms, tools = (lax.axis_size(axis) for axis in AXES)
    at_dom, at_tool = (lax.axis_index(axis) for axis in AXES)
    seg = lax.broadcasted_iota(jnp.int32, (peers, segs), 1).astype(F32)
    local = got_ref[pl.ds(0, peers, stride=1 + share), :] - ((at_dom * tools + at_tool) * segs).astype(F32)
    hits = (local >= 0.0) & (local < float(segs))
    rank = ranks(hits)
    picks = []
    for s in range(capacity):
        row = jnp.sum(jnp.where(hits & (rank == s + 1.0), local, 0.0), axis=1, keepdims=True)
        picks.append((seg == row).astype(F32).astype(BF16))
    picks = jnp.concatenate(picks, axis=0)
    for c in range(0, chunks, 2):
        got = None
        for p in range(PARTS):
            at = p * width + c * LANES
            term = jnp.dot(picks, part_ref[:, at : at + 2 * LANES], preferred_element_type=F32)
            got = term if got is None else got + term
        for s in range(capacity):
            for i in range(2):
                out_ref[pl.ds(s * chunks + c + i, peers, stride=stride * chunks), :] = got[
                    s * peers : (s + 1) * peers, i * LANES : (i + 1) * LANES
                ]
    me = at_tool * doms + at_dom
    peer = lax.broadcasted_iota(jnp.int32, (peers, LANES), 0)
    for r in range(share):
        edge = got_ref[pl.ds(1 + r, peers, stride=1 + share), :]
        following = jnp.where(
            peer < peers - doms, pltpu.roll(edge, peers - doms, 0), pltpu.roll(edge, peers - doms - 1, 0)
        )
        following = jnp.where(peer == peers - 1, 0.0, following)
        previous = jnp.where(peer >= doms, pltpu.roll(edge, doms, 0), pltpu.roll(edge, doms + 1, 0))
        previous = jnp.where(peer == 0, 0.0, previous)
        out_ref[pl.ds(capacity * chunks + r, peers, stride=stride * chunks), :] = jnp.where(
            me < peers // 2, following, previous
        )


def parts_kernel(after_prep, tool_hbm, part_ref, tool_ref, sems):
    copies_of((tool_hbm,), (tool_ref,), sems)[0].wait()
    width = tool_ref.shape[1]
    for p, part in enumerate(three(tool_ref[...])):
        part_ref[:, p * width : (p + 1) * width] = part.astype(BF16)


def ordered(row, h, m, l, order):
    out = jnp.zeros(row.shape, F32)
    for value, name in ((h, "h"), (m, "m"), (l, "l")):
        for i, at in enumerate(order):
            if at == name:
                out = jnp.where(row == i, value, out)
    return out


def main_kernel(
    doms, peers, capacity, stride,
    columns_hbm, vec_hbm, rec_hbm, act_hbm, owners_hbm, stiff_hbm, out_hbm, slot_ref, own_ref, field_ref, edge_ref,
    columns_ref, vec_ref, rec_ref, act_ref, owners_ref, stiff_ref,
    wide_ref, left_ref, last_ref, out_ref, sems, out_sem,
):
    nnz, groups = stiff_ref.shape[:2]
    blocks = groups * SUB
    pairs = NODE // 2
    even_count = nnz // 2 * 2
    half = left_half(SUB)
    half_rows = left_half(pairs)
    got = copies_of(
        (columns_hbm, vec_hbm, rec_hbm, act_hbm, owners_hbm) + tuple(stiff_hbm.at[:, g] for g in range(groups)),
        (columns_ref, vec_ref, rec_ref, act_ref, owners_ref) + tuple(stiff_ref.at[:, g] for g in range(groups)),
        sems,
    )
    zero = jnp.zeros((NODE, LANES), BF16)
    for h in range(HB):
        wide_ref[h] = zero
        wide_ref[blocks + HB + h] = zero

    def tile(m):
        return pl.ds(m * SUB, SUB)

    def spread(g):
        for at in range(0, pairs, 2 * SUB):
            evens, odds = [], []
            for m in range(at, at + 2 * SUB):
                even, odd = doubled(vec_ref[g, tile(m), :], half)
                evens.append(high_low(even, half))
                odds.append(high_low(odd, half))
            for q, values in enumerate((evens, odds)):
                for j, x in enumerate(flip_all(values)):
                    own_ref[g * SUB + j, q * pairs + at : q * pairs + at + 2 * SUB, :] = x.astype(BF16)
            mixed = [x for both in zip(evens, odds) for x in both]
            for j, x in enumerate(flip_all(mixed)):
                wide_ref[HB + g * SUB + j, 2 * at : 2 * at + 4 * SUB, :] = x.astype(BF16)

    row, place, _ = field_rows((SUB, LANES))
    scale = jnp.where(place, REACH, 1.0)
    lane = lax.broadcasted_iota(jnp.int32, (SUB, LANES), 1)
    turn = lane // NODE * NODE + lane % pairs * 2 + lane % NODE // pairs

    def evens_first(x):
        return jnp.take_along_axis(x, turn, axis=1, mode="promise_in_bounds")

    def fields(g):
        for j in range(0, SUB, 2):
            x = rec_ref[g, pl.ds(j, FIELDS // 2, stride=SUB), :]
            y = rec_ref[g, pl.ds(j + 1, FIELDS // 2, stride=SUB), :]
            part = pair_fields(x, y) * scale
            norm = -0.5 * jnp.sum(jnp.where(place, part * part, 0.0), axis=0, keepdims=True)
            at = g * SUB + j
            flags = jnp.concatenate([act_ref[pl.ds(at, 1), :], act_ref[pl.ds(at + 1, 1), :]], axis=1)
            norm = jnp.where(flags == 0, FAR, norm)
            h, m, l = three(evens_first(part))
            norms = three(evens_first(jnp.broadcast_to(norm, (SUB, LANES))))
            slip = ordered(row, h[7:8], m[7:8], l[7:8], "hhmhlm")
            lists = [jnp.where(row == 7, n, v) for n, v in zip(norms + (1.0, 1.0, 1.0), (h, h, m, h, l, m))]
            more = jnp.zeros((LANES - 8 * SUB, LANES), F32)
            stack = jnp.concatenate(lists + [slip, swap(slip), more], axis=0).T.astype(BF16)
            field_ref[at] = stack[:NODE]
            field_ref[at + 1] = stack[NODE:]

    def prepare(g):
        for at in range(0, pairs, 2 * SUB):
            for e in range(0, nnz, 2):
                evens, odds = [], []
                for m in range(at, at + 2 * SUB):
                    x = stiff_ref[e, g, tile(m), :]
                    if e < even_count:
                        y = stiff_ref[e + 1, g, tile(m), :]
                        evens.append(jnp.where(half, x, swap(y)))
                        odds.append(jnp.where(half, swap(x), y))
                    else:
                        even, odd = doubled(x, half)
                        evens.append(high_low(even, half))
                        odds.append(high_low(odd, half))
                for q, values in enumerate((evens, odds)):
                    rows = slice(q * pairs + at, q * pairs + at + 2 * SUB)
                    for j, x in enumerate(flip_all(values)):
                        if e < even_count:
                            high, low = split(x)
                            cols = slice(e * NODE, (e + 2) * NODE)
                            left_ref[j, rows, cols] = high
                            left_ref[j, NODE + rows.start : NODE + rows.stop, cols] = low
                        else:
                            last_ref[j, rows, :] = x.astype(BF16)

    def product(g):
        folded = []
        for j in range(SUB):
            cols = [wide_ref[columns_ref[e, g * SUB + j]] for e in range(nnz)]
            folded.append(fold(times(left_ref[j], last_ref[j], cols), half_rows))
        for m, x in enumerate(tiles_from(folded)):
            out_ref[g, m * SUB : (m + 1) * SUB, :] = x

    def edges(side, g, first):
        for i in range(HB):
            j = first + i
            sums = []
            for h in range(HB):
                total = jnp.zeros((pairs, LANES), F32)
                for e in range(nnz):
                    here = columns_ref[e, g * SUB + j] == side * (blocks + HB) + h
                    total = total + jnp.where(here, stiff_ref[e, g, pl.ds(j, pairs, stride=SUB), :], 0.0)
                sums.append(total)
            x, y = sums
            left = jnp.concatenate([jnp.where(half_rows, x, swap(y)), jnp.where(half_rows, swap(x), y)], axis=0)
            high, low = split(left)
            edge_ref[side, i * 2 * NODE : i * 2 * NODE + NODE, :] = high
            edge_ref[side, i * 2 * NODE + NODE : (i + 1) * 2 * NODE, :] = low

    got[1].wait()
    spread(0)
    spread(1)
    got[5].wait()
    prepare(0)
    got[0].wait()
    edges(0, 0, 0)
    got[2].wait()
    got[3].wait()
    got[4].wait()
    cands = owners_ref.shape[0]
    owner_ids = lax.broadcasted_iota(jnp.int32, (peers, blocks), 0)
    before = jnp.zeros((peers, 1), F32)
    for k in range(cands):
        target = owners_ref[k : k + 1, :]
        hits = owner_ids == jnp.broadcast_to(target, (peers, blocks))
        places = jnp.where(hits, before + ranks(hits) - 1.0, 0.0)
        before = before + jnp.sum(hits.astype(F32), axis=1, keepdims=True)
        rank = jnp.sum(places, axis=0, keepdims=True)
        tools = peers // doms
        slot_ref[k : k + 1, :] = (target % tools * doms + target // tools) * stride + rank.astype(jnp.int32)

    def body(g, carry):
        pltpu.make_async_copy(stiff_hbm.at[:, g + 1], stiff_ref.at[:, g + 1], sems.at[6 + g]).wait()
        product(g)
        prepare(g + 1)
        spread(jnp.minimum(g + 2, groups - 1))
        fields(g)
        return carry

    lax.fori_loop(0, groups - 1, body, 0)
    product(groups - 1)
    inners = pltpu.make_async_copy(out_ref, out_hbm, out_sem)
    inners.start()
    fields(groups - 1)
    edges(1, groups - 1, SUB - HB)
    inners.wait()


def times(left, last, cols):
    even_count = left.shape[1] // NODE
    out = jnp.dot(left, jnp.concatenate(cols[:even_count], axis=0), preferred_element_type=F32)
    out = out[:NODE] + out[NODE:]
    if len(cols) > even_count:
        out = out + jnp.dot(last, jnp.concatenate([cols[-1], cols[-1]], axis=0), preferred_element_type=F32)
    return out


def contact_kernel(
    peers, capacity, stride, inner_hbm, slots_ref, rows_ref, field_ref, own_ref, edge_ref, out_hbm,
    slot_ref, inner_ref, out_ref, tall_ref, gram_ref, fold_ref, halo_ref, wide_ref, hold_ref, delta_ref, sems, out_sems,
):
    got = copies_of((slots_ref, inner_hbm), (slot_ref, inner_ref), sems)
    blocks = slot_ref.shape[1]
    groups = blocks // SUB
    pairs = NODE // 2
    half = left_half(pairs)
    full = left_half(NODE)
    row, place, angle = field_rows((SUB, LANES))
    scale = jnp.where(place, REACH, jnp.where(row == 3, TURN, jnp.where(angle, 3.0 * TURN, 1.0)))
    none = jnp.zeros((SUB, LANES), F32)
    tail = row == 7

    def tile_of(reach, phase, slip):
        turn = jnp.abs(phase - ((phase + ROUND) - ROUND)) - 0.25
        square = turn * turn
        wave = square + SINE[2] / SINE[3]
        wave = wave * square + SINE[1] / SINE[3]
        wave = wave * square + SINE[0] / SINE[3]
        return jnp.exp2(reach) * (wave * turn) * (2.0 + jnp.tanh(slip))

    def tiles(g, j):
        raws, slips = [], []
        for i in range(2):
            b = g * SUB + j + i
            tool = pair_fields(rows_ref[slot_ref[0, b]], rows_ref[slot_ref[1, b]]) * scale
            norm = LIFT - 0.5 * jnp.sum(jnp.where(place, tool * tool, 0.0), axis=0, keepdims=True)
            h, m, l = three(tool)
            nh, nm, nl = three(norm)
            ones = jnp.where(tail, 1.0, 0.0)
            hp, mp, lp = (jnp.where(place, v, 0.0) for v in (h, m, l))
            ha, ma, la = (jnp.where(angle, v, 0.0) for v in (h, m, l))
            reach = [hp + ones, mp + ones, hp + ones, jnp.where(tail, nh, lp), jnp.where(tail, nm, hp), jnp.where(tail, nl, mp)]
            right = jnp.concatenate(
                [jnp.concatenate(x, axis=0).astype(BF16) for x in (reach, [ha, ma, ha, la, ha, ma])], axis=1
            )
            raws.append(jnp.dot(field_ref[b][:, : 6 * SUB], right, preferred_element_type=F32))
            slips.append(ordered(row, h[7:8], m[7:8], l[7:8], "hmhlhm"))
        right = jnp.concatenate(
            [jnp.concatenate([slips[0], none], axis=1), jnp.concatenate([none, slips[1]], axis=1)], axis=0
        ).astype(BF16)
        slide = jnp.dot(field_ref[g * SUB + j][:, 6 * SUB : 8 * SUB], right, preferred_element_type=F32)
        for i, raw in enumerate(raws):
            high, low = split(tile_of(raw[:, :LANES], raw[:, LANES:], slide[:, i * LANES : (i + 1) * LANES]))
            tall_ref[j + i, :NODE, :] = high
            tall_ref[j + i, NODE:, :] = low

    def gram(j):
        tall = tall_ref[j]
        out = lax.dot_general(tall, tall, (((1,), (1,)), ((), ())), preferred_element_type=F32)
        out = out[:NODE] + out[NODE:]
        gram_ref[j] = high_low(out + swap(out), full).astype(BF16)

    def apply(g, j):
        own = own_ref[g * SUB + j]
        out = jnp.dot(gram_ref[j], jnp.concatenate([own, own], axis=0), preferred_element_type=F32)
        fold_ref[j] = fold(out, half)

    def out_copy(g):
        return pltpu.make_async_copy(out_ref.at[g], out_hbm.at[g], out_sems.at[g])

    def emit(g):
        for m, x in enumerate(tiles_from([fold_ref[j] for j in range(SUB)])):
            spot = slice(m * SUB, (m + 1) * SUB)
            out_ref[g, spot, :] = inner_ref[g, spot, :] + x
        out_copy(g).start()

    def stages(g, first=0, last=3):
        if last >= 3:
            emit(g - 3)
        for j in range(0, SUB, 2):
            for i in range(j, j + 2):
                if first <= 2 <= last:
                    apply(g - 2, i)
                if first <= 1 <= last:
                    gram(i)
            if first == 0:
                tiles(g, j)

    share = 2 * HB * pairs // peers
    step = min(share, rows_ref.shape[1])
    for at in range(0, 2 * HB * pairs, step):
        q, r = at // share, at % share
        halo_ref[at : at + step, :] = rows_ref[q * stride + capacity + r // step][:step]
    for side in range(2):
        for h in range(HB):
            at = ((1 - side) * HB + h) * pairs
            even, odd = doubled(halo_ref[at : at + pairs, :], half)
            hold_ref[h, pl.ds(0, pairs, stride=2), :] = even
            hold_ref[h, pl.ds(1, pairs, stride=2), :] = odd
            wide_ref[side, h * NODE : (h + 1) * NODE, :] = high_low(hold_ref[h], full).astype(BF16)
        out = jnp.dot(edge_ref[side], wide_ref[side], preferred_element_type=F32)
        for i in range(HB):
            at = i * 2 * NODE
            delta_ref[side * HB + i] = fold(out[at : at + NODE] + out[at + NODE : at + 2 * NODE], half)
    got[0].wait()
    for g in range(3):
        stages(g, last=g)
    got[1].wait()
    for i in range(2 * HB):
        g, j = (0, i) if i < HB else (groups - 1, SUB - 2 * HB + i)
        spot = pl.ds(j, pairs, stride=SUB)
        inner_ref[g, spot, :] = inner_ref[g, spot, :] + delta_ref[i]

    def body(g, carry):
        stages(g)
        return carry

    lax.fori_loop(3, groups, body, 0)
    for k in range(1, 4):
        stages(groups - 1 + k, first=k)
    for g in range(groups):
        out_copy(g).wait()


def per_device(records, tool_data, owners, local_seg, active, stiffness, columns, vectors):
    doms, tools = (lax.axis_size(axis) for axis in AXES)
    peers = doms * tools
    blocks, cands = owners.shape
    nnz = columns.shape[1]
    segs, width = tool_data.shape
    capacity = max(2, (3 * blocks * cands + 2 * peers - 1) // (2 * peers))
    groups = blocks // SUB
    pairs = NODE // 2
    chunks = width // LANES
    i32 = jnp.int32

    def shape(dims, dtype=F32):
        return jax.ShapeDtypeStruct(dims, dtype)

    def tiles_of(x, rows):
        lead = x.shape[:-2]
        n = len(lead)
        x = x.reshape(lead + (rows // SUB, SUB, x.shape[-1] // LANES, LANES))
        x = jnp.swapaxes(x, n + 1, n + 2)
        return x.reshape(lead + (rows // SUB, -1, LANES))

    vec = tiles_of(vectors, blocks)
    rec = tiles_of(records, blocks)
    stiff = tiles_of(jnp.swapaxes(stiffness, 0, 1), blocks)
    share = 2 * HB * pairs // peers
    stride = capacity + -(-share // chunks)

    def in_hbm(*arrays):
        return [pltpu.with_memory_space_constraint(x, pltpu.HBM) for x in arrays]

    send = pl.pallas_call(
        functools.partial(prep_kernel, peers, segs),
        out_shape=shape((peers * (1 + share), LANES)),
        in_specs=[HBM] * 3,
        out_specs=VMEM,
        scratch_shapes=[
            pltpu.VMEM((cands, blocks), i32),
            pltpu.VMEM((cands, blocks), i32),
            pltpu.VMEM(vec.shape[1:], F32),
            pltpu.VMEM(vec.shape[1:], F32),
            pltpu.VMEM((2 * HB * pairs, LANES), F32),
            pltpu.SemaphoreType.DMA((4,)),
        ],
        compiler_params=params(8),
        name="prep",
    )(*in_hbm(owners.T, local_seg.T, vec))

    members = AXES[::-1]
    wanted = lax.all_to_all(send.reshape(peers, 1 + share, 1, LANES), members, split_axis=0, concat_axis=0, tiled=True)
    wanted = wanted.reshape(peers * (1 + share), LANES)

    parts = pl.pallas_call(
        parts_kernel,
        out_shape=shape((segs, PARTS * width), BF16),
        in_specs=[HBM] * 2,
        out_specs=VMEM,
        scratch_shapes=[pltpu.VMEM(tool_data.shape, F32), pltpu.SemaphoreType.DMA((1,))],
        compiler_params=params(8),
        cost_estimate=pl.CostEstimate(flops=1 << 20, bytes_accessed=4 << 20, transcendentals=0),
        name="parts",
    )(*in_hbm(send, tool_data))

    rows_out = pl.pallas_call(
        functools.partial(rows_kernel, peers, capacity, stride),
        out_shape=shape((peers * stride * chunks, LANES)),
        in_specs=[VMEM] * 2,
        out_specs=VMEM,
        compiler_params=params(8),
        name="rows",
    )(wanted, parts)
    fetched = lax.all_to_all(
        rows_out.reshape(peers, stride, chunks, LANES), members, split_axis=0, concat_axis=0, tiled=True
    )

    wide = (blocks, NODE, LANES)
    left = (2 * NODE, nnz // 2 * 2 * NODE)
    inner, slot, own, fields, edges = pl.pallas_call(
        functools.partial(main_kernel, doms, peers, capacity, stride),
        out_shape=(
            pltpu.HBM(vec.shape, F32),
            shape((cands, blocks), i32),
            shape(wide, BF16),
            shape(wide, BF16),
            shape((2, HB * 2 * NODE, LANES), BF16),
        ),
        in_specs=[HBM] * 6,
        out_specs=(HBM,) + (VMEM,) * 4,
        scratch_shapes=[
            pltpu.SMEM((nnz, blocks), i32),
            pltpu.VMEM(vec.shape, F32),
            pltpu.VMEM(rec.shape, F32),
            pltpu.VMEM(active.shape, i32),
            pltpu.VMEM((cands, blocks), i32),
            pltpu.VMEM(stiff.shape, F32),
            pltpu.VMEM((blocks + 2 * HB, NODE, LANES), BF16),
            pltpu.VMEM((SUB,) + left, BF16),
            pltpu.VMEM((SUB, NODE, LANES), BF16),
            pltpu.VMEM(vec.shape, F32),
            pltpu.SemaphoreType.DMA((groups + 5,)),
            pltpu.SemaphoreType.DMA,
        ],
        compiler_params=params(20),
        cost_estimate=pl.CostEstimate(
            flops=6 * blocks * nnz * NODE * NODE * NVEC, bytes_accessed=24 << 20, transcendentals=0
        ),
        name="main",
    )(*in_hbm(columns.T, vec, rec, active, owners.T, stiff))

    out = pl.pallas_call(
        functools.partial(contact_kernel, peers, capacity, stride),
        out_shape=pltpu.HBM(vec.shape, F32),
        in_specs=[HBM] + [VMEM] * 5,
        out_specs=HBM,
        scratch_shapes=[
            pltpu.SMEM((cands, blocks), i32),
            pltpu.VMEM(vec.shape, F32),
            pltpu.VMEM(vec.shape, F32),
            pltpu.VMEM((SUB, 2 * NODE, LANES), BF16),
            pltpu.VMEM((SUB, NODE, LANES), BF16),
            pltpu.VMEM((SUB, pairs, LANES), F32),
            pltpu.VMEM((2 * HB * pairs, LANES), F32),
            pltpu.VMEM((2, HB * NODE, LANES), BF16),
            pltpu.VMEM((HB, NODE, LANES), F32),
            pltpu.VMEM((2 * HB, pairs, LANES), F32),
            pltpu.SemaphoreType.DMA((2,)),
            pltpu.SemaphoreType.DMA((groups,)),
        ],
        compiler_params=params(16),
        cost_estimate=pl.CostEstimate(
            flops=80 * blocks * cands * NODE * NODE, bytes_accessed=4 << 20, transcendentals=2 * blocks * cands * NODE * NODE
        ),
        name="contact",
    )(*in_hbm(inner), slot, fetched.reshape(peers * stride, chunks, LANES), fields, own, edges)
    out = out.reshape(groups, pairs, SUB, LANES)
    return jnp.swapaxes(out, 1, 2).reshape(blocks, NODE * NVEC)


def solution(mesh):
    split_rows = P(AXES, None)
    return jax.shard_map(
        per_device,
        mesh=mesh,
        in_specs=(split_rows,) * 5 + (P(AXES, None, None),) + (split_rows,) * 2,
        out_specs=split_rows,
        check_vma=False,
    )
```

```python
import functools
import math

import jax
import jax.numpy as jnp
from jax import lax
from jax.experimental import pallas as pl
from jax.experimental.pallas import tpu as pltpu
from jax.sharding import PartitionSpec as P

NODE = 64
NVEC = 64
FIELDS = 8
HB = 2
LANES = 128
SUB = 8
AXES = ("dom", "tool")
TURN = 1.0 / (2.0 * math.pi)
REACH = math.sqrt(math.log2(math.e) / 4.0)
SHARE = math.sqrt(0.05)
FAR = -1e30
SINE = (6.283164044071425, -41.33714233428813, 81.34076747811504, -70.99341826772617)
LIFT = math.log2(-SINE[3] * SHARE * 0.5)
F32 = jnp.float32
BF16 = jnp.bfloat16
VMEM = pl.BlockSpec(memory_space=pltpu.VMEM)
SMEM = pl.BlockSpec(memory_space=pltpu.SMEM)
HBM = pl.BlockSpec(memory_space=pltpu.HBM)
ROUND = 1.5 * 2.0**23
PARTS = 3


def params(mib):
    return pltpu.CompilerParams(vmem_limit_bytes=mib << 20)


def left_half(rows):
    return lax.broadcasted_iota(jnp.int32, (rows, LANES), 1) < NODE


def swap(x):
    return pltpu.roll(x, NODE, 1)


def split(x):
    high = x.astype(BF16)
    return high, (x - high.astype(F32)).astype(BF16)


def three(x):
    high = x.astype(BF16).astype(F32)
    rest = x - high
    mid = rest.astype(BF16).astype(F32)
    return high, mid, rest - mid


def fold(out, half):
    pairs = NODE // 2
    even, odd = out[:pairs], out[pairs:]
    return jnp.where(half, even, odd) + swap(jnp.where(half, odd, even))


def flip(tiles):
    tiles = list(tiles)
    row = lax.broadcasted_iota(jnp.int32, (SUB, LANES), 0)
    for d in (4, 2, 1):
        keep = (row & d) == 0
        for i in range(SUB):
            if i & d:
                continue
            a, b = tiles[i], tiles[i + d]
            if 2 * d == SUB:
                moved = pltpu.roll(jnp.where(keep, b, a), d, 0)
                tiles[i], tiles[i + d] = jnp.where(keep, a, moved), jnp.where(keep, moved, b)
            else:
                tiles[i] = jnp.where(keep, a, pltpu.roll(b, d, 0))
                tiles[i + d] = jnp.where(keep, pltpu.roll(a, SUB - d, 0), b)
    return tiles


def flip_all(tiles):
    runs = [flip(tiles[i : i + SUB]) for i in range(0, len(tiles), SUB)]
    return [jnp.concatenate([run[j] for run in runs], axis=0) for j in range(SUB)]


def tiles_from(blocks):
    out = []
    for at in range(0, blocks[0].shape[0], SUB):
        out += flip([x[at : at + SUB] for x in blocks])
    return out


def doubled(x, half):
    other = swap(x)
    return jnp.where(half, x, other), jnp.where(half, other, x)


def high_low(x, half):
    return jnp.where(half, x, x - x.astype(BF16).astype(F32))


def copies_of(sources, targets, sems):
    made = [pltpu.make_async_copy(a, b, sems.at[i]) for i, (a, b) in enumerate(zip(sources, targets))]
    for copy in made:
        copy.start()
    return made


def pair_fields(x, y):
    quarter = left_half(x.shape[0])
    return jnp.concatenate([jnp.where(quarter, x, swap(y)), jnp.where(quarter, swap(x), y)], axis=0)


def field_rows(shape):
    row = lax.broadcasted_iota(jnp.int32, shape, 0)
    place = (row < 2) | (row == 4)
    return row, place, (row != 7) & ~place


def ranks(hits):
    n = hits.shape[1]
    upper = (
        lax.broadcasted_iota(jnp.int32, (n, n), 0) <= lax.broadcasted_iota(jnp.int32, (n, n), 1)
    ).astype(BF16)
    return jnp.dot(hits.astype(F32).astype(BF16), upper, preferred_element_type=F32)


def prep_kernel(
    peers, segs, owners_hbm, seg_hbm, vec_hbm, send_ref, owners_ref, seg_ref, first_ref, last_ref, edge_ref, sems
):
    last = vec_hbm.shape[0] - 1
    got = copies_of(
        (owners_hbm, seg_hbm, vec_hbm.at[0], vec_hbm.at[last]), (owners_ref, seg_ref, first_ref, last_ref), sems
    )
    cands = owners_ref.shape[0]
    pairs = NODE // 2
    share = 2 * HB * pairs // peers
    got[0].wait()
    got[1].wait()
    wanted = [owners_ref[k : k + 1, :] * segs + seg_ref[k : k + 1, :] for k in range(cands)]
    wanted = jnp.concatenate(wanted, axis=1).astype(F32)
    send_ref[pl.ds(0, peers, stride=1 + share), :] = jnp.broadcast_to(wanted, (peers, LANES))
    got[2].wait()
    got[3].wait()
    for h in range(HB):
        edge_ref[h * pairs : (h + 1) * pairs, :] = first_ref[pl.ds(h, pairs, stride=SUB), :]
        edge_ref[(HB + h) * pairs : (HB + h + 1) * pairs, :] = last_ref[pl.ds(SUB - HB + h, pairs, stride=SUB), :]
    for r in range(share):
        send_ref[pl.ds(1 + r, peers, stride=1 + share), :] = edge_ref[pl.ds(r, peers, stride=share), :]


def rows_kernel(peers, capacity, stride, got_ref, part_ref, out_ref):
    segs, width = part_ref.shape[0], part_ref.shape[1] // PARTS
    chunks = width // LANES
    share = got_ref.shape[0] // peers - 1
    doms, tools = (lax.axis_size(axis) for axis in AXES)
    at_dom, at_tool = (lax.axis_index(axis) for axis in AXES)
    seg = lax.broadcasted_iota(jnp.int32, (peers, segs), 1).astype(F32)
    local = got_ref[pl.ds(0, peers, stride=1 + share), :] - ((at_dom * tools + at_tool) * segs).astype(F32)
    hits = (local >= 0.0) & (local < float(segs))
    rank = ranks(hits)
    picks = []
    for s in range(capacity):
        row = jnp.sum(jnp.where(hits & (rank == s + 1.0), local, 0.0), axis=1, keepdims=True)
        picks.append((seg == row).astype(F32).astype(BF16))
    picks = jnp.concatenate(picks, axis=0)
    for c in range(0, chunks, 2):
        got = None
        for p in range(PARTS):
            at = p * width + c * LANES
            term = jnp.dot(picks, part_ref[:, at : at + 2 * LANES], preferred_element_type=F32)
            got = term if got is None else got + term
        for s in range(capacity):
            for i in range(2):
                out_ref[pl.ds(s * chunks + c + i, peers, stride=stride * chunks), :] = got[
                    s * peers : (s + 1) * peers, i * LANES : (i + 1) * LANES
                ]
    me = at_tool * doms + at_dom
    peer = lax.broadcasted_iota(jnp.int32, (peers, LANES), 0)
    for r in range(share):
        edge = got_ref[pl.ds(1 + r, peers, stride=1 + share), :]
        following = jnp.where(
            peer < peers - doms, pltpu.roll(edge, peers - doms, 0), pltpu.roll(edge, peers - doms - 1, 0)
        )
        following = jnp.where(peer == peers - 1, 0.0, following)
        previous = jnp.where(peer >= doms, pltpu.roll(edge, doms, 0), pltpu.roll(edge, doms + 1, 0))
        previous = jnp.where(peer == 0, 0.0, previous)
        out_ref[pl.ds(capacity * chunks + r, peers, stride=stride * chunks), :] = jnp.where(
            me < peers // 2, following, previous
        )


def parts_kernel(after_prep, tool_hbm, part_ref, tool_ref, sems):
    copies_of((tool_hbm,), (tool_ref,), sems)[0].wait()
    width = tool_ref.shape[1]
    for p, part in enumerate(three(tool_ref[...])):
        part_ref[:, p * width : (p + 1) * width] = part.astype(BF16)


def ordered(row, h, m, l, order):
    out = jnp.zeros(row.shape, F32)
    for value, name in ((h, "h"), (m, "m"), (l, "l")):
        for i, at in enumerate(order):
            if at == name:
                out = jnp.where(row == i, value, out)
    return out


def main_kernel(
    doms, peers, capacity, stride,
    columns_hbm, vec_hbm, rec_hbm, act_hbm, owners_hbm, stiff_hbm, out_hbm, slot_ref, own_ref, field_ref, edge_ref,
    columns_ref, vec_ref, rec_ref, act_ref, owners_ref, stiff_ref,
    wide_ref, left_ref, last_ref, out_ref, sems, out_sem,
):
    nnz, groups = stiff_ref.shape[:2]
    blocks = groups * SUB
    pairs = NODE // 2
    even_count = nnz // 2 * 2
    half = left_half(SUB)
    half_rows = left_half(pairs)
    got = copies_of(
        (columns_hbm, vec_hbm, rec_hbm, act_hbm, owners_hbm) + tuple(stiff_hbm.at[:, g] for g in range(groups)),
        (columns_ref, vec_ref, rec_ref, act_ref, owners_ref) + tuple(stiff_ref.at[:, g] for g in range(groups)),
        sems,
    )
    zero = jnp.zeros((NODE, LANES), BF16)
    for h in range(HB):
        wide_ref[h] = zero
        wide_ref[blocks + HB + h] = zero

    def tile(m):
        return pl.ds(m * SUB, SUB)

    def spread(g):
        for at in range(0, pairs, 2 * SUB):
            evens, odds = [], []
            for m in range(at, at + 2 * SUB):
                even, odd = doubled(vec_ref[g, tile(m), :], half)
                evens.append(high_low(even, half))
                odds.append(high_low(odd, half))
            for q, values in enumerate((evens, odds)):
                for j, x in enumerate(flip_all(values)):
                    own_ref[g * SUB + j, q * pairs + at : q * pairs + at + 2 * SUB, :] = x.astype(BF16)
            mixed = [x for both in zip(evens, odds) for x in both]
            for j, x in enumerate(flip_all(mixed)):
                wide_ref[HB + g * SUB + j, 2 * at : 2 * at + 4 * SUB, :] = x.astype(BF16)

    row, place, _ = field_rows((SUB, LANES))
    scale = jnp.where(place, REACH, 1.0)
    lane = lax.broadcasted_iota(jnp.int32, (SUB, LANES), 1)
    turn = lane // NODE * NODE + lane % pairs * 2 + lane % NODE // pairs

    def evens_first(x):
        return jnp.take_along_axis(x, turn, axis=1, mode="promise_in_bounds")

    def fields(g):
        for j in range(0, SUB, 2):
            x = rec_ref[g, pl.ds(j, FIELDS // 2, stride=SUB), :]
            y = rec_ref[g, pl.ds(j + 1, FIELDS // 2, stride=SUB), :]
            part = pair_fields(x, y) * scale
            norm = -0.5 * jnp.sum(jnp.where(place, part * part, 0.0), axis=0, keepdims=True)
            at = g * SUB + j
            flags = jnp.concatenate([act_ref[pl.ds(at, 1), :], act_ref[pl.ds(at + 1, 1), :]], axis=1)
            norm = jnp.where(flags == 0, FAR, norm)
            h, m, l = three(evens_first(part))
            norms = three(evens_first(jnp.broadcast_to(norm, (SUB, LANES))))
            slip = ordered(row, h[7:8], m[7:8], l[7:8], "hhmhlm")
            lists = [jnp.where(row == 7, n, v) for n, v in zip(norms + (1.0, 1.0, 1.0), (h, h, m, h, l, m))]
            more = jnp.zeros((LANES - 8 * SUB, LANES), F32)
            stack = jnp.concatenate(lists + [slip, swap(slip), more], axis=0).T.astype(BF16)
            field_ref[at] = stack[:NODE]
            field_ref[at + 1] = stack[NODE:]

    def prepare(g):
        for at in range(0, pairs, 2 * SUB):
            for e in range(0, nnz, 2):
                evens, odds = [], []
                for m in range(at, at + 2 * SUB):
                    x = stiff_ref[e, g, tile(m), :]
                    if e < even_count:
                        y = stiff_ref[e + 1, g, tile(m), :]
                        evens.append(jnp.where(half, x, swap(y)))
                        odds.append(jnp.where(half, swap(x), y))
                    else:
                        even, odd = doubled(x, half)
                        evens.append(high_low(even, half))
                        odds.append(high_low(odd, half))
                for q, values in enumerate((evens, odds)):
                    rows = slice(q * pairs + at, q * pairs + at + 2 * SUB)
                    for j, x in enumerate(flip_all(values)):
                        if e < even_count:
                            high, low = split(x)
                            cols = slice(e * NODE, (e + 2) * NODE)
                            left_ref[j, rows, cols] = high
                            left_ref[j, NODE + rows.start : NODE + rows.stop, cols] = low
                        else:
                            last_ref[j, rows, :] = x.astype(BF16)

    def product(g):
        folded = []
        for j in range(SUB):
            cols = [wide_ref[columns_ref[e, g * SUB + j]] for e in range(nnz)]
            folded.append(fold(times(left_ref[j], last_ref[j], cols), half_rows))
        for m, x in enumerate(tiles_from(folded)):
            out_ref[g, m * SUB : (m + 1) * SUB, :] = x

    def edges(side, g, first):
        for i in range(HB):
            j = first + i
            sums = []
            for h in range(HB):
                total = jnp.zeros((pairs, LANES), F32)
                for e in range(nnz):
                    here = columns_ref[e, g * SUB + j] == side * (blocks + HB) + h
                    total = total + jnp.where(here, stiff_ref[e, g, pl.ds(j, pairs, stride=SUB), :], 0.0)
                sums.append(total)
            x, y = sums
            left = jnp.concatenate([jnp.where(half_rows, x, swap(y)), jnp.where(half_rows, swap(x), y)], axis=0)
            high, low = split(left)
            edge_ref[side, i * 2 * NODE : i * 2 * NODE + NODE, :] = high
            edge_ref[side, i * 2 * NODE + NODE : (i + 1) * 2 * NODE, :] = low

    got[1].wait()
    spread(0)
    spread(1)
    got[5].wait()
    prepare(0)
    got[0].wait()
    edges(0, 0, 0)
    got[2].wait()
    got[3].wait()
    got[4].wait()
    cands = owners_ref.shape[0]
    owner_ids = lax.broadcasted_iota(jnp.int32, (peers, blocks), 0)
    before = jnp.zeros((peers, 1), F32)
    for k in range(cands):
        target = owners_ref[k : k + 1, :]
        hits = owner_ids == jnp.broadcast_to(target, (peers, blocks))
        places = jnp.where(hits, before + ranks(hits) - 1.0, 0.0)
        before = before + jnp.sum(hits.astype(F32), axis=1, keepdims=True)
        rank = jnp.sum(places, axis=0, keepdims=True)
        tools = peers // doms
        slot_ref[k : k + 1, :] = (target % tools * doms + target // tools) * stride + rank.astype(jnp.int32)

    def body(g, carry):
        pltpu.make_async_copy(stiff_hbm.at[:, g + 1], stiff_ref.at[:, g + 1], sems.at[6 + g]).wait()
        product(g)
        prepare(g + 1)
        spread(jnp.minimum(g + 2, groups - 1))
        fields(g)
        return carry

    lax.fori_loop(0, groups - 1, body, 0)
    product(groups - 1)
    inners = pltpu.make_async_copy(out_ref, out_hbm, out_sem)
    inners.start()
    fields(groups - 1)
    edges(1, groups - 1, SUB - HB)
    inners.wait()


def times(left, last, cols):
    even_count = left.shape[1] // NODE
    out = jnp.dot(left, jnp.concatenate(cols[:even_count], axis=0), preferred_element_type=F32)
    out = out[:NODE] + out[NODE:]
    if len(cols) > even_count:
        out = out + jnp.dot(last, jnp.concatenate([cols[-1], cols[-1]], axis=0), preferred_element_type=F32)
    return out


def contact_kernel(
    peers, capacity, stride, inner_hbm, slots_ref, rows_ref, field_ref, own_ref, edge_ref, out_hbm,
    slot_ref, inner_ref, out_ref, tall_ref, gram_ref, fold_ref, halo_ref, wide_ref, hold_ref, delta_ref, sems, out_sems,
):
    got = copies_of((slots_ref, inner_hbm), (slot_ref, inner_ref), sems)
    blocks = slot_ref.shape[1]
    groups = blocks // SUB
    pairs = NODE // 2
    half = left_half(pairs)
    full = left_half(NODE)
    row, place, angle = field_rows((SUB, LANES))
    scale = jnp.where(place, REACH, jnp.where(row == 3, TURN, jnp.where(angle, 3.0 * TURN, 1.0)))
    none = jnp.zeros((SUB, LANES), F32)
    tail = row == 7

    def tile_of(reach, phase, slip):
        turn = jnp.abs(phase - ((phase + ROUND) - ROUND)) - 0.25
        square = turn * turn
        wave = square + SINE[2] / SINE[3]
        wave = wave * square + SINE[1] / SINE[3]
        wave = wave * square + SINE[0] / SINE[3]
        return jnp.exp2(reach) * (wave * turn) * (2.0 + jnp.tanh(slip))

    def sums(g, j):
        raws, slips = [], []
        for i in range(2):
            b = g * SUB + j + i
            tool = pair_fields(rows_ref[slot_ref[0, b]], rows_ref[slot_ref[1, b]]) * scale
            norm = LIFT - 0.5 * jnp.sum(jnp.where(place, tool * tool, 0.0), axis=0, keepdims=True)
            h, m, l = three(tool)
            nh, nm, nl = three(norm)
            ones = jnp.where(tail, 1.0, 0.0)
            hp, mp, lp = (jnp.where(place, v, 0.0) for v in (h, m, l))
            ha, ma, la = (jnp.where(angle, v, 0.0) for v in (h, m, l))
            reach = [hp + ones, mp + ones, hp + ones, jnp.where(tail, nh, lp), jnp.where(tail, nm, hp), jnp.where(tail, nl, mp)]
            right = jnp.concatenate(
                [jnp.concatenate(x, axis=0).astype(BF16) for x in (reach, [ha, ma, ha, la, ha, ma])], axis=1
            )
            raws.append(jnp.dot(field_ref[b][:, : 6 * SUB], right, preferred_element_type=F32))
            slips.append(ordered(row, h[7:8], m[7:8], l[7:8], "hmhlhm"))
        right = jnp.concatenate(
            [jnp.concatenate([slips[0], none], axis=1), jnp.concatenate([none, slips[1]], axis=1)], axis=0
        ).astype(BF16)
        slide = jnp.dot(field_ref[g * SUB + j][:, 6 * SUB : 8 * SUB], right, preferred_element_type=F32)
        return raws, slide

    def tiles(j, raws, slide):
        for i, raw in enumerate(raws):
            high, low = split(tile_of(raw[:, :LANES], raw[:, LANES:], slide[:, i * LANES : (i + 1) * LANES]))
            tall_ref[j + i, :NODE, :] = high
            tall_ref[j + i, NODE:, :] = low

    def gram(j):
        tall = tall_ref[j]
        out = lax.dot_general(tall, tall, (((1,), (1,)), ((), ())), preferred_element_type=F32)
        out = out[:NODE] + out[NODE:]
        gram_ref[j] = high_low(out + swap(out), full).astype(BF16)

    def apply(g, j):
        own = own_ref[g * SUB + j]
        out = jnp.dot(gram_ref[j], jnp.concatenate([own, own], axis=0), preferred_element_type=F32)
        fold_ref[j] = fold(out, half)

    def out_copy(g):
        return pltpu.make_async_copy(out_ref.at[g], out_hbm.at[g], out_sems.at[g])

    def emit(g):
        for m, x in enumerate(tiles_from([fold_ref[j] for j in range(SUB)])):
            spot = slice(m * SUB, (m + 1) * SUB)
            out_ref[g, spot, :] = inner_ref[g, spot, :] + x
        out_copy(g).start()

    def stages(g, first=0, last=3):
        if last >= 3:
            emit(g - 3)
        for j in range(0, SUB, 2):
            if first == 0:
                values = sums(g, j)
            for i in range(j, j + 2):
                if first <= 2 <= last:
                    apply(g - 2, i)
                if first <= 1 <= last:
                    gram(i)
            if first == 0:
                tiles(j, *values)

    share = 2 * HB * pairs // peers
    step = min(share, rows_ref.shape[1])
    for at in range(0, 2 * HB * pairs, step):
        q, r = at // share, at % share
        halo_ref[at : at + step, :] = rows_ref[q * stride + capacity + r // step][:step]
    for side in range(2):
        for h in range(HB):
            at = ((1 - side) * HB + h) * pairs
            even, odd = doubled(halo_ref[at : at + pairs, :], half)
            hold_ref[h, pl.ds(0, pairs, stride=2), :] = even
            hold_ref[h, pl.ds(1, pairs, stride=2), :] = odd
            wide_ref[side, h * NODE : (h + 1) * NODE, :] = high_low(hold_ref[h], full).astype(BF16)
        out = jnp.dot(edge_ref[side], wide_ref[side], preferred_element_type=F32)
        for i in range(HB):
            at = i * 2 * NODE
            delta_ref[side * HB + i] = fold(out[at : at + NODE] + out[at + NODE : at + 2 * NODE], half)
    got[0].wait()
    for g in range(3):
        stages(g, last=g)
    got[1].wait()
    for i in range(2 * HB):
        g, j = (0, i) if i < HB else (groups - 1, SUB - 2 * HB + i)
        spot = pl.ds(j, pairs, stride=SUB)
        inner_ref[g, spot, :] = inner_ref[g, spot, :] + delta_ref[i]

    def body(g, carry):
        stages(g)
        return carry

    lax.fori_loop(3, groups, body, 0)
    for k in range(1, 4):
        stages(groups - 1 + k, first=k)
    for g in range(groups):
        out_copy(g).wait()


def per_device(records, tool_data, owners, local_seg, active, stiffness, columns, vectors):
    doms, tools = (lax.axis_size(axis) for axis in AXES)
    peers = doms * tools
    blocks, cands = owners.shape
    nnz = columns.shape[1]
    segs, width = tool_data.shape
    capacity = max(2, (3 * blocks * cands + 2 * peers - 1) // (2 * peers))
    groups = blocks // SUB
    pairs = NODE // 2
    chunks = width // LANES
    i32 = jnp.int32

    def shape(dims, dtype=F32):
        return jax.ShapeDtypeStruct(dims, dtype)

    def tiles_of(x, rows):
        lead = x.shape[:-2]
        n = len(lead)
        x = x.reshape(lead + (rows // SUB, SUB, x.shape[-1] // LANES, LANES))
        x = jnp.swapaxes(x, n + 1, n + 2)
        return x.reshape(lead + (rows // SUB, -1, LANES))

    vec = tiles_of(vectors, blocks)
    rec = tiles_of(records, blocks)
    stiff = tiles_of(jnp.swapaxes(stiffness, 0, 1), blocks)
    share = 2 * HB * pairs // peers
    stride = capacity + -(-share // chunks)

    def in_hbm(*arrays):
        return [pltpu.with_memory_space_constraint(x, pltpu.HBM) for x in arrays]

    send = pl.pallas_call(
        functools.partial(prep_kernel, peers, segs),
        out_shape=shape((peers * (1 + share), LANES)),
        in_specs=[HBM] * 3,
        out_specs=VMEM,
        scratch_shapes=[
            pltpu.VMEM((cands, blocks), i32),
            pltpu.VMEM((cands, blocks), i32),
            pltpu.VMEM(vec.shape[1:], F32),
            pltpu.VMEM(vec.shape[1:], F32),
            pltpu.VMEM((2 * HB * pairs, LANES), F32),
            pltpu.SemaphoreType.DMA((4,)),
        ],
        compiler_params=params(8),
        name="prep",
    )(*in_hbm(owners.T, local_seg.T, vec))

    members = AXES[::-1]
    wanted = lax.all_to_all(send.reshape(peers, 1 + share, 1, LANES), members, split_axis=0, concat_axis=0, tiled=True)
    wanted = wanted.reshape(peers * (1 + share), LANES)

    parts = pl.pallas_call(
        parts_kernel,
        out_shape=shape((segs, PARTS * width), BF16),
        in_specs=[HBM] * 2,
        out_specs=VMEM,
        scratch_shapes=[pltpu.VMEM(tool_data.shape, F32), pltpu.SemaphoreType.DMA((1,))],
        compiler_params=params(8),
        cost_estimate=pl.CostEstimate(flops=1 << 20, bytes_accessed=4 << 20, transcendentals=0),
        name="parts",
    )(*in_hbm(send, tool_data))

    rows_out = pl.pallas_call(
        functools.partial(rows_kernel, peers, capacity, stride),
        out_shape=shape((peers * stride * chunks, LANES)),
        in_specs=[VMEM] * 2,
        out_specs=VMEM,
        compiler_params=params(8),
        name="rows",
    )(wanted, parts)
    fetched = lax.all_to_all(
        rows_out.reshape(peers, stride, chunks, LANES), members, split_axis=0, concat_axis=0, tiled=True
    )

    wide = (blocks, NODE, LANES)
    left = (2 * NODE, nnz // 2 * 2 * NODE)
    inner, slot, own, fields, edges = pl.pallas_call(
        functools.partial(main_kernel, doms, peers, capacity, stride),
        out_shape=(
            pltpu.HBM(vec.shape, F32),
            shape((cands, blocks), i32),
            shape(wide, BF16),
            shape(wide, BF16),
            shape((2, HB * 2 * NODE, LANES), BF16),
        ),
        in_specs=[HBM] * 6,
        out_specs=(HBM,) + (VMEM,) * 4,
        scratch_shapes=[
            pltpu.SMEM((nnz, blocks), i32),
            pltpu.VMEM(vec.shape, F32),
            pltpu.VMEM(rec.shape, F32),
            pltpu.VMEM(active.shape, i32),
            pltpu.VMEM((cands, blocks), i32),
            pltpu.VMEM(stiff.shape, F32),
            pltpu.VMEM((blocks + 2 * HB, NODE, LANES), BF16),
            pltpu.VMEM((SUB,) + left, BF16),
            pltpu.VMEM((SUB, NODE, LANES), BF16),
            pltpu.VMEM(vec.shape, F32),
            pltpu.SemaphoreType.DMA((groups + 5,)),
            pltpu.SemaphoreType.DMA,
        ],
        compiler_params=params(20),
        cost_estimate=pl.CostEstimate(
            flops=6 * blocks * nnz * NODE * NODE * NVEC, bytes_accessed=24 << 20, transcendentals=0
        ),
        name="main",
    )(*in_hbm(columns.T, vec, rec, active, owners.T, stiff))

    out = pl.pallas_call(
        functools.partial(contact_kernel, peers, capacity, stride),
        out_shape=pltpu.HBM(vec.shape, F32),
        in_specs=[HBM] + [VMEM] * 5,
        out_specs=HBM,
        scratch_shapes=[
            pltpu.SMEM((cands, blocks), i32),
            pltpu.VMEM(vec.shape, F32),
            pltpu.VMEM(vec.shape, F32),
            pltpu.VMEM((SUB, 2 * NODE, LANES), BF16),
            pltpu.VMEM((SUB, NODE, LANES), BF16),
            pltpu.VMEM((SUB, pairs, LANES), F32),
            pltpu.VMEM((2 * HB * pairs, LANES), F32),
            pltpu.VMEM((2, HB * NODE, LANES), BF16),
            pltpu.VMEM((HB, NODE, LANES), F32),
            pltpu.VMEM((2 * HB, pairs, LANES), F32),
            pltpu.SemaphoreType.DMA((2,)),
            pltpu.SemaphoreType.DMA((groups,)),
        ],
        compiler_params=params(16),
        cost_estimate=pl.CostEstimate(
            flops=80 * blocks * cands * NODE * NODE, bytes_accessed=4 << 20, transcendentals=2 * blocks * cands * NODE * NODE
        ),
        name="contact",
    )(*in_hbm(inner), slot, fetched.reshape(peers * stride, chunks, LANES), fields, own, edges)
    out = out.reshape(groups, pairs, SUB, LANES)
    return jnp.swapaxes(out, 1, 2).reshape(blocks, NODE * NVEC)


def solution(mesh):
    split_rows = P(AXES, None)
    return jax.shard_map(
        per_device,
        mesh=mesh,
        in_specs=(split_rows,) * 5 + (P(AXES, None, None),) + (split_rows,) * 2,
        out_specs=split_rows,
        check_vma=False,
    )
```

```python
import functools
import math

import jax
import jax.numpy as jnp
from jax import lax
from jax.experimental import pallas as pl
from jax.experimental.pallas import tpu as pltpu
from jax.sharding import PartitionSpec as P

NODE = 64
NVEC = 64
FIELDS = 8
HB = 2
LANES = 128
SUB = 8
AXES = ("dom", "tool")
TURN = 1.0 / (2.0 * math.pi)
REACH = math.sqrt(math.log2(math.e) / 4.0)
SHARE = math.sqrt(0.05)
FAR = -1e30
SINE = (6.283164044071425, -41.33714233428813, 81.34076747811504, -70.99341826772617)
LIFT = math.log2(-SINE[3] * SHARE * 0.5)
F32 = jnp.float32
BF16 = jnp.bfloat16
VMEM = pl.BlockSpec(memory_space=pltpu.VMEM)
SMEM = pl.BlockSpec(memory_space=pltpu.SMEM)
HBM = pl.BlockSpec(memory_space=pltpu.HBM)
ROUND = 1.5 * 2.0**23
PARTS = 3


def params(mib):
    return pltpu.CompilerParams(vmem_limit_bytes=mib << 20)


def left_half(rows):
    return lax.broadcasted_iota(jnp.int32, (rows, LANES), 1) < NODE


def swap(x):
    return pltpu.roll(x, NODE, 1)


def split(x):
    high = x.astype(BF16)
    return high, (x - high.astype(F32)).astype(BF16)


def three(x):
    high = x.astype(BF16).astype(F32)
    rest = x - high
    mid = rest.astype(BF16).astype(F32)
    return high, mid, rest - mid


def fold(out, half):
    pairs = NODE // 2
    even, odd = out[:pairs], out[pairs:]
    return jnp.where(half, even, odd) + swap(jnp.where(half, odd, even))


def flip(tiles):
    tiles = list(tiles)
    row = lax.broadcasted_iota(jnp.int32, (SUB, LANES), 0)
    for d in (4, 2, 1):
        keep = (row & d) == 0
        for i in range(SUB):
            if i & d:
                continue
            a, b = tiles[i], tiles[i + d]
            if 2 * d == SUB:
                moved = pltpu.roll(jnp.where(keep, b, a), d, 0)
                tiles[i], tiles[i + d] = jnp.where(keep, a, moved), jnp.where(keep, moved, b)
            else:
                tiles[i] = jnp.where(keep, a, pltpu.roll(b, d, 0))
                tiles[i + d] = jnp.where(keep, pltpu.roll(a, SUB - d, 0), b)
    return tiles


def flip_all(tiles):
    runs = [flip(tiles[i : i + SUB]) for i in range(0, len(tiles), SUB)]
    return [jnp.concatenate([run[j] for run in runs], axis=0) for j in range(SUB)]


def tiles_from(blocks):
    out = []
    for at in range(0, blocks[0].shape[0], SUB):
        out += flip([x[at : at + SUB] for x in blocks])
    return out


def doubled(x, half):
    other = swap(x)
    return jnp.where(half, x, other), jnp.where(half, other, x)


def high_low(x, half):
    return jnp.where(half, x, x - x.astype(BF16).astype(F32))


def copies_of(sources, targets, sems):
    made = [pltpu.make_async_copy(a, b, sems.at[i]) for i, (a, b) in enumerate(zip(sources, targets))]
    for copy in made:
        copy.start()
    return made


def pair_fields(x, y):
    quarter = left_half(x.shape[0])
    return jnp.concatenate([jnp.where(quarter, x, swap(y)), jnp.where(quarter, swap(x), y)], axis=0)


def field_rows(shape):
    row = lax.broadcasted_iota(jnp.int32, shape, 0)
    place = (row < 2) | (row == 4)
    return row, place, (row != 7) & ~place


def ranks(hits):
    n = hits.shape[1]
    upper = (
        lax.broadcasted_iota(jnp.int32, (n, n), 0) <= lax.broadcasted_iota(jnp.int32, (n, n), 1)
    ).astype(BF16)
    return jnp.dot(hits.astype(F32).astype(BF16), upper, preferred_element_type=F32)


def prep_kernel(
    peers, segs, owners_hbm, seg_hbm, vec_hbm, send_ref, owners_ref, seg_ref, first_ref, last_ref, edge_ref, sems
):
    last = vec_hbm.shape[0] - 1
    got = copies_of(
        (owners_hbm, seg_hbm, vec_hbm.at[0], vec_hbm.at[last]), (owners_ref, seg_ref, first_ref, last_ref), sems
    )
    cands = owners_ref.shape[0]
    pairs = NODE // 2
    share = 2 * HB * pairs // peers
    got[0].wait()
    got[1].wait()
    wanted = [owners_ref[k : k + 1, :] * segs + seg_ref[k : k + 1, :] for k in range(cands)]
    wanted = jnp.concatenate(wanted, axis=1).astype(F32)
    send_ref[pl.ds(0, peers, stride=1 + share), :] = jnp.broadcast_to(wanted, (peers, LANES))
    got[2].wait()
    got[3].wait()
    for h in range(HB):
        edge_ref[h * pairs : (h + 1) * pairs, :] = first_ref[pl.ds(h, pairs, stride=SUB), :]
        edge_ref[(HB + h) * pairs : (HB + h + 1) * pairs, :] = last_ref[pl.ds(SUB - HB + h, pairs, stride=SUB), :]
    for r in range(share):
        send_ref[pl.ds(1 + r, peers, stride=1 + share), :] = edge_ref[pl.ds(r, peers, stride=share), :]


def rows_kernel(peers, capacity, stride, got_ref, part_ref, out_ref):
    segs, width = part_ref.shape[0], part_ref.shape[1] // PARTS
    chunks = width // LANES
    share = got_ref.shape[0] // peers - 1
    doms, tools = (lax.axis_size(axis) for axis in AXES)
    at_dom, at_tool = (lax.axis_index(axis) for axis in AXES)
    seg = lax.broadcasted_iota(jnp.int32, (peers, segs), 1).astype(F32)
    local = got_ref[pl.ds(0, peers, stride=1 + share), :] - ((at_dom * tools + at_tool) * segs).astype(F32)
    hits = (local >= 0.0) & (local < float(segs))
    rank = ranks(hits)
    picks = []
    for s in range(capacity):
        row = jnp.sum(jnp.where(hits & (rank == s + 1.0), local, 0.0), axis=1, keepdims=True)
        picks.append((seg == row).astype(F32).astype(BF16))
    picks = jnp.concatenate(picks, axis=0)
    for c in range(0, chunks, 2):
        got = None
        for p in range(PARTS):
            at = p * width + c * LANES
            term = jnp.dot(picks, part_ref[:, at : at + 2 * LANES], preferred_element_type=F32)
            got = term if got is None else got + term
        for s in range(capacity):
            for i in range(2):
                out_ref[pl.ds(s * chunks + c + i, peers, stride=stride * chunks), :] = got[
                    s * peers : (s + 1) * peers, i * LANES : (i + 1) * LANES
                ]
    me = at_tool * doms + at_dom
    peer = lax.broadcasted_iota(jnp.int32, (peers, LANES), 0)
    for r in range(share):
        edge = got_ref[pl.ds(1 + r, peers, stride=1 + share), :]
        following = jnp.where(
            peer < peers - doms, pltpu.roll(edge, peers - doms, 0), pltpu.roll(edge, peers - doms - 1, 0)
        )
        following = jnp.where(peer == peers - 1, 0.0, following)
        previous = jnp.where(peer >= doms, pltpu.roll(edge, doms, 0), pltpu.roll(edge, doms + 1, 0))
        previous = jnp.where(peer == 0, 0.0, previous)
        out_ref[pl.ds(capacity * chunks + r, peers, stride=stride * chunks), :] = jnp.where(
            me < peers // 2, following, previous
        )


def parts_kernel(after_prep, tool_hbm, part_ref, tool_ref, sems):
    copies_of((tool_hbm,), (tool_ref,), sems)[0].wait()
    width = tool_ref.shape[1]
    field = lax.broadcasted_iota(jnp.int32, tool_ref.shape, 1) // NODE
    scale = jnp.where(field < 3, REACH, jnp.where(field < 6, 3.0 * TURN, jnp.where(field == 6, TURN, 1.0)))
    for p, part in enumerate(three(tool_ref[...] * scale)):
        part_ref[:, p * width : (p + 1) * width] = part.astype(BF16)


def ordered(row, h, m, l, order):
    out = jnp.zeros(row.shape, F32)
    for value, name in ((h, "h"), (m, "m"), (l, "l")):
        for i, at in enumerate(order):
            if at == name:
                out = jnp.where(row == i, value, out)
    return out


def main_kernel(
    doms, peers, capacity, stride,
    columns_hbm, vec_hbm, rec_hbm, act_hbm, owners_hbm, stiff_hbm, out_hbm, slot_ref, own_ref, field_ref, edge_ref,
    columns_ref, vec_ref, rec_ref, act_ref, owners_ref, stiff_ref,
    wide_ref, left_ref, last_ref, out_ref, sems, out_sem,
):
    nnz, groups = stiff_ref.shape[:2]
    blocks = groups * SUB
    pairs = NODE // 2
    even_count = nnz // 2 * 2
    half = left_half(SUB)
    half_rows = left_half(pairs)
    got = copies_of(
        (columns_hbm, vec_hbm, rec_hbm, act_hbm, owners_hbm) + tuple(stiff_hbm.at[:, g] for g in range(groups)),
        (columns_ref, vec_ref, rec_ref, act_ref, owners_ref) + tuple(stiff_ref.at[:, g] for g in range(groups)),
        sems,
    )
    zero = jnp.zeros((NODE, LANES), BF16)
    for h in range(HB):
        wide_ref[h] = zero
        wide_ref[blocks + HB + h] = zero

    def tile(m):
        return pl.ds(m * SUB, SUB)

    def spread(g):
        for at in range(0, pairs, 2 * SUB):
            evens, odds = [], []
            for m in range(at, at + 2 * SUB):
                even, odd = doubled(vec_ref[g, tile(m), :], half)
                evens.append(high_low(even, half))
                odds.append(high_low(odd, half))
            for q, values in enumerate((evens, odds)):
                for j, x in enumerate(flip_all(values)):
                    own_ref[g * SUB + j, q * pairs + at : q * pairs + at + 2 * SUB, :] = x.astype(BF16)
            mixed = [x for both in zip(evens, odds) for x in both]
            for j, x in enumerate(flip_all(mixed)):
                wide_ref[HB + g * SUB + j, 2 * at : 2 * at + 4 * SUB, :] = x.astype(BF16)

    row, place, _ = field_rows((SUB, LANES))
    scale = jnp.where(place, REACH, 1.0)
    lane = lax.broadcasted_iota(jnp.int32, (SUB, LANES), 1)
    turn = lane // NODE * NODE + lane % pairs * 2 + lane % NODE // pairs

    def evens_first(x):
        return jnp.take_along_axis(x, turn, axis=1, mode="promise_in_bounds")

    def fields(g):
        for j in range(0, SUB, 2):
            x = rec_ref[g, pl.ds(j, FIELDS // 2, stride=SUB), :]
            y = rec_ref[g, pl.ds(j + 1, FIELDS // 2, stride=SUB), :]
            part = pair_fields(x, y) * scale
            norm = -0.5 * jnp.sum(jnp.where(place, part * part, 0.0), axis=0, keepdims=True)
            at = g * SUB + j
            flags = jnp.concatenate([act_ref[pl.ds(at, 1), :], act_ref[pl.ds(at + 1, 1), :]], axis=1)
            norm = jnp.where(flags == 0, FAR, norm)
            h, m, l = three(evens_first(part))
            norms = three(evens_first(jnp.broadcast_to(norm, (SUB, LANES))))
            slip = ordered(row, h[7:8], m[7:8], l[7:8], "hhmhlm")
            lists = [jnp.where(row == 7, n, v) for n, v in zip(norms + (1.0, 1.0, 1.0), (h, h, m, h, l, m))]
            more = jnp.zeros((LANES - 8 * SUB, LANES), F32)
            stack = jnp.concatenate(lists + [slip, swap(slip), more], axis=0).T.astype(BF16)
            field_ref[at] = stack[:NODE]
            field_ref[at + 1] = stack[NODE:]

    def prepare(g):
        for at in range(0, pairs, 2 * SUB):
            for e in range(0, nnz, 2):
                evens, odds = [], []
                for m in range(at, at + 2 * SUB):
                    x = stiff_ref[e, g, tile(m), :]
                    if e < even_count:
                        y = stiff_ref[e + 1, g, tile(m), :]
                        evens.append(jnp.where(half, x, swap(y)))
                        odds.append(jnp.where(half, swap(x), y))
                    else:
                        even, odd = doubled(x, half)
                        evens.append(high_low(even, half))
                        odds.append(high_low(odd, half))
                for q, values in enumerate((evens, odds)):
                    rows = slice(q * pairs + at, q * pairs + at + 2 * SUB)
                    for j, x in enumerate(flip_all(values)):
                        if e < even_count:
                            high, low = split(x)
                            cols = slice(e * NODE, (e + 2) * NODE)
                            left_ref[j, rows, cols] = high
                            left_ref[j, NODE + rows.start : NODE + rows.stop, cols] = low
                        else:
                            last_ref[j, rows, :] = x.astype(BF16)

    def product(g):
        folded = []
        for j in range(SUB):
            cols = [wide_ref[columns_ref[e, g * SUB + j]] for e in range(nnz)]
            folded.append(fold(times(left_ref[j], last_ref[j], cols), half_rows))
        for m, x in enumerate(tiles_from(folded)):
            out_ref[g, m * SUB : (m + 1) * SUB, :] = x

    def edges(side, g, first):
        for i in range(HB):
            j = first + i
            sums = []
            for h in range(HB):
                total = jnp.zeros((pairs, LANES), F32)
                for e in range(nnz):
                    here = columns_ref[e, g * SUB + j] == side * (blocks + HB) + h
                    total = total + jnp.where(here, stiff_ref[e, g, pl.ds(j, pairs, stride=SUB), :], 0.0)
                sums.append(total)
            x, y = sums
            left = jnp.concatenate([jnp.where(half_rows, x, swap(y)), jnp.where(half_rows, swap(x), y)], axis=0)
            high, low = split(left)
            edge_ref[side, i * 2 * NODE : i * 2 * NODE + NODE, :] = high
            edge_ref[side, i * 2 * NODE + NODE : (i + 1) * 2 * NODE, :] = low

    got[1].wait()
    spread(0)
    spread(1)
    got[5].wait()
    prepare(0)
    got[0].wait()
    edges(0, 0, 0)
    got[2].wait()
    got[3].wait()
    got[4].wait()
    cands = owners_ref.shape[0]
    owner_ids = lax.broadcasted_iota(jnp.int32, (peers, blocks), 0)
    before = jnp.zeros((peers, 1), F32)
    for k in range(cands):
        target = owners_ref[k : k + 1, :]
        hits = owner_ids == jnp.broadcast_to(target, (peers, blocks))
        places = jnp.where(hits, before + ranks(hits) - 1.0, 0.0)
        before = before + jnp.sum(hits.astype(F32), axis=1, keepdims=True)
        rank = jnp.sum(places, axis=0, keepdims=True)
        tools = peers // doms
        slot_ref[k : k + 1, :] = (target % tools * doms + target // tools) * stride + rank.astype(jnp.int32)

    def body(g, carry):
        pltpu.make_async_copy(stiff_hbm.at[:, g + 1], stiff_ref.at[:, g + 1], sems.at[6 + g]).wait()
        product(g)
        prepare(g + 1)
        spread(jnp.minimum(g + 2, groups - 1))
        fields(g)
        return carry

    lax.fori_loop(0, groups - 1, body, 0)
    product(groups - 1)
    inners = pltpu.make_async_copy(out_ref, out_hbm, out_sem)
    inners.start()
    fields(groups - 1)
    edges(1, groups - 1, SUB - HB)
    inners.wait()


def times(left, last, cols):
    even_count = left.shape[1] // NODE
    out = jnp.dot(left, jnp.concatenate(cols[:even_count], axis=0), preferred_element_type=F32)
    out = out[:NODE] + out[NODE:]
    if len(cols) > even_count:
        out = out + jnp.dot(last, jnp.concatenate([cols[-1], cols[-1]], axis=0), preferred_element_type=F32)
    return out


def contact_kernel(
    peers, capacity, stride, inner_hbm, slots_ref, rows_ref, field_ref, own_ref, edge_ref, out_hbm,
    slot_ref, inner_ref, out_ref, tall_ref, gram_ref, fold_ref, halo_ref, wide_ref, hold_ref, delta_ref, sems, out_sems,
):
    got = copies_of((slots_ref, inner_hbm), (slot_ref, inner_ref), sems)
    blocks = slot_ref.shape[1]
    groups = blocks // SUB
    pairs = NODE // 2
    half = left_half(pairs)
    full = left_half(NODE)
    row, place, angle = field_rows((SUB, LANES))
    none = jnp.zeros((SUB, LANES), F32)
    tail = row == 7

    def tile_of(reach, phase, slip):
        turn = jnp.abs(phase - ((phase + ROUND) - ROUND)) - 0.25
        square = turn * turn
        wave = square + SINE[2] / SINE[3]
        wave = wave * square + SINE[1] / SINE[3]
        wave = wave * square + SINE[0] / SINE[3]
        return jnp.exp2(reach) * (wave * turn) * (2.0 + jnp.tanh(slip))

    def tiles(g, j):
        raws, slips = [], []
        for i in range(2):
            b = g * SUB + j + i
            tool = pair_fields(rows_ref[slot_ref[0, b]], rows_ref[slot_ref[1, b]])
            norm = LIFT - 0.5 * jnp.sum(jnp.where(place, tool * tool, 0.0), axis=0, keepdims=True)
            h, m, l = three(tool)
            nh, nm, nl = three(norm)
            ones = jnp.where(tail, 1.0, 0.0)
            hp, mp, lp = (jnp.where(place, v, 0.0) for v in (h, m, l))
            ha, ma, la = (jnp.where(angle, v, 0.0) for v in (h, m, l))
            reach = [hp + ones, mp + ones, hp + ones, jnp.where(tail, nh, lp), jnp.where(tail, nm, hp), jnp.where(tail, nl, mp)]
            right = jnp.concatenate(
                [jnp.concatenate(x, axis=0).astype(BF16) for x in (reach, [ha, ma, ha, la, ha, ma])], axis=1
            )
            raws.append(jnp.dot(field_ref[b][:, : 6 * SUB], right, preferred_element_type=F32))
            slips.append(ordered(row, h[7:8], m[7:8], l[7:8], "hmhlhm"))
        right = jnp.concatenate(
            [jnp.concatenate([slips[0], none], axis=1), jnp.concatenate([none, slips[1]], axis=1)], axis=0
        ).astype(BF16)
        slide = jnp.dot(field_ref[g * SUB + j][:, 6 * SUB : 8 * SUB], right, preferred_element_type=F32)
        for i, raw in enumerate(raws):
            high, low = split(tile_of(raw[:, :LANES], raw[:, LANES:], slide[:, i * LANES : (i + 1) * LANES]))
            tall_ref[j + i, :NODE, :] = high
            tall_ref[j + i, NODE:, :] = low

    def gram(j):
        tall = tall_ref[j]
        out = lax.dot_general(tall, tall, (((1,), (1,)), ((), ())), preferred_element_type=F32)
        out = out[:NODE] + out[NODE:]
        gram_ref[j] = high_low(out + swap(out), full).astype(BF16)

    def apply(g, j):
        own = own_ref[g * SUB + j]
        out = jnp.dot(gram_ref[j], jnp.concatenate([own, own], axis=0), preferred_element_type=F32)
        fold_ref[j] = fold(out, half)

    def out_copy(g):
        return pltpu.make_async_copy(out_ref.at[g], out_hbm.at[g], out_sems.at[g])

    def emit(g):
        for m, x in enumerate(tiles_from([fold_ref[j] for j in range(SUB)])):
            spot = slice(m * SUB, (m + 1) * SUB)
            out_ref[g, spot, :] = inner_ref[g, spot, :] + x
        out_copy(g).start()

    def stages(g, first=0, last=3):
        if last >= 3:
            emit(g - 3)
        for j in range(0, SUB, 2):
            for i in range(j, j + 2):
                if first <= 2 <= last:
                    apply(g - 2, i)
                if first <= 1 <= last:
                    gram(i)
            if first == 0:
                tiles(g, j)

    share = 2 * HB * pairs // peers
    step = min(share, rows_ref.shape[1])
    for at in range(0, 2 * HB * pairs, step):
        q, r = at // share, at % share
        halo_ref[at : at + step, :] = rows_ref[q * stride + capacity + r // step][:step]
    got[0].wait()
    stages(0, last=0)
    for side in range(2):
        for h in range(HB):
            at = ((1 - side) * HB + h) * pairs
            even, odd = doubled(halo_ref[at : at + pairs, :], half)
            hold_ref[h, pl.ds(0, pairs, stride=2), :] = even
            hold_ref[h, pl.ds(1, pairs, stride=2), :] = odd
            wide_ref[side, h * NODE : (h + 1) * NODE, :] = high_low(hold_ref[h], full).astype(BF16)
        out = jnp.dot(edge_ref[side], wide_ref[side], preferred_element_type=F32)
        for i in range(HB):
            at = i * 2 * NODE
            delta_ref[side * HB + i] = fold(out[at : at + NODE] + out[at + NODE : at + 2 * NODE], half)
    stages(1, last=1)
    stages(2, last=2)
    got[1].wait()
    for i in range(2 * HB):
        g, j = (0, i) if i < HB else (groups - 1, SUB - 2 * HB + i)
        spot = pl.ds(j, pairs, stride=SUB)
        inner_ref[g, spot, :] = inner_ref[g, spot, :] + delta_ref[i]

    def body(g, carry):
        stages(g)
        return carry

    lax.fori_loop(3, groups, body, 0)
    for k in range(1, 4):
        stages(groups - 1 + k, first=k)
    for g in range(groups):
        out_copy(g).wait()


def per_device(records, tool_data, owners, local_seg, active, stiffness, columns, vectors):
    doms, tools = (lax.axis_size(axis) for axis in AXES)
    peers = doms * tools
    blocks, cands = owners.shape
    nnz = columns.shape[1]
    segs, width = tool_data.shape
    capacity = max(2, (3 * blocks * cands + 2 * peers - 1) // (2 * peers))
    groups = blocks // SUB
    pairs = NODE // 2
    chunks = width // LANES
    i32 = jnp.int32

    def shape(dims, dtype=F32):
        return jax.ShapeDtypeStruct(dims, dtype)

    def tiles_of(x, rows):
        lead = x.shape[:-2]
        n = len(lead)
        x = x.reshape(lead + (rows // SUB, SUB, x.shape[-1] // LANES, LANES))
        x = jnp.swapaxes(x, n + 1, n + 2)
        return x.reshape(lead + (rows // SUB, -1, LANES))

    vec = tiles_of(vectors, blocks)
    rec = tiles_of(records, blocks)
    stiff = tiles_of(jnp.swapaxes(stiffness, 0, 1), blocks)
    share = 2 * HB * pairs // peers
    stride = capacity + -(-share // chunks)

    def in_hbm(*arrays):
        return [pltpu.with_memory_space_constraint(x, pltpu.HBM) for x in arrays]

    send = pl.pallas_call(
        functools.partial(prep_kernel, peers, segs),
        out_shape=shape((peers * (1 + share), LANES)),
        in_specs=[HBM] * 3,
        out_specs=VMEM,
        scratch_shapes=[
            pltpu.VMEM((cands, blocks), i32),
            pltpu.VMEM((cands, blocks), i32),
            pltpu.VMEM(vec.shape[1:], F32),
            pltpu.VMEM(vec.shape[1:], F32),
            pltpu.VMEM((2 * HB * pairs, LANES), F32),
            pltpu.SemaphoreType.DMA((4,)),
        ],
        compiler_params=params(8),
        name="prep",
    )(*in_hbm(owners.T, local_seg.T, vec))

    members = AXES[::-1]
    wanted = lax.all_to_all(send.reshape(peers, 1 + share, 1, LANES), members, split_axis=0, concat_axis=0, tiled=True)
    wanted = wanted.reshape(peers * (1 + share), LANES)

    parts = pl.pallas_call(
        parts_kernel,
        out_shape=shape((segs, PARTS * width), BF16),
        in_specs=[HBM] * 2,
        out_specs=VMEM,
        scratch_shapes=[pltpu.VMEM(tool_data.shape, F32), pltpu.SemaphoreType.DMA((1,))],
        compiler_params=params(8),
        cost_estimate=pl.CostEstimate(flops=1 << 20, bytes_accessed=4 << 20, transcendentals=0),
        name="parts",
    )(*in_hbm(send, tool_data))

    rows_out = pl.pallas_call(
        functools.partial(rows_kernel, peers, capacity, stride),
        out_shape=shape((peers * stride * chunks, LANES)),
        in_specs=[VMEM] * 2,
        out_specs=VMEM,
        compiler_params=params(8),
        name="rows",
    )(wanted, parts)
    fetched = lax.all_to_all(
        rows_out.reshape(peers, stride, chunks, LANES), members, split_axis=0, concat_axis=0, tiled=True
    )

    wide = (blocks, NODE, LANES)
    left = (2 * NODE, nnz // 2 * 2 * NODE)
    inner, slot, own, fields, edges = pl.pallas_call(
        functools.partial(main_kernel, doms, peers, capacity, stride),
        out_shape=(
            pltpu.HBM(vec.shape, F32),
            shape((cands, blocks), i32),
            shape(wide, BF16),
            shape(wide, BF16),
            shape((2, HB * 2 * NODE, LANES), BF16),
        ),
        in_specs=[HBM] * 6,
        out_specs=(HBM,) + (VMEM,) * 4,
        scratch_shapes=[
            pltpu.SMEM((nnz, blocks), i32),
            pltpu.VMEM(vec.shape, F32),
            pltpu.VMEM(rec.shape, F32),
            pltpu.VMEM(active.shape, i32),
            pltpu.VMEM((cands, blocks), i32),
            pltpu.VMEM(stiff.shape, F32),
            pltpu.VMEM((blocks + 2 * HB, NODE, LANES), BF16),
            pltpu.VMEM((SUB,) + left, BF16),
            pltpu.VMEM((SUB, NODE, LANES), BF16),
            pltpu.VMEM(vec.shape, F32),
            pltpu.SemaphoreType.DMA((groups + 5,)),
            pltpu.SemaphoreType.DMA,
        ],
        compiler_params=params(20),
        cost_estimate=pl.CostEstimate(
            flops=6 * blocks * nnz * NODE * NODE * NVEC, bytes_accessed=24 << 20, transcendentals=0
        ),
        name="main",
    )(*in_hbm(columns.T, vec, rec, active, owners.T, stiff))

    out = pl.pallas_call(
        functools.partial(contact_kernel, peers, capacity, stride),
        out_shape=pltpu.HBM(vec.shape, F32),
        in_specs=[HBM] + [VMEM] * 5,
        out_specs=HBM,
        scratch_shapes=[
            pltpu.SMEM((cands, blocks), i32),
            pltpu.VMEM(vec.shape, F32),
            pltpu.VMEM(vec.shape, F32),
            pltpu.VMEM((SUB, 2 * NODE, LANES), BF16),
            pltpu.VMEM((SUB, NODE, LANES), BF16),
            pltpu.VMEM((SUB, pairs, LANES), F32),
            pltpu.VMEM((2 * HB * pairs, LANES), F32),
            pltpu.VMEM((2, HB * NODE, LANES), BF16),
            pltpu.VMEM((HB, NODE, LANES), F32),
            pltpu.VMEM((2 * HB, pairs, LANES), F32),
            pltpu.SemaphoreType.DMA((2,)),
            pltpu.SemaphoreType.DMA((groups,)),
        ],
        compiler_params=params(16),
        cost_estimate=pl.CostEstimate(
            flops=80 * blocks * cands * NODE * NODE, bytes_accessed=4 << 20, transcendentals=2 * blocks * cands * NODE * NODE
        ),
        name="contact",
    )(*in_hbm(inner), slot, fetched.reshape(peers * stride, chunks, LANES), fields, own, edges)
    out = out.reshape(groups, pairs, SUB, LANES)
    return jnp.swapaxes(out, 1, 2).reshape(blocks, NODE * NVEC)


def solution(mesh):
    split_rows = P(AXES, None)
    return jax.shard_map(
        per_device,
        mesh=mesh,
        in_specs=(split_rows,) * 5 + (P(AXES, None, None),) + (split_rows,) * 2,
        out_specs=split_rows,
        check_vma=False,
    )
```

```python
import functools
import math

import jax
import jax.numpy as jnp
from jax import lax
from jax.experimental import pallas as pl
from jax.experimental.pallas import tpu as pltpu
from jax.sharding import PartitionSpec as P

NODE = 64
NVEC = 64
FIELDS = 8
HB = 2
LANES = 128
SUB = 8
AXES = ("dom", "tool")
TURN = 1.0 / (2.0 * math.pi)
REACH = math.sqrt(math.log2(math.e) / 4.0)
SHARE = math.sqrt(0.05)
FAR = -1e30
SINE = (6.283164044071425, -41.33714233428813, 81.34076747811504, -70.99341826772617)
LIFT = math.log2(-SINE[3] * SHARE * 0.5)
F32 = jnp.float32
BF16 = jnp.bfloat16
VMEM = pl.BlockSpec(memory_space=pltpu.VMEM)
SMEM = pl.BlockSpec(memory_space=pltpu.SMEM)
HBM = pl.BlockSpec(memory_space=pltpu.HBM)
ROUND = 1.5 * 2.0**23
PARTS = 3


def params(mib):
    return pltpu.CompilerParams(vmem_limit_bytes=mib << 20)


def left_half(rows):
    return lax.broadcasted_iota(jnp.int32, (rows, LANES), 1) < NODE


def swap(x):
    return pltpu.roll(x, NODE, 1)


def split(x):
    high = x.astype(BF16)
    return high, (x - high.astype(F32)).astype(BF16)


def three(x):
    high = x.astype(BF16).astype(F32)
    rest = x - high
    mid = rest.astype(BF16).astype(F32)
    return high, mid, rest - mid


def fold(out, half):
    pairs = NODE // 2
    even, odd = out[:pairs], out[pairs:]
    return jnp.where(half, even, odd) + swap(jnp.where(half, odd, even))


def flip(tiles):
    tiles = list(tiles)
    row = lax.broadcasted_iota(jnp.int32, (SUB, LANES), 0)
    for d in (4, 2, 1):
        keep = (row & d) == 0
        for i in range(SUB):
            if i & d:
                continue
            a, b = tiles[i], tiles[i + d]
            if 2 * d == SUB:
                moved = pltpu.roll(jnp.where(keep, b, a), d, 0)
                tiles[i], tiles[i + d] = jnp.where(keep, a, moved), jnp.where(keep, moved, b)
            else:
                tiles[i] = jnp.where(keep, a, pltpu.roll(b, d, 0))
                tiles[i + d] = jnp.where(keep, pltpu.roll(a, SUB - d, 0), b)
    return tiles


def flip_all(tiles):
    runs = [flip(tiles[i : i + SUB]) for i in range(0, len(tiles), SUB)]
    return [jnp.concatenate([run[j] for run in runs], axis=0) for j in range(SUB)]


def tiles_from(blocks):
    out = []
    for at in range(0, blocks[0].shape[0], SUB):
        out += flip([x[at : at + SUB] for x in blocks])
    return out


def doubled(x, half):
    other = swap(x)
    return jnp.where(half, x, other), jnp.where(half, other, x)


def high_low(x, half):
    return jnp.where(half, x, x - x.astype(BF16).astype(F32))


def copies_of(sources, targets, sems):
    made = [pltpu.make_async_copy(a, b, sems.at[i]) for i, (a, b) in enumerate(zip(sources, targets))]
    for copy in made:
        copy.start()
    return made


def pair_fields(x, y):
    quarter = left_half(x.shape[0])
    return jnp.concatenate([jnp.where(quarter, x, swap(y)), jnp.where(quarter, swap(x), y)], axis=0)


def field_rows(shape):
    row = lax.broadcasted_iota(jnp.int32, shape, 0)
    place = (row < 2) | (row == 4)
    return row, place, (row != 7) & ~place


def ranks(hits):
    n = hits.shape[1]
    upper = (
        lax.broadcasted_iota(jnp.int32, (n, n), 0) <= lax.broadcasted_iota(jnp.int32, (n, n), 1)
    ).astype(BF16)
    return jnp.dot(hits.astype(F32).astype(BF16), upper, preferred_element_type=F32)


def prep_kernel(
    peers, segs, owners_hbm, seg_hbm, vec_hbm, send_ref, owners_ref, seg_ref, first_ref, last_ref, edge_ref, sems
):
    last = vec_hbm.shape[0] - 1
    got = copies_of(
        (owners_hbm, seg_hbm, vec_hbm.at[0], vec_hbm.at[last]), (owners_ref, seg_ref, first_ref, last_ref), sems
    )
    cands = owners_ref.shape[0]
    pairs = NODE // 2
    share = 2 * HB * pairs // peers
    got[0].wait()
    got[1].wait()
    wanted = [owners_ref[k : k + 1, :] * segs + seg_ref[k : k + 1, :] for k in range(cands)]
    wanted = jnp.concatenate(wanted, axis=1).astype(F32)
    send_ref[pl.ds(0, peers, stride=1 + share), :] = jnp.broadcast_to(wanted, (peers, LANES))
    got[2].wait()
    got[3].wait()
    for h in range(HB):
        edge_ref[h * pairs : (h + 1) * pairs, :] = first_ref[pl.ds(h, pairs, stride=SUB), :]
        edge_ref[(HB + h) * pairs : (HB + h + 1) * pairs, :] = last_ref[pl.ds(SUB - HB + h, pairs, stride=SUB), :]
    for r in range(share):
        send_ref[pl.ds(1 + r, peers, stride=1 + share), :] = edge_ref[pl.ds(r, peers, stride=share), :]


def rows_kernel(peers, capacity, stride, got_ref, part_ref, out_ref):
    segs, width = part_ref.shape[0], part_ref.shape[1] // PARTS
    chunks = width // LANES
    share = got_ref.shape[0] // peers - 1
    doms, tools = (lax.axis_size(axis) for axis in AXES)
    at_dom, at_tool = (lax.axis_index(axis) for axis in AXES)
    seg = lax.broadcasted_iota(jnp.int32, (peers, segs), 1).astype(F32)
    local = got_ref[pl.ds(0, peers, stride=1 + share), :] - ((at_dom * tools + at_tool) * segs).astype(F32)
    hits = (local >= 0.0) & (local < float(segs))
    rank = ranks(hits)
    picks = []
    for s in range(capacity):
        row = jnp.sum(jnp.where(hits & (rank == s + 1.0), local, 0.0), axis=1, keepdims=True)
        picks.append((seg == row).astype(F32).astype(BF16))
    picks = jnp.concatenate(picks, axis=0)
    for c in range(0, chunks, 2):
        got = None
        for p in range(PARTS):
            at = p * width + c * LANES
            term = jnp.dot(picks, part_ref[:, at : at + 2 * LANES], preferred_element_type=F32)
            got = term if got is None else got + term
        for s in range(capacity):
            for i in range(2):
                out_ref[pl.ds(s * chunks + c + i, peers, stride=stride * chunks), :] = got[
                    s * peers : (s + 1) * peers, i * LANES : (i + 1) * LANES
                ]
    me = at_tool * doms + at_dom
    peer = lax.broadcasted_iota(jnp.int32, (peers, LANES), 0)
    for r in range(share):
        edge = got_ref[pl.ds(1 + r, peers, stride=1 + share), :]
        following = jnp.where(
            peer < peers - doms, pltpu.roll(edge, peers - doms, 0), pltpu.roll(edge, peers - doms - 1, 0)
        )
        following = jnp.where(peer == peers - 1, 0.0, following)
        previous = jnp.where(peer >= doms, pltpu.roll(edge, doms, 0), pltpu.roll(edge, doms + 1, 0))
        previous = jnp.where(peer == 0, 0.0, previous)
        out_ref[pl.ds(capacity * chunks + r, peers, stride=stride * chunks), :] = jnp.where(
            me < peers // 2, following, previous
        )


def parts_kernel(after_prep, tool_hbm, part_ref, tool_ref, sems):
    copies_of((tool_hbm,), (tool_ref,), sems)[0].wait()
    width = tool_ref.shape[1]
    field = lax.broadcasted_iota(jnp.int32, tool_ref.shape, 1) // NODE
    scale = jnp.where(field < 3, REACH, jnp.where(field < 6, 3.0 * TURN, jnp.where(field == 6, TURN, 1.0)))
    for p, part in enumerate(three(tool_ref[...] * scale)):
        part_ref[:, p * width : (p + 1) * width] = part.astype(BF16)


def ordered(row, h, m, l, order):
    out = jnp.zeros(row.shape, F32)
    for value, name in ((h, "h"), (m, "m"), (l, "l")):
        for i, at in enumerate(order):
            if at == name:
                out = jnp.where(row == i, value, out)
    return out


def main_kernel(
    doms, peers, capacity, stride,
    columns_hbm, vec_hbm, rec_hbm, act_hbm, owners_hbm, stiff_hbm, out_hbm, slot_ref, own_ref, field_ref, edge_ref,
    columns_ref, vec_ref, rec_ref, act_ref, owners_ref, stiff_ref,
    wide_ref, left_ref, last_ref, out_ref, sems, out_sem,
):
    nnz, groups = stiff_ref.shape[:2]
    blocks = groups * SUB
    pairs = NODE // 2
    even_count = nnz // 2 * 2
    half = left_half(SUB)
    half_rows = left_half(pairs)
    got = copies_of(
        (columns_hbm, vec_hbm, rec_hbm, act_hbm, owners_hbm) + tuple(stiff_hbm.at[:, g] for g in range(groups)),
        (columns_ref, vec_ref, rec_ref, act_ref, owners_ref) + tuple(stiff_ref.at[:, g] for g in range(groups)),
        sems,
    )
    zero = jnp.zeros((NODE, LANES), BF16)
    for h in range(HB):
        wide_ref[h] = zero
        wide_ref[blocks + HB + h] = zero

    def tile(m):
        return pl.ds(m * SUB, SUB)

    def spread(g):
        for at in range(0, pairs, 2 * SUB):
            evens, odds = [], []
            for m in range(at, at + 2 * SUB):
                even, odd = doubled(vec_ref[g, tile(m), :], half)
                evens.append(high_low(even, half))
                odds.append(high_low(odd, half))
            for q, values in enumerate((evens, odds)):
                for j, x in enumerate(flip_all(values)):
                    own_ref[g * SUB + j, q * pairs + at : q * pairs + at + 2 * SUB, :] = x.astype(BF16)
            mixed = [x for both in zip(evens, odds) for x in both]
            for j, x in enumerate(flip_all(mixed)):
                wide_ref[HB + g * SUB + j, 2 * at : 2 * at + 4 * SUB, :] = x.astype(BF16)

    row, place, _ = field_rows((SUB, LANES))
    scale = jnp.where(place, REACH, 1.0)
    lane = lax.broadcasted_iota(jnp.int32, (SUB, LANES), 1)
    turn = lane // NODE * NODE + lane % pairs * 2 + lane % NODE // pairs

    def evens_first(x):
        return jnp.take_along_axis(x, turn, axis=1, mode="promise_in_bounds")

    def fields(g):
        for j in range(0, SUB, 2):
            x = rec_ref[g, pl.ds(j, FIELDS // 2, stride=SUB), :]
            y = rec_ref[g, pl.ds(j + 1, FIELDS // 2, stride=SUB), :]
            part = pair_fields(x, y) * scale
            norm = -0.5 * jnp.sum(jnp.where(place, part * part, 0.0), axis=0, keepdims=True)
            at = g * SUB + j
            flags = jnp.concatenate([act_ref[pl.ds(at, 1), :], act_ref[pl.ds(at + 1, 1), :]], axis=1)
            norm = jnp.where(flags == 0, FAR, norm)
            h, m, l = three(evens_first(part))
            norms = three(evens_first(jnp.broadcast_to(norm, (SUB, LANES))))
            slip = ordered(row, h[7:8], m[7:8], l[7:8], "hhmhlm")
            lists = [jnp.where(row == 7, n, v) for n, v in zip(norms + (1.0, 1.0, 1.0), (h, h, m, h, l, m))]
            more = jnp.zeros((LANES - 8 * SUB, LANES), F32)
            stack = jnp.concatenate(lists + [slip, swap(slip), more], axis=0).T.astype(BF16)
            field_ref[at] = stack[:NODE]
            field_ref[at + 1] = stack[NODE:]

    def prepare(g):
        for at in range(0, pairs, 2 * SUB):
            for e in range(0, nnz, 2):
                evens, odds = [], []
                for m in range(at, at + 2 * SUB):
                    x = stiff_ref[e, g, tile(m), :]
                    if e < even_count:
                        y = stiff_ref[e + 1, g, tile(m), :]
                        evens.append(jnp.where(half, x, swap(y)))
                        odds.append(jnp.where(half, swap(x), y))
                    else:
                        even, odd = doubled(x, half)
                        evens.append(high_low(even, half))
                        odds.append(high_low(odd, half))
                for q, values in enumerate((evens, odds)):
                    rows = slice(q * pairs + at, q * pairs + at + 2 * SUB)
                    for j, x in enumerate(flip_all(values)):
                        if e < even_count:
                            high, low = split(x)
                            cols = slice(e * NODE, (e + 2) * NODE)
                            left_ref[j, rows, cols] = high
                            left_ref[j, NODE + rows.start : NODE + rows.stop, cols] = low
                        else:
                            last_ref[j, rows, :] = x.astype(BF16)

    def product(g):
        folded = []
        for j in range(SUB):
            cols = [wide_ref[columns_ref[e, g * SUB + j]] for e in range(nnz)]
            folded.append(fold(times(left_ref[j], last_ref[j], cols), half_rows))
        for m, x in enumerate(tiles_from(folded)):
            out_ref[g, m * SUB : (m + 1) * SUB, :] = x

    def edges(side, g, first):
        for i in range(HB):
            j = first + i
            sums = []
            for h in range(HB):
                total = jnp.zeros((pairs, LANES), F32)
                for e in range(nnz):
                    here = columns_ref[e, g * SUB + j] == side * (blocks + HB) + h
                    total = total + jnp.where(here, stiff_ref[e, g, pl.ds(j, pairs, stride=SUB), :], 0.0)
                sums.append(total)
            x, y = sums
            left = jnp.concatenate([jnp.where(half_rows, x, swap(y)), jnp.where(half_rows, swap(x), y)], axis=0)
            high, low = split(left)
            edge_ref[side, i * 2 * NODE : i * 2 * NODE + NODE, :] = high
            edge_ref[side, i * 2 * NODE + NODE : (i + 1) * 2 * NODE, :] = low

    got[1].wait()
    spread(0)
    spread(1)
    got[5].wait()
    prepare(0)
    got[0].wait()
    edges(0, 0, 0)
    got[2].wait()
    got[3].wait()
    got[4].wait()
    cands = owners_ref.shape[0]
    owner_ids = lax.broadcasted_iota(jnp.int32, (peers, blocks), 0)
    before = jnp.zeros((peers, 1), F32)
    for k in range(cands):
        target = owners_ref[k : k + 1, :]
        hits = owner_ids == jnp.broadcast_to(target, (peers, blocks))
        places = jnp.where(hits, before + ranks(hits) - 1.0, 0.0)
        before = before + jnp.sum(hits.astype(F32), axis=1, keepdims=True)
        rank = jnp.sum(places, axis=0, keepdims=True)
        tools = peers // doms
        slot_ref[k : k + 1, :] = (target % tools * doms + target // tools) * stride + rank.astype(jnp.int32)

    def body(g, carry):
        pltpu.make_async_copy(stiff_hbm.at[:, g + 1], stiff_ref.at[:, g + 1], sems.at[6 + g]).wait()
        product(g)
        prepare(g + 1)
        spread(jnp.minimum(g + 2, groups - 1))
        fields(g)
        return carry

    lax.fori_loop(0, groups - 1, body, 0)
    product(groups - 1)
    inners = pltpu.make_async_copy(out_ref, out_hbm, out_sem)
    inners.start()
    fields(groups - 1)
    edges(1, groups - 1, SUB - HB)
    inners.wait()


def times(left, last, cols):
    even_count = left.shape[1] // NODE
    out = jnp.dot(left, jnp.concatenate(cols[:even_count], axis=0), preferred_element_type=F32)
    out = out[:NODE] + out[NODE:]
    if len(cols) > even_count:
        out = out + jnp.dot(last, jnp.concatenate([cols[-1], cols[-1]], axis=0), preferred_element_type=F32)
    return out


def contact_kernel(
    peers, capacity, stride, inner_hbm, slots_ref, rows_ref, field_ref, own_ref, edge_ref, out_hbm,
    slot_ref, inner_ref, out_ref, tall_ref, gram_ref, fold_ref, halo_ref, wide_ref, hold_ref, delta_ref, sems, out_sems,
):
    got = copies_of((slots_ref, inner_hbm), (slot_ref, inner_ref), sems)
    blocks = slot_ref.shape[1]
    groups = blocks // SUB
    pairs = NODE // 2
    half = left_half(pairs)
    full = left_half(NODE)
    row, place, angle = field_rows((SUB, LANES))
    none = jnp.zeros((SUB, LANES), F32)
    tail = row == 7

    def tile_of(reach, phase, slip):
        turn = jnp.abs(phase - ((phase + ROUND) - ROUND)) - 0.25
        square = turn * turn
        wave = square + SINE[2] / SINE[3]
        wave = wave * square + SINE[1] / SINE[3]
        wave = wave * square + SINE[0] / SINE[3]
        return jnp.exp2(reach) * (wave * turn) * (2.0 + jnp.tanh(slip))

    def tiles(g, j):
        raws, slips = [], []
        for i in range(2):
            b = g * SUB + j + i
            tool = pair_fields(rows_ref[slot_ref[0, b]], rows_ref[slot_ref[1, b]])
            norm = LIFT - 0.5 * jnp.sum(jnp.where(place, tool * tool, 0.0), axis=0, keepdims=True)
            h, m, l = three(tool)
            nh, nm, nl = three(norm)
            ones = jnp.where(tail, 1.0, 0.0)
            hp, mp, lp = (jnp.where(place, v, 0.0) for v in (h, m, l))
            ha, ma, la = (jnp.where(angle, v, 0.0) for v in (h, m, l))
            reach = [hp + ones, mp + ones, hp + ones, jnp.where(tail, nh, lp), jnp.where(tail, nm, hp), jnp.where(tail, nl, mp)]
            right = jnp.concatenate(
                [jnp.concatenate(x, axis=0).astype(BF16) for x in (reach, [ha, ma, ha, la, ha, ma])], axis=1
            )
            raws.append(jnp.dot(field_ref[b][:, : 6 * SUB], right, preferred_element_type=F32))
            slips.append(ordered(row, h[7:8], m[7:8], l[7:8], "hmhlhm"))
        right = jnp.concatenate(
            [jnp.concatenate([slips[0], none], axis=1), jnp.concatenate([none, slips[1]], axis=1)], axis=0
        ).astype(BF16)
        slide = jnp.dot(field_ref[g * SUB + j][:, 6 * SUB : 8 * SUB], right, preferred_element_type=F32)
        for i, raw in enumerate(raws):
            high, low = split(tile_of(raw[:, :LANES], raw[:, LANES:], slide[:, i * LANES : (i + 1) * LANES]))
            tall_ref[j + i, :NODE, :] = high
            tall_ref[j + i, NODE:, :] = low

    def gram(j):
        tall = tall_ref[j]
        out = lax.dot_general(tall, tall, (((1,), (1,)), ((), ())), preferred_element_type=F32)
        out = out[:NODE] + out[NODE:]
        gram_ref[j] = high_low(out + swap(out), full).astype(BF16)

    def apply(g, j):
        own = own_ref[g * SUB + j]
        out = jnp.dot(gram_ref[j], jnp.concatenate([own, own], axis=0), preferred_element_type=F32)
        fold_ref[j] = fold(out, half)

    def out_copy(g):
        return pltpu.make_async_copy(out_ref.at[g], out_hbm.at[g], out_sems.at[g])

    def emit(g):
        for m, x in enumerate(tiles_from([fold_ref[j] for j in range(SUB)])):
            spot = slice(m * SUB, (m + 1) * SUB)
            out_ref[g, spot, :] = inner_ref[g, spot, :] + x
        out_copy(g).start()

    def stages(g, first=0, last=3):
        if last >= 3:
            emit(g - 3)
        for j in range(0, SUB, 2):
            if first <= 2 <= last:
                apply(g - 2, j)
                apply(g - 2, j + 1)
            if first <= 1 <= last:
                gram(j)
                gram(j + 1)
            if first == 0:
                tiles(g, j)

    share = 2 * HB * pairs // peers
    step = min(share, rows_ref.shape[1])
    for at in range(0, 2 * HB * pairs, step):
        q, r = at // share, at % share
        halo_ref[at : at + step, :] = rows_ref[q * stride + capacity + r // step][:step]
    got[0].wait()
    stages(0, last=0)
    for side in range(2):
        for h in range(HB):
            at = ((1 - side) * HB + h) * pairs
            even, odd = doubled(halo_ref[at : at + pairs, :], half)
            hold_ref[h, pl.ds(0, pairs, stride=2), :] = even
            hold_ref[h, pl.ds(1, pairs, stride=2), :] = odd
            wide_ref[side, h * NODE : (h + 1) * NODE, :] = high_low(hold_ref[h], full).astype(BF16)
        out = jnp.dot(edge_ref[side], wide_ref[side], preferred_element_type=F32)
        for i in range(HB):
            at = i * 2 * NODE
            delta_ref[side * HB + i] = fold(out[at : at + NODE] + out[at + NODE : at + 2 * NODE], half)
    stages(1, last=1)
    stages(2, last=2)
    got[1].wait()
    for i in range(2 * HB):
        g, j = (0, i) if i < HB else (groups - 1, SUB - 2 * HB + i)
        spot = pl.ds(j, pairs, stride=SUB)
        inner_ref[g, spot, :] = inner_ref[g, spot, :] + delta_ref[i]

    def body(g, carry):
        stages(g)
        return carry

    lax.fori_loop(3, groups, body, 0)
    for k in range(1, 4):
        stages(groups - 1 + k, first=k)
    for g in range(groups):
        out_copy(g).wait()


def per_device(records, tool_data, owners, local_seg, active, stiffness, columns, vectors):
    doms, tools = (lax.axis_size(axis) for axis in AXES)
    peers = doms * tools
    blocks, cands = owners.shape
    nnz = columns.shape[1]
    segs, width = tool_data.shape
    capacity = max(2, (3 * blocks * cands + 2 * peers - 1) // (2 * peers))
    groups = blocks // SUB
    pairs = NODE // 2
    chunks = width // LANES
    i32 = jnp.int32

    def shape(dims, dtype=F32):
        return jax.ShapeDtypeStruct(dims, dtype)

    def tiles_of(x, rows):
        lead = x.shape[:-2]
        n = len(lead)
        x = x.reshape(lead + (rows // SUB, SUB, x.shape[-1] // LANES, LANES))
        x = jnp.swapaxes(x, n + 1, n + 2)
        return x.reshape(lead + (rows // SUB, -1, LANES))

    vec = tiles_of(vectors, blocks)
    rec = tiles_of(records, blocks)
    stiff = tiles_of(jnp.swapaxes(stiffness, 0, 1), blocks)
    share = 2 * HB * pairs // peers
    stride = capacity + -(-share // chunks)

    def in_hbm(*arrays):
        return [pltpu.with_memory_space_constraint(x, pltpu.HBM) for x in arrays]

    send = pl.pallas_call(
        functools.partial(prep_kernel, peers, segs),
        out_shape=shape((peers * (1 + share), LANES)),
        in_specs=[HBM] * 3,
        out_specs=VMEM,
        scratch_shapes=[
            pltpu.VMEM((cands, blocks), i32),
            pltpu.VMEM((cands, blocks), i32),
            pltpu.VMEM(vec.shape[1:], F32),
            pltpu.VMEM(vec.shape[1:], F32),
            pltpu.VMEM((2 * HB * pairs, LANES), F32),
            pltpu.SemaphoreType.DMA((4,)),
        ],
        compiler_params=params(8),
        name="prep",
    )(*in_hbm(owners.T, local_seg.T, vec))

    members = AXES[::-1]
    wanted = lax.all_to_all(send.reshape(peers, 1 + share, 1, LANES), members, split_axis=0, concat_axis=0, tiled=True)
    wanted = wanted.reshape(peers * (1 + share), LANES)

    parts = pl.pallas_call(
        parts_kernel,
        out_shape=shape((segs, PARTS * width), BF16),
        in_specs=[HBM] * 2,
        out_specs=VMEM,
        scratch_shapes=[pltpu.VMEM(tool_data.shape, F32), pltpu.SemaphoreType.DMA((1,))],
        compiler_params=params(8),
        cost_estimate=pl.CostEstimate(flops=1 << 20, bytes_accessed=4 << 20, transcendentals=0),
        name="parts",
    )(*in_hbm(send, tool_data))

    rows_out = pl.pallas_call(
        functools.partial(rows_kernel, peers, capacity, stride),
        out_shape=shape((peers * stride * chunks, LANES)),
        in_specs=[VMEM] * 2,
        out_specs=VMEM,
        compiler_params=params(8),
        name="rows",
    )(wanted, parts)
    fetched = lax.all_to_all(
        rows_out.reshape(peers, stride, chunks, LANES), members, split_axis=0, concat_axis=0, tiled=True
    )

    wide = (blocks, NODE, LANES)
    left = (2 * NODE, nnz // 2 * 2 * NODE)
    inner, slot, own, fields, edges = pl.pallas_call(
        functools.partial(main_kernel, doms, peers, capacity, stride),
        out_shape=(
            pltpu.HBM(vec.shape, F32),
            shape((cands, blocks), i32),
            shape(wide, BF16),
            shape(wide, BF16),
            shape((2, HB * 2 * NODE, LANES), BF16),
        ),
        in_specs=[HBM] * 6,
        out_specs=(HBM,) + (VMEM,) * 4,
        scratch_shapes=[
            pltpu.SMEM((nnz, blocks), i32),
            pltpu.VMEM(vec.shape, F32),
            pltpu.VMEM(rec.shape, F32),
            pltpu.VMEM(active.shape, i32),
            pltpu.VMEM((cands, blocks), i32),
            pltpu.VMEM(stiff.shape, F32),
            pltpu.VMEM((blocks + 2 * HB, NODE, LANES), BF16),
            pltpu.VMEM((SUB,) + left, BF16),
            pltpu.VMEM((SUB, NODE, LANES), BF16),
            pltpu.VMEM(vec.shape, F32),
            pltpu.SemaphoreType.DMA((groups + 5,)),
            pltpu.SemaphoreType.DMA,
        ],
        compiler_params=params(20),
        cost_estimate=pl.CostEstimate(
            flops=6 * blocks * nnz * NODE * NODE * NVEC, bytes_accessed=24 << 20, transcendentals=0
        ),
        name="main",
    )(*in_hbm(columns.T, vec, rec, active, owners.T, stiff))

    out = pl.pallas_call(
        functools.partial(contact_kernel, peers, capacity, stride),
        out_shape=pltpu.HBM(vec.shape, F32),
        in_specs=[HBM] + [VMEM] * 5,
        out_specs=HBM,
        scratch_shapes=[
            pltpu.SMEM((cands, blocks), i32),
            pltpu.VMEM(vec.shape, F32),
            pltpu.VMEM(vec.shape, F32),
            pltpu.VMEM((SUB, 2 * NODE, LANES), BF16),
            pltpu.VMEM((SUB, NODE, LANES), BF16),
            pltpu.VMEM((SUB, pairs, LANES), F32),
            pltpu.VMEM((2 * HB * pairs, LANES), F32),
            pltpu.VMEM((2, HB * NODE, LANES), BF16),
            pltpu.VMEM((HB, NODE, LANES), F32),
            pltpu.VMEM((2 * HB, pairs, LANES), F32),
            pltpu.SemaphoreType.DMA((2,)),
            pltpu.SemaphoreType.DMA((groups,)),
        ],
        compiler_params=params(16),
        cost_estimate=pl.CostEstimate(
            flops=80 * blocks * cands * NODE * NODE, bytes_accessed=4 << 20, transcendentals=2 * blocks * cands * NODE * NODE
        ),
        name="contact",
    )(*in_hbm(inner), slot, fetched.reshape(peers * stride, chunks, LANES), fields, own, edges)
    out = out.reshape(groups, pairs, SUB, LANES)
    return jnp.swapaxes(out, 1, 2).reshape(blocks, NODE * NVEC)


def solution(mesh):
    split_rows = P(AXES, None)
    return jax.shard_map(
        per_device,
        mesh=mesh,
        in_specs=(split_rows,) * 5 + (P(AXES, None, None),) + (split_rows,) * 2,
        out_specs=split_rows,
        check_vma=False,
    )
```
